32 devices in a mesh: section: 2 (over core), dp: 16 (over z, y, x).
Axes of the slice: x: 2, y: 2, z: 4, core: 2. Of those that a mesh axis runs over, the one named last changes fastest.
Arguments:
- enc_in: bfloat16 [32, 512, 768], P('dp'), may hold values from -6 to 6
- dec_in: bfloat16 [128, 768], P('dp'), may hold values from -6 to 6
- segment: int32 [32, 512], P('dp'), may hold values from 0 to 3, never falling along the last dimension, each value on 1 to 256 neighbouring positions
- d_out: bfloat16 [128, 768], P('dp'), may hold values from -6 to 6
- attn_gain: bfloat16 [2, 768], P('section', 'dp'), may hold values from 0.5 to 1.5
- w_query: bfloat16 [2, 768, 768], P('section', 'dp'), may hold values from -0.0390625 to 0.0390625
- w_key: bfloat16 [2, 768, 768], P('section', 'dp'), may hold values from -0.21875 to 0.21875
- w_value: bfloat16 [2, 768, 768], P('section', 'dp'), may hold values from -0.21875 to 0.21875
- w_out: bfloat16 [2, 768, 768], P('section', 'dp'), may hold values from -0.625 to 0.625
- ffn_gain: bfloat16 [2, 768], P('section', 'dp'), may hold values from 0.5 to 1.5
- w_in: bfloat16 [2, 768, 3072], P('section', 'dp'), may hold values from -0.21875 to 0.21875
- w_back: bfloat16 [2, 3072, 768], P('section', 'dp'), may hold values from -0.109375 to 0.109375
- self_gain: bfloat16 [768], P(('section', 'dp')), may hold values from 0.5 to 1.5
- self_value: bfloat16 [768, 768], P(('section', 'dp')), may hold values from -0.21875 to 0.21875
- self_out: bfloat16 [768, 768], P(('section', 'dp')), may hold values from -0.21875 to 0.21875
- rel_table: float32 [32, 12], replicated, may hold values from -4 to 4
Outputs:
- dec_out: bfloat16 [128, 768], P('dp', 'section')
- enc_in_grad: bfloat16 [32, 512, 768], P('dp', None, 'section')
- dec_in_grad: bfloat16 [128, 768], P('dp', 'section')
- g_attn_gain: float32 [2, 768], P('section', 'dp')
- g_w_query: float32 [2, 768, 768], P('section', 'dp')
- g_w_key: float32 [2, 768, 768], P('section', 'dp')
- g_w_value: float32 [2, 768, 768], P('section', 'dp')
- g_w_out: float32 [2, 768, 768], P('section', 'dp')
- g_ffn_gain: float32 [2, 768], P('section', 'dp')
- g_w_in: float32 [2, 768, 3072], P('section', 'dp')
- g_w_back: float32 [2, 3072, 768], P('section', 'dp')
- g_self_gain: float32 [768], P(('section', 'dp'))
- g_self_value: float32 [768, 768], P(('section', 'dp'))
- g_self_out: float32 [768, 768], P(('section', 'dp'))
- g_rel_table: float32 [32, 12], replicated
The draws below stay inside these ranges and needn't reach their ends.
Inputs may be any that keep to these rules, and one draw needn't show every extreme that they name: `segment`: in each row the pair numbers never fall along the tokens, each of the 4 numbers covers 1 to 256 tokens, and one covers exactly 256.
All inputs are finite; a program needn't handle non-finite values.
Results may differ from the reference program's by a relative error of at most 0.025.
The reference program's roundings to bfloat16 on the way count: a program that leaves them out, or rounds other values in their place, can miss the bound.
Values may be sent and summed in bfloat16 or wider, within the bound.
No kernel may reach another device: no remote copies, remote signals or barrier semaphores. Data moves between devices by JAX's collectives and lax.ppermute only.
A program may use at most 448 MiB of HBM per device.

```python
import math
import jax
import jax.numpy as jnp
import numpy as np
from jax import lax

D = 768
HEADS = 12
HEAD_DIM = 64
FF = 3072
BUCKETS = 32
MAX_DIST = 128
ROW_LEN = 512
SEGS = 4
MOST_SEG = 256
ROWS = 32
PAIRS = 128


def strengthened(entries, key, source, target, blocks, factor):
    owner, partner = [(jnp.arange(entries.shape[dim]) // (entries.shape[dim] // blocks)).reshape([-1 if axis == dim else 1 for axis in range(entries.ndim)]) for dim in (source, target)]
    chosen = jax.random.permutation(key, blocks)[partner]
    strong = (owner == chosen) | (owner == (partner + blocks // 2) % blocks)
    return jnp.where(strong, factor * entries, entries)


def block_scale(key, shape, split, low, high):
    level = 1.0
    for position, blocks in split:
        draws = jax.random.uniform(jax.random.fold_in(jax.random.fold_in(key, 6), position), (blocks,), jnp.float32, low / len(split), high / len(split))
        level = level * jnp.repeat(jnp.exp(draws), shape[position] // blocks).reshape((-1,) + (1,) * (len(shape) - 1 - position))
    return level


def length_profile(amount, total, bound, lean):
    portions = [(1 << 20) // math.isqrt(rank ** lean) + 1 for rank in range(2, amount + 1)]
    surplus, holding = total - bound - (amount - 1), [1] * (amount - 1)
    while surplus > 0:
        free = [i for i in range(amount - 1) if holding[i] < bound]
        mass, left = sum([portions[i] for i in free]), surplus
        for i in free:
            extra = min(bound - holding[i], max(1, left * portions[i] // mass), surplus)
            holding[i] = holding[i] + extra
            surplus = surplus - extra
    return np.array([bound] + holding)


def ragged_sizes(own_key, count, total, reach, skew):
    if count == 2:
        one = jax.random.randint(own_key, (), max(1, total - reach), min(reach, total - 1) + 1)
        return jnp.stack([one, total - one])
    tallies = jnp.asarray(length_profile(count, total, reach, skew), jnp.int32)
    couples = (count - 1) // 2
    source_of, receiver = tallies[1:1 + 2 * couples:2], tallies[2:2 + 2 * couples:2]
    slack = jnp.minimum(source_of - 1, reach - receiver)
    passed = jax.random.randint(jax.random.fold_in(own_key, 1), (couples,), 0, 1 << 20) % (slack + 1)
    tallies = tallies.at[1:1 + 2 * couples:2].set(source_of - passed).at[2:2 + 2 * couples:2].set(receiver + passed)
    return tallies[jax.random.permutation(jax.random.fold_in(own_key, 2), count)]


def noise(stream_key, shape, deviation, reach, cuts=(), held_as=jnp.bfloat16):
    loudness = block_scale(stream_key, shape, cuts, -0.22, 0.18) if cuts else 1.0
    drawn = jax.random.normal(stream_key, shape, jnp.float32) * deviation * loudness
    return jnp.minimum(jnp.maximum(drawn, -reach), reach).astype(held_as)


def gaussian_with(stream_key, extent, scale, bound, split, heavy, held_as=jnp.bfloat16):
    drawn = scale * jax.random.normal(stream_key, extent, jnp.float32)
    if split:
        drawn = drawn * block_scale(stream_key, extent, split, -0.22, 0.18)
    return jnp.clip(strengthened(drawn, jax.random.fold_in(stream_key, 3), *heavy), -bound, bound).astype(held_as)


def setup_inputs(seed: int = 0) -> dict:
    key_list = jax.random.split(jax.random.key(seed), 17)
    return {
        "enc_in": gaussian_with(key_list[0], (ROWS, ROW_LEN, D), 1.0, 6.0, ((0, 16),), (0, 2, 16, 2.0)),
        "dec_in": gaussian_with(key_list[1], (PAIRS, D), 1.0, 6.0, ((0, 16),), (0, 1, 16, 2.0)),
        "segment": jax.vmap(lambda own: jnp.searchsorted(jnp.cumsum(ragged_sizes(own, SEGS, ROW_LEN, MOST_SEG, 1)), jnp.arange(ROW_LEN), side="right"))(jax.random.split(key_list[2], ROWS)).reshape((ROWS, ROW_LEN)).astype(jnp.int32),
        "d_out": gaussian_with(key_list[3], (PAIRS, D), 1.0, 6.0, ((0, 16),), (0, 1, 16, 2.0)),
        "attn_gain": jnp.clip(1.0 + 0.1 * jax.random.normal(key_list[4], (2, D), jnp.float32), 0.5, 1.5).astype(jnp.bfloat16),
        "w_query": noise(key_list[5], (2, D, D), (D * 32) ** -0.5, 0.0390625, ((0, 2), (1, 16))),
        "w_key": noise(key_list[6], (2, D, D), D ** -0.5, 0.21875, ((0, 2), (1, 16))),
        "w_value": noise(key_list[7], (2, D, D), D ** -0.5, 0.21875, ((0, 2), (1, 16))),
        "w_out": noise(key_list[8], (2, D, D), (D // 8) ** -0.5, 0.625, ((0, 2), (1, 16))),
        "ffn_gain": jnp.clip(1.0 + 0.1 * jax.random.normal(key_list[9], (2, D), jnp.float32), 0.5, 1.5).astype(jnp.bfloat16),
        "w_in": noise(key_list[10], (2, D, FF), D ** -0.5, 0.21875, ((0, 2), (1, 16))),
        "w_back": noise(key_list[11], (2, FF, D), FF ** -0.5, 0.109375, ((0, 2), (1, 16))),
        "self_gain": jnp.clip(1.0 + 0.1 * jax.random.normal(key_list[12], (D,), jnp.float32), 0.5, 1.5).astype(jnp.bfloat16),
        "self_value": noise(key_list[13], (D, D), D ** -0.5, 0.21875, ((0, 32),)),
        "self_out": noise(key_list[14], (D, D), D ** -0.5, 0.21875, ((0, 32),)),
        "rel_table": noise(key_list[15], (BUCKETS, HEADS), 1.0, 4.0, (), jnp.float32),
    }


@jax.custom_vjp
def low(v):
    return lax.optimization_barrier(v.astype(jnp.bfloat16)).astype(jnp.float32)

@jax.custom_vjp
def low_back(v):
    return v

def low_keep(v):
    return (low(v), None)

def low_pass(kept, grad):
    return (grad,)

def back_keep(v):
    return (v, None)

def back_low(kept, grad):
    return (low(grad),)
low.defvjp(low_keep, low_pass)
low_back.defvjp(back_keep, back_low)
epsilon = 1e-06
masked_score = -1000000000.0

def bucket_matrix(length, buckets, reach_max):
    half_count = buckets // 2
    exact_count = half_count // 2
    exponent = half_count - exact_count
    growth = reach_max // exact_count
    by_distance = []
    for distance in range(length):
        if distance < exact_count:
            by_distance.append(distance)
        else:
            levels = 0
            while levels < exponent and exact_count ** exponent * growth ** (levels + 1) <= distance ** exponent:
                levels += 1
            by_distance.append(min(exact_count + levels, half_count - 1))
    by_distance = np.array(by_distance, dtype=np.int32)
    places = np.arange(length)
    offset = places[None, :] - places[:, None]
    return (np.where(offset > 0, half_count, 0) + by_distance[np.abs(offset)]).astype(np.int32)

def rms_gain(values, gain):
    return values * lax.rsqrt(lax.optimization_barrier(jnp.mean(values * values, axis=-1, keepdims=True)) + epsilon) * gain

def gelu_tanh(pre_act):
    return jax.nn.gelu(pre_act, approximate=True)

def matmul(left_arr, right_arr):
    return jnp.dot(left_arr, right_arr, precision=lax.Precision.HIGHEST, preferred_element_type=jnp.float32)

def encode_row(x_row, seg_row, weights, score_bias):
    attn_g, w_q, w_k, w_v, w_o, ffn_g, w_i, w_b = weights
    head_shape = (ROW_LEN, HEADS, HEAD_DIM)
    normed = low(rms_gain(x_row, attn_g))
    queries = low_back(low(matmul(normed, w_q))).reshape(head_shape)
    key_rows = low_back(low(matmul(normed, w_k))).reshape(head_shape)
    value_rows = low_back(low(matmul(normed, w_v))).reshape(head_shape)
    scores = low_back(jnp.einsum('ihd,jhd->hij', queries, key_rows, precision=lax.Precision.HIGHEST) + score_bias)
    same_pair = seg_row[:, None] == seg_row[None, :]
    scores = jnp.where(same_pair[None], scores, masked_score)
    attn_probs = low(jax.nn.softmax(scores, axis=-1))
    context = low_back(low(jnp.einsum('hij,jhd->ihd', attn_probs, value_rows, precision=lax.Precision.HIGHEST)))
    context = context.reshape(ROW_LEN, D)
    residual = x_row + low_back(matmul(context, w_o))
    normed_two = low(rms_gain(residual, ffn_g))
    hidden = low(gelu_tanh(low_back(matmul(normed_two, w_i))))
    return low_back(low(residual + low_back(matmul(hidden, w_b))))

def decode_row(z_rows, encoded, seg_row, weights, self_weights):
    attn_g, w_q, w_k, w_v, w_o, ffn_g, w_i, w_b = weights
    self_g, self_v, self_o = self_weights
    normed_self = low(rms_gain(z_rows, self_g))
    self_vals = low_back(low(matmul(normed_self, self_v)))
    after_self = z_rows + low_back(matmul(self_vals, self_o))
    normed_cross = low(rms_gain(after_self, attn_g))
    cross_q = low_back(low(matmul(normed_cross, w_q))).reshape(SEGS, HEADS, HEAD_DIM)
    cross_k = low_back(low(matmul(encoded, w_k))).reshape(ROW_LEN, HEADS, HEAD_DIM)
    cross_v = low_back(low(matmul(encoded, w_v))).reshape(ROW_LEN, HEADS, HEAD_DIM)
    scores = low_back(jnp.einsum('shd,jhd->hsj', cross_q, cross_k, precision=lax.Precision.HIGHEST))
    owner_mask = seg_row[None, :] == jnp.arange(SEGS, dtype=jnp.int32)[:, None]
    scores = jnp.where(owner_mask[None], scores, masked_score)
    attn_probs = low(jax.nn.softmax(scores, axis=-1))
    context = low_back(low(jnp.einsum('hsj,jhd->shd', attn_probs, cross_v, precision=lax.Precision.HIGHEST)))
    context = context.reshape(SEGS, D)
    after_cross = after_self + low_back(matmul(context, w_o))
    normed_ffn = low(rms_gain(after_cross, ffn_g))
    hidden = low(gelu_tanh(low_back(matmul(normed_ffn, w_i))))
    return after_cross + low_back(matmul(hidden, w_b))

def reference(enc_in, dec_in, segment, d_out, attn_gain, w_query, w_key, w_value, w_out, ffn_gain, w_in, w_back, self_gain, self_value, self_out, rel_table):
    params = tuple((arr.astype(jnp.float32) for arr in (attn_gain, w_query, w_key, w_value, w_out, ffn_gain, w_in, w_back, self_gain, self_value, self_out, rel_table)))
    enc_x = enc_in.astype(jnp.float32)
    dec_z = dec_in.astype(jnp.float32)
    buckets_idx = jnp.asarray(bucket_matrix(ROW_LEN, BUCKETS, MAX_DIST))
    group_rows = 4

    def forward(params_in, enc_arr, dec_arr):
        stacked = params_in[:8]
        self_weights = params_in[8:11]
        table = params_in[11]
        score_bias = jnp.transpose(table[buckets_idx], (2, 0, 1))
        enc_weights = tuple((arr[0] for arr in stacked))
        dec_weights = tuple((arr[1] for arr in stacked))

        def one_row(x_row, seg_row, z_rows):
            encoded = encode_row(x_row, seg_row, enc_weights, score_bias)
            return decode_row(z_rows, encoded, seg_row, dec_weights, self_weights)

        def one_group(pieces):
            return jax.vmap(one_row)(pieces[0], pieces[1], pieces[2])
        grouped = (enc_arr.reshape(-1, group_rows, ROW_LEN, D), segment.reshape(-1, group_rows, ROW_LEN), dec_arr.reshape(-1, group_rows, SEGS, D))
        results = lax.map(jax.checkpoint(one_group), grouped)
        return results.reshape(-1, D)
    result, pull = jax.vjp(forward, params, enc_x, dec_z)
    grads, enc_grad, dec_grad = pull(d_out.astype(jnp.float32))
    return (result.astype(jnp.bfloat16), enc_grad.astype(jnp.bfloat16), dec_grad.astype(jnp.bfloat16), grads[0], grads[1], grads[2], grads[3], grads[4], grads[5], grads[6], grads[7], grads[8], grads[9], grads[10], grads[11])
```

```python
import functools

import jax
import jax.numpy as jnp
import numpy as np
from jax import lax
from jax.experimental import pallas as pl
from jax.experimental.pallas import tpu as pltpu
from jax.sharding import PartitionSpec as P

D = 768
HEADS = 12
HEAD_DIM = 64
FF = 3072
BUCKETS = 32
MAX_DIST = 128
ROW_LEN = 512
SEGS = 4
GROUP = 48
GROUPS = D // GROUP
TILE = 128
EPS = 1e-06
MASKED = -1000000000.0
BF = jnp.bfloat16
F32 = jnp.float32
VMEM_LIMIT = 58 * 1024 * 1024


def bucket_of(offset):
    half, exact = BUCKETS // 2, BUCKETS // 4
    exponent, growth = half - exact, MAX_DIST // exact
    distance = abs(offset)
    if distance < exact:
        level = distance
    else:
        k = 0
        while k < exponent and exact**exponent * growth ** (k + 1) <= distance**exponent:
            k += 1
        level = min(exact + k, half - 1)
    return (half if offset > 0 else 0) + level


def window_onehots():
    table = np.zeros((2, 3, 2 * TILE, BUCKETS), np.float32)
    for d in range(3):
        for t in range(2 * TILE):
            table[0, d, t, bucket_of(TILE * (d - 1) - TILE + t)] = 1.0
            table[1, d, t, bucket_of(TILE * (d - 1) + TILE - t)] = 1.0
    return table


def diagonal_onehots():
    table = np.zeros((5, 2 * TILE, BUCKETS), np.float32)
    table[1:4] = window_onehots()[1]
    table[0, :, bucket_of(-TILE - 1)] = 1.0
    table[4, :, bucket_of(TILE + 1)] = 1.0
    return table


def across(value):
    return lax.ppermute(value, "section", [(0, 1), (1, 0)])


def along(value, bit):
    count = lax.axis_size("dp")
    return lax.ppermute(value, "dp", [(i, i ^ (1 << bit)) for i in range(count)])


def bit_of(index, bit):
    return lax.rem(lax.div(index, 1 << bit), 2)


def low_bits(rows):
    count = 0
    while rows < GROUP:
        rows *= 2
        count += 1
    return count


def filled(piece, pre, chip, axis):
    for bit in range(pre):
        other = along(piece, bit)
        upper = bit_of(chip, bit) == 1
        first = jnp.where(upper, other, piece)
        second = jnp.where(upper, piece, other)
        piece = jnp.concatenate([first, second], axis=axis)
    return piece


def narrowed(total, pre, chip):
    for bit in reversed(range(pre)):
        length = total.shape[0] // 2
        upper = bit_of(chip, bit)
        kept = lax.dynamic_slice_in_dim(total, upper * length, length, 0)
        sent = lax.dynamic_slice_in_dim(total, (1 - upper) * length, length, 0)
        total = added(kept, along(sent.astype(BF), bit), F32)
    return total


def gather_groups(piece, order, pre):
    held = [(piece[None], [0])]
    for bit in order:
        held += [(along(part, bit + pre), [g ^ (1 << bit) for g in ids]) for part, ids in held]
        slots = sum(len(ids) for part, ids in held)
        if slots <= 4:
            merged = jnp.concatenate([part for part, ids in held], axis=0)
            held = [(merged, sum([ids for part, ids in held], []))]
    return held


def on_both(held):
    return [(part, ids, 0) for part, ids in held] + [(across(part), ids, 1) for part, ids in held]


def added(left, right, kind=BF):
    return (left.astype(F32) + right.astype(F32)).astype(kind)


def scatter_groups(mine, theirs, order, pre):
    got = across(theirs)
    half = GROUPS // 2
    keep, send = added(mine[:half], got[:half]), added(mine[half:], got[half:])
    for bit in order:
        got = along(send, bit + pre)
        half = keep.shape[0] // 2
        if half:
            keep, send = added(keep[:half], got[:half]), added(keep[half:], got[half:])
        else:
            total = added(keep[0], got[0], F32)
    return total


def nn(a, b):
    return lax.dot_general(a, b, (((1,), (0,)), ((), ())), preferred_element_type=F32)


def nt(a, b):
    return lax.dot_general(a, b, (((1,), (1,)), ((), ())), preferred_element_type=F32)


def tn(a, b):
    return lax.dot_general(a, b, (((0,), (0,)), ((), ())), preferred_element_type=F32)


def rms(v, gain):
    return v * lax.rsqrt(jnp.mean(v * v, axis=-1, keepdims=True) + EPS) * gain


def rms_back(v, gain, dy):
    r = lax.rsqrt(jnp.mean(v * v, axis=-1, keepdims=True) + EPS)
    dgain = jnp.sum(dy * v * r, axis=0, keepdims=True)
    dyg = dy * gain
    dv = r * dyg - v * (r * r * r) * jnp.mean(v * dyg, axis=-1, keepdims=True)
    return dv, dgain


def gelu_both(u):
    c = 0.7978845608028654
    t = jnp.tanh(c * (u + 0.044715 * u * u * u))
    value = 0.5 * u * (1.0 + t)
    slope = 0.5 * (1.0 + t) + (0.5 * c) * u * (1.0 - t * t) * (1.0 + 3 * 0.044715 * u * u)
    return value, slope


def square_row(core, b, g):
    return (core * 2 + b) * D + GROUP * g


def back_row(core, b, g):
    return 4 * GROUP * g + GROUP * (2 * core + b)


def self_row(core, b, g):
    return b * D + core * (D // 2) + GROUP * g


def start_fetch(meta, refs, plan, dst, row_of, sem, which=0):
    me, core = meta[which], meta[2]
    for ref, (ids, other) in zip(refs, plan):
        source = 1 - core if other else core
        for slot, rel in enumerate(ids):
            group = jnp.bitwise_xor(me, rel)
            for b in range(ref.shape[1]):
                off = pl.multiple_of(row_of(source, b, group), 16)
                pltpu.make_async_copy(ref.at[slot, b], dst.at[pl.ds(off, GROUP)], sem).start()


def drain(ref, sem):
    pltpu.make_async_copy(ref, ref, sem).wait()


def slot_of(meta, group, order):
    rel = jnp.bitwise_xor(meta[0], group)
    slot = 0
    for k, bit in enumerate(order):
        slot = slot + bit_of(rel, bit) * (1 << (len(order) - 1 - k))
    return slot


def start_store(meta, src, group, core, b, mine, theirs, order, sem):
    slot = slot_of(meta, group, order)

    @pl.when(meta[2] == core)
    def _():
        pltpu.make_async_copy(src, mine.at[slot, b], sem).start()

    @pl.when(meta[2] != core)
    def _():
        pltpu.make_async_copy(src, theirs.at[slot, b], sem).start()


def head_lanes(h):
    lane = lax.broadcasted_iota(jnp.int32, (1, D), 1)
    return (lane >= h * HEAD_DIM) & (lane < (h + 1) * HEAD_DIM)


def pair_lanes(hh):
    lane = lax.broadcasted_iota(jnp.int32, (1, TILE), 1)
    return (lane < HEAD_DIM) if hh == 0 else (lane >= HEAD_DIM)


def masked(value, lanes):
    return jnp.where(lanes, value, jnp.zeros_like(value))


def fill_bias(window_ref, tiles, transposed):
    part = 1 if transposed else 0

    def one(h, carry):
        for d in range(3):
            row = jnp.broadcast_to(window_ref[h, pl.ds(part * 3 + d, 1), :], (TILE, 2 * TILE))
            rolled = pltpu.roll(row, TILE, 1, stride=1, stride_axis=0)
            tiles[h, d + 1] = rolled[:, :TILE]
        low = window_ref[h, pl.ds(0, 1), pl.ds(0, 1)]
        high = window_ref[h, pl.ds(2, 1), pl.ds(2 * TILE - 1, 1)]
        tiles[h, 0] = jnp.broadcast_to(low, (TILE, TILE))
        tiles[h, 4] = jnp.broadcast_to(high, (TILE, TILE))
        return carry

    lax.fori_loop(0, HEADS, one, 0)


def whole(space=pltpu.VMEM):
    return pl.BlockSpec(memory_space=space)


def call(body, name, ins, spaces, outs, out_spaces, scratch, flops=0, bytes_=0):
    return pl.pallas_call(
        body,
        name=name,
        in_specs=[whole(s) for s in spaces],
        out_specs=[whole(s) for s in out_spaces],
        out_shape=[jax.ShapeDtypeStruct(s, k) for s, k in outs],
        scratch_shapes=scratch,
        compiler_params=pltpu.CompilerParams(vmem_limit_bytes=VMEM_LIMIT),
        cost_estimate=pl.CostEstimate(flops=int(flops), bytes_accessed=int(bytes_), transcendentals=0),
    )(*ins)


VM, SM, ANY = pltpu.VMEM, pltpu.SMEM, pl.ANY


def plan_of(sets):
    return [part for part, ids, other in sets], [(ids, other) for part, ids, other in sets]


def enc_attention(meta, x, gains, segr, segc, windows, sets):
    arrays, plan = plan_of(sets)
    n = len(arrays)

    def body(meta, x, gains, segr, segc, windows, *rest):
        parts, rest = rest[:n], rest[n:]
        n1, q, k, v, c, h1, n2, lse, w, tiles, lcol, sem = rest
        start_fetch(meta, parts, plan, w, square_row, sem)
        fill_bias(windows, tiles, False)
        xf = x[...].astype(F32)
        n1[...] = rms(xf, gains[0:1, :]).astype(BF)
        drain(w, sem)
        for ref, at in ((q, 0), (k, 2), (v, 3)):
            ref[...] = nn(n1[...], w[at * D : (at + 1) * D, :]).astype(BF)
        lane = lax.broadcasted_iota(jnp.int32, (1, TILE), 1)
        lcol[...] = jnp.zeros_like(lcol)

        def pair(pr, carry):
            cols = pl.ds(pl.multiple_of(pr * TILE, TILE), TILE)
            kp, vp = k[:, cols], v[:, cols]
            for ib in range(ROW_LEN // TILE):
                rows = slice(ib * TILE, (ib + 1) * TILE)
                same = segc[rows, :] == segr[...]
                qp = q[rows, cols]
                total = jnp.zeros((TILE, TILE), F32)
                for hh in range(2):
                    h = 2 * pr + hh
                    lanes = pair_lanes(hh)
                    bias = jnp.concatenate(
                        [tiles[h, min(max(jb - ib, -2), 2) + 2] for jb in range(ROW_LEN // TILE)], axis=1
                    )
                    s = jnp.where(same, nt(masked(qp, lanes), kp) + bias, MASKED)
                    top = jnp.max(s, axis=-1, keepdims=True)
                    ex = jnp.exp(s - top)
                    tot = jnp.sum(ex, axis=-1, keepdims=True)
                    p = (ex * (1.0 / tot)).astype(BF)
                    total = total + nn(p, masked(vp, lanes))
                    lcol[rows, :] = jnp.where(lane == h, top + jnp.log(tot), lcol[rows, :])
                c[rows, cols] = total.astype(BF)
            return carry

        lax.fori_loop(0, HEADS // 2, pair, 0)
        lse[...] = lcol[...].T
        res = x[...].astype(F32) + nn(c[...], w[D : 2 * D, :])
        h1[...] = res
        n2[...] = rms(res, gains[1:2, :]).astype(BF)

    rows = (ROW_LEN, D)
    return call(
        body, "enc_attention", [meta, x, gains, segr, segc, windows, *arrays],
        [SM, VM, VM, VM, VM, VM] + [ANY] * n,
        [(rows, BF)] * 5 + [(rows, F32), (rows, BF), ((TILE, ROW_LEN), F32)], [VM] * 8,
        [pltpu.VMEM((4 * D, D), BF), pltpu.VMEM((HEADS, 5, TILE, TILE), F32),
         pltpu.VMEM((ROW_LEN, TILE), F32), pltpu.SemaphoreType.DMA],
        flops=4e9, bytes_=12e6,
    )


def enc_ffn(meta, h1, n2, in_sets, back_sets):
    in_arrays, in_plan = plan_of(in_sets)
    back_arrays, back_plan = plan_of(back_sets)
    n = len(in_arrays)

    def body(meta, h1, n2, *rest):
        ins, backs, rest = rest[:n], rest[n : 2 * n], rest[2 * n :]
        f, slope, e, w_in, w_back, acc, sems = rest
        start_fetch(meta, ins, in_plan, w_in, square_row, sems.at[0])
        start_fetch(meta, backs, back_plan, w_back, back_row, sems.at[1])
        acc[...] = h1[...]
        drain(w_in, sems.at[0])
        drain(w_back, sems.at[1])

        def block(b, carry):
            rows = pl.ds(pl.multiple_of(b * D, D), D)
            value, grad = gelu_both(nn(n2[...], w_in[rows, :]))
            fb = value.astype(BF)
            f[:, rows] = fb
            slope[:, rows] = grad.astype(BF)
            acc[...] += nn(fb, w_back[rows, :])
            return carry

        lax.fori_loop(0, FF // D, block, 0)
        e[...] = acc[...].astype(BF)

    return call(
        body, "enc_ffn", [meta, h1, n2, *in_arrays, *back_arrays], [SM, VM, VM] + [ANY] * (2 * n),
        [((ROW_LEN, FF), BF), ((ROW_LEN, FF), BF), ((ROW_LEN, D), BF)], [VM] * 3,
        [pltpu.VMEM((FF, D), BF), pltpu.VMEM((FF, D), BF), pltpu.VMEM((ROW_LEN, D), F32),
         pltpu.SemaphoreType.DMA((2,))],
        flops=5e9, bytes_=18e6,
    )


def enc_ffn_back_out(meta, de, f, slope, back_sets, order):
    arrays, plan = plan_of(back_sets)
    n = len(arrays)

    def body(meta, de, f, slope, *rest):
        parts, rest = rest[:n], rest[n:]
        du, mine, theirs, w, buf, sems = rest
        start_fetch(meta, parts, plan, w, back_row, sems.at[0])
        drain(w, sems.at[0])
        for b in range(FF // D):
            cols = slice(b * D, (b + 1) * D)
            du[:, cols] = (slope[:, cols].astype(F32) * nt(de[...], w[cols, :])).astype(BF)
            at = b % 2
            if b >= 2:
                drain(buf.at[at], sems.at[1 + at])
            buf[at] = tn(f[:, cols], de[...]).astype(BF)
            for k in range(D // GROUP):
                group, piece = b * (D // GROUP // 4) + k // 4, k % 4
                start_store(meta, buf.at[at, pl.ds(k * GROUP, GROUP)], group, piece // 2, piece % 2,
                            mine, theirs, order, sems.at[1 + at])
        drain(buf.at[0], sems.at[1])
        drain(buf.at[1], sems.at[2])

    part = (GROUPS, 2, GROUP, D)
    return call(
        body, "enc_ffn_back_out", [meta, de, f, slope, *arrays], [SM, VM, VM, VM] + [ANY] * n,
        [((ROW_LEN, FF), BF), (part, BF), (part, BF)], [VM, ANY, ANY],
        [pltpu.VMEM((FF, D), BF), pltpu.VMEM((2, D, D), BF), pltpu.SemaphoreType.DMA((3,))],
        flops=5e9, bytes_=18e6,
    )


def enc_ffn_back_in(meta, du, n2, h1, de, gains, in_sets, order):
    arrays, plan = plan_of(in_sets)
    n = len(arrays)

    def body(meta, du, n2, h1, de, gains, *rest):
        parts, rest = rest[:n], rest[n:]
        dh1, da, dgain, mine, theirs, w, buf, acc, sems = rest
        start_fetch(meta, parts, plan, w, square_row, sems.at[0])
        drain(w, sems.at[0])
        for b in range(FF // D):
            cols = slice(b * D, (b + 1) * D)
            at = b % 2
            if b >= 2:
                drain(buf.at[at], sems.at[1 + at])
            buf[at] = tn(n2[...], du[:, cols]).astype(BF)
            for g in range(GROUPS):
                start_store(meta, buf.at[at, pl.ds(g * GROUP, GROUP)], g, b // 2, b % 2,
                            mine, theirs, order, sems.at[1 + at])
            part = nt(du[:, cols], w[cols, :])
            acc[...] = part if b == 0 else acc[...] + part
        dv, dg = rms_back(h1[...], gains[1:2, :], acc[...])
        total = de[...].astype(F32) + dv
        dh1[...] = total
        da[...] = total.astype(BF)
        dgain[...] = dg
        drain(buf.at[0], sems.at[1])
        drain(buf.at[1], sems.at[2])

    part, rows = (GROUPS, 2, GROUP, D), (ROW_LEN, D)
    return call(
        body, "enc_ffn_back_in", [meta, du, n2, h1, de, gains, *arrays], [SM, VM, VM, VM, VM, VM] + [ANY] * n,
        [(rows, F32), (rows, BF), ((1, D), F32), (part, BF), (part, BF)], [VM, VM, VM, ANY, ANY],
        [pltpu.VMEM((FF, D), BF), pltpu.VMEM((2, D, D), BF), pltpu.VMEM(rows, F32), pltpu.SemaphoreType.DMA((3,))],
        flops=5e9, bytes_=18e6,
    )


def enc_attention_back(meta, da, c, q, k, v, lse, segr, segc, windows, sets):
    arrays, plan = plan_of(sets)
    n = len(arrays)
    wide = 2 * TILE

    def body(meta, da, c, q, k, v, lse, segr, segc, windows, *rest):
        parts, rest = rest[:n], rest[n:]
        g_out, dq, dk, dv, diag, w, dc, tiles, sums, kacc, vacc, sem = rest
        start_fetch(meta, parts, plan, w, square_row, sem)
        fill_bias(windows, tiles, True)
        g_out[...] = tn(c[...], da[...]).astype(BF)
        drain(w, sem)
        dc[...] = nt(da[...], w[D : 2 * D, :]).astype(BF)
        row = lax.broadcasted_iota(jnp.int32, (TILE, TILE), 0)
        col = lax.broadcasted_iota(jnp.int32, (TILE, TILE), 1)
        flip = (row + col == TILE - 1).astype(F32)

        def pair(pr, carry):
            cols = pl.ds(pl.multiple_of(pr * TILE, TILE), TILE)
            for hh in range(2):
                h = 2 * pr + hh
                lanes = pair_lanes(hh)
                km, vm = masked(k[:, cols], lanes), masked(v[:, cols], lanes)
                sums[...] = jnp.zeros_like(sums)
                for ib in range(ROW_LEN // wide):
                    rows = slice(ib * wide, (ib + 1) * wide)
                    same = segc[...] == segr[:, rows]
                    qp, dcp = q[rows, cols], dc[rows, cols]
                    bias = jnp.concatenate([
                        jnp.concatenate([
                            tiles[h, min(max(jb - (2 * ib + i), -2), 2) + 2] for i in range(2)
                        ], axis=1) for jb in range(ROW_LEN // TILE)
                    ], axis=0)
                    s = jnp.where(same, nt(km, qp) + bias, MASKED)
                    prob = jnp.exp(s - lse[pl.ds(h, 1), rows])
                    dprob = nt(vm, dcp)
                    inner = jnp.sum(prob * dprob, axis=0, keepdims=True)
                    ds = (prob * (dprob - inner)).astype(BF)
                    dvp = nn(prob.astype(BF), masked(dcp, lanes))
                    dkp = nn(ds, masked(qp, lanes))
                    dqp = tn(ds, km)
                    if hh == 0 and ib == 0:
                        vacc[...], kacc[...] = dvp, dkp
                    else:
                        vacc[...] += dvp
                        kacc[...] += dkp
                    if hh == 0:
                        dq[rows, cols] = dqp.astype(BF)
                    else:
                        dq[rows, cols] = dq[rows, cols] + dqp.astype(BF)
                    for jb in range(ROW_LEN // TILE):
                        for i in range(2):
                            d = min(max(jb - (2 * ib + i), -2), 2) + 2
                            sums[d] += ds[jb * TILE : (jb + 1) * TILE, i * TILE : (i + 1) * TILE].astype(F32)
                for d in range(5):
                    if d in (0, 4):
                        line = jnp.sum(sums[d], axis=0, keepdims=True)
                        diag[h, d : d + 1, :] = jnp.concatenate([line, jnp.zeros_like(line)], axis=1)
                    else:
                        turned = lax.dot_general(
                            flip, sums[d], (((1,), (0,)), ((), ())),
                            precision=lax.Precision.HIGHEST, preferred_element_type=F32,
                        )
                        wider = jnp.concatenate([turned, jnp.zeros_like(turned)], axis=1)
                        rolled = pltpu.roll(wider, 1, 1, stride=1, stride_axis=0)
                        diag[h, d : d + 1, :] = jnp.sum(rolled, axis=0, keepdims=True)
            dk[:, cols] = kacc[...].astype(BF)
            dv[:, cols] = vacc[...].astype(BF)
            return carry

        lax.fori_loop(0, HEADS // 2, pair, 0)

    rows = (ROW_LEN, D)
    return call(
        body, "enc_attention_back", [meta, da, c, q, k, v, lse, segr, segc, windows, *arrays],
        [SM] + [VM] * 9 + [ANY] * n,
        [((D, D), BF), (rows, BF), (rows, BF), (rows, BF), ((HEADS, 5, 2 * TILE), F32)], [VM] * 5,
        [pltpu.VMEM((4 * D, D), BF), pltpu.VMEM(rows, BF), pltpu.VMEM((HEADS, 5, TILE, TILE), F32),
         pltpu.VMEM((5, TILE, TILE), F32), pltpu.VMEM((ROW_LEN, TILE), F32), pltpu.VMEM((ROW_LEN, TILE), F32),
         pltpu.SemaphoreType.DMA],
        flops=6e9, bytes_=12e6,
    )


def enc_square_grads(meta, n1, dq, dk, dv, g_out, order):
    def body(meta, n1, dq, dk, dv, g_out, mine, theirs, buf, sem):
        for at, (grad, core, b) in enumerate(((dq, 0, 0), (dk, 1, 0), (dv, 1, 1))):
            buf[at] = tn(n1[...], grad[...]).astype(BF)
            for g in range(GROUPS):
                start_store(meta, buf.at[at, pl.ds(g * GROUP, GROUP)], g, core, b, mine, theirs, order, sem)
        for g in range(GROUPS):
            start_store(meta, g_out.at[pl.ds(g * GROUP, GROUP)], g, 0, 1, mine, theirs, order, sem)
        drain(buf, sem)
        drain(g_out, sem)

    part = (GROUPS, 2, GROUP, D)
    return call(
        body, "enc_square_grads", [meta, n1, dq, dk, dv, g_out], [SM] + [VM] * 5,
        [(part, BF), (part, BF)], [ANY, ANY],
        [pltpu.VMEM((3, D, D), BF), pltpu.SemaphoreType.DMA],
        flops=2e9, bytes_=8e6,
    )


def enc_input_grad(meta, dq, dk, dv, x, dh1, gains, sets):
    arrays, plan = plan_of(sets)
    n = len(arrays)

    def body(meta, dq, dk, dv, x, dh1, gains, *rest):
        parts, rest = rest[:n], rest[n:]
        keep, send, dgain, w, sem = rest
        start_fetch(meta, parts, plan, w, square_row, sem)
        drain(w, sem)
        total = nt(dq[...], w[0:D, :]) + nt(dk[...], w[2 * D : 3 * D, :]) + nt(dv[...], w[3 * D :, :])
        dx, dg = rms_back(x[...].astype(F32), gains[0:1, :], total)
        out = (dh1[...] + dx).astype(BF)
        dgain[...] = dg
        half = D // 2

        @pl.when(meta[2] == 0)
        def _():
            keep[...] = out[:, :half]
            send[...] = out[:, half:]

        @pl.when(meta[2] != 0)
        def _():
            keep[...] = out[:, half:]
            send[...] = out[:, :half]

    return call(
        body, "enc_input_grad", [meta, dq, dk, dv, x, dh1, gains, *arrays], [SM] + [VM] * 6 + [ANY] * n,
        [((ROW_LEN, D // 2), BF), ((ROW_LEN, D // 2), BF), ((1, D), F32)], [VM] * 3,
        [pltpu.VMEM((4 * D, D), BF), pltpu.SemaphoreType.DMA],
        flops=2e9, bytes_=10e6,
    )


def spread_heads(value):
    return jnp.concatenate([masked(value, head_lanes(h)) for h in range(HEADS)], axis=0)


def join_heads(value):
    total = jnp.zeros((8, D), F32)
    for h in range(HEADS):
        total = total + masked(value[8 * h : 8 * h + 8, :], head_lanes(h))
    return total


def own_rows(meta):
    row = lax.broadcasted_iota(jnp.int32, (8, 1), 0)
    return (row >= 4 * meta[2]) & (row < 4 * meta[2] + 4)


def dec_before(meta, z, gains, self_sets, sets):
    self_arrays, self_plan = plan_of(self_sets)
    arrays, plan = plan_of(sets)
    n0, n = len(self_arrays), len(arrays)

    def body(meta, z, gains, *rest):
        selfs, parts, rest = rest[:n0], rest[n0 : n0 + n], rest[n0 + n :]
        m1, sv, z1, m2, qc, qk, w_self, w, sems = rest
        start_fetch(meta, selfs, self_plan, w_self, self_row, sems.at[0], 1)
        start_fetch(meta, parts, plan, w, square_row, sems.at[1])
        zf = z[...].astype(F32)
        m1v = rms(zf, gains[4:5, :]).astype(BF)
        drain(w_self, sems.at[0])
        drain(w, sems.at[1])
        svv = nn(m1v, w_self[0:D, :]).astype(BF)
        z1v = zf + nn(svv, w_self[D:, :])
        m2v = rms(z1v, gains[2:3, :]).astype(BF)
        qcv = nn(m2v, w[0:D, :]).astype(BF)
        qk[...] = nt(spread_heads(qcv), w[2 * D : 3 * D, :]).astype(BF)
        m1[...], sv[...], z1[...], m2[...], qc[...] = m1v, svv, z1v, m2v, qcv

    rows = (8, D)
    return call(
        body, "dec_before", [meta, z, gains, *self_arrays, *arrays], [SM, VM, VM] + [ANY] * (n0 + n),
        [(rows, BF), (rows, BF), (rows, F32), (rows, BF), (rows, BF), ((8 * HEADS, D), BF)], [VM] * 6,
        [pltpu.VMEM((2 * D, D), BF), pltpu.VMEM((4 * D, D), BF), pltpu.SemaphoreType.DMA((2,))],
        flops=1e9, bytes_=8e6,
    )


def dec_grad_hidden(meta, g, sets):
    arrays, plan = plan_of(sets)
    n = len(arrays)

    def body(meta, g, *rest):
        parts, rest = rest[:n], rest[n:]
        gm, gw, w, sem = rest
        start_fetch(meta, parts, plan, w, back_row, sem)
        own = jnp.where(own_rows(meta), g[...].astype(F32), 0.0).astype(BF)
        gm[...] = own
        drain(w, sem)
        for b in range(FF // D):
            gw[:, b * D : (b + 1) * D] = nt(own, w[b * D : (b + 1) * D, :])

    return call(
        body, "dec_grad_hidden", [meta, g, *arrays], [SM, VM] + [ANY] * n,
        [((8, D), BF), ((8, FF), F32)], [VM] * 2,
        [pltpu.VMEM((FF, D), BF), pltpu.SemaphoreType.DMA],
        flops=1e9, bytes_=5e6,
    )


def dec_core(meta, e, segr, qk, z1, g, gw, gains, sets, in_sets):
    arrays, plan = plan_of(sets)
    in_arrays, in_plan = plan_of(in_sets)
    n, n2 = len(arrays), len(in_arrays)

    def body(meta, e, segr, qk, z1, g, gw, gains, *rest):
        parts, ins, rest = rest[:n], rest[n : n + n2], rest[n + n2 :]
        de, cc, z2, m3, fc, duc, da2, dz2, dcc, edt, ebar, dgain, w, w_in, sems = rest
        start_fetch(meta, parts, plan, w, square_row, sems.at[0])
        start_fetch(meta, ins, in_plan, w_in, square_row, sems.at[1])
        pairs = lax.broadcasted_iota(jnp.int32, (8 * HEADS, 1), 0)
        owner = segr[...] == jnp.bitwise_and(pairs, 7) - 4 * meta[2]
        t = jnp.where(owner, nt(qk[...], e[...]), MASKED)
        ex = jnp.where(owner, jnp.exp(t - jnp.max(t, axis=-1, keepdims=True)), 0.0)
        tot = jnp.sum(ex, axis=-1, keepdims=True)
        prob = ex * (1.0 / jnp.where(tot > 0.0, tot, 1.0))
        pc = prob.astype(BF)
        ebv = nn(pc, e[...]).astype(BF)
        ebar[...] = ebv
        drain(w, sems.at[0])
        ccv = join_heads(nn(ebv, w[3 * D :, :])).astype(BF)
        z2v = z1[...] + nn(ccv, w[D : 2 * D, :])
        m3v = rms(z2v, gains[3:4, :]).astype(BF)
        drain(w_in, sems.at[1])
        dm3 = jnp.zeros((8, D), F32)
        for b in range(FF // D):
            cols = slice(b * D, (b + 1) * D)
            value, slope = gelu_both(nn(m3v, w_in[cols, :]))
            fc[:, cols] = value.astype(BF)
            ducv = (slope * gw[:, cols]).astype(BF)
            duc[:, cols] = ducv
            dm3 = dm3 + nt(ducv, w_in[cols, :])
        back, dg = rms_back(z2v, gains[3:4, :], dm3)
        dz2v = g[...].astype(F32) + back
        da2v = dz2v.astype(BF)
        dccv = nt(da2v, w[D : 2 * D, :]).astype(BF)
        dvw = nt(spread_heads(dccv), w[3 * D :, :]).astype(BF)
        dprob = nt(dvw, e[...])
        dt = (prob * (dprob - jnp.sum(prob * dprob, axis=-1, keepdims=True))).astype(BF)
        de[...] = tn(jnp.concatenate([pc, dt], axis=0), jnp.concatenate([dvw, qk[...]], axis=0)).astype(BF)
        edt[...] = nn(dt, e[...]).astype(BF)
        cc[...], z2[...], m3[...], da2[...], dz2[...], dcc[...], dgain[...] = ccv, z2v, m3v, da2v, dz2v, dccv, dg

    rows, spread = (8, D), (8 * HEADS, D)
    return call(
        body, "dec_core", [meta, e, segr, qk, z1, g, gw, gains, *arrays, *in_arrays],
        [SM] + [VM] * 7 + [ANY] * (n + n2),
        [((ROW_LEN, D), BF), (rows, BF), (rows, F32), (rows, BF), ((8, FF), BF), ((8, FF), BF), (rows, BF),
         (rows, F32), (rows, BF), (spread, BF), (spread, BF), ((1, D), F32)], [VM] * 12,
        [pltpu.VMEM((4 * D, D), BF), pltpu.VMEM((FF, D), BF), pltpu.SemaphoreType.DMA((2,))],
        flops=4e9, bytes_=12e6,
    )


def dec_after(meta, z, sv, z1, z2, dz2, qc, dcc, edt, ebar, fc, gains, self_sets, sets, back_sets, order):
    self_arrays, self_plan = plan_of(self_sets)
    arrays, plan = plan_of(sets)
    back_arrays, back_plan = plan_of(back_sets)
    n0, n, n2 = len(self_arrays), len(arrays), len(back_arrays)

    def body(meta, z, sv, z1, z2, dz2, qc, dcc, edt, ebar, fc, gains, *rest):
        selfs, parts, backs = rest[:n0], rest[n0 : n0 + n], rest[n0 + n : n0 + n + n2]
        dqc, ds1, dsv, dec_grad, dec_out, dg_attn, dg_self, mine, theirs, w_self, w, w_back, buf, sems = rest[n0 + n + n2 :]
        start_fetch(meta, parts, plan, w, square_row, sems.at[1])
        start_fetch(meta, selfs, self_plan, w_self, self_row, sems.at[0], 1)
        start_fetch(meta, backs, back_plan, w_back, back_row, sems.at[2])
        buf[0] = tn(edt[...], spread_heads(qc[...])).astype(BF)
        buf[1] = tn(ebar[...], spread_heads(dcc[...])).astype(BF)
        for at in range(2):
            for grp in range(GROUPS):
                start_store(meta, buf.at[at, pl.ds(grp * GROUP, GROUP)], grp, at, 0, mine, theirs, order, sems.at[3])
        drain(w, sems.at[1])
        dqv = join_heads(nn(edt[...], w[2 * D : 3 * D, :])).astype(BF)
        back, dg = rms_back(z1[...], gains[2:3, :], nt(dqv, w[0:D, :]))
        dz1 = dz2[...] + back
        ds1v = dz1.astype(BF)
        drain(w_self, sems.at[0])
        dsvv = nt(ds1v, w_self[D:, :]).astype(BF)
        back0, dg0 = rms_back(z[...].astype(F32), gains[4:5, :], nt(dsvv, w_self[0:D, :]))
        own = own_rows(meta)
        dec_grad[...] = jnp.where(own, dz1 + back0, 0.0).astype(BF)
        drain(w_back, sems.at[2])
        y = z2[...]
        for b in range(FF // D):
            cols = slice(b * D, (b + 1) * D)
            y = y + nn(fc[:, cols], w_back[cols, :])
        dec_out[...] = jnp.where(own, y, 0.0).astype(BF)
        dqc[...], ds1[...], dsv[...], dg_attn[...], dg_self[...] = dqv, ds1v, dsvv, dg, dg0
        drain(buf, sems.at[3])

    rows, part = (8, D), (GROUPS, 1, GROUP, D)
    return call(
        body, "dec_after",
        [meta, z, sv, z1, z2, dz2, qc, dcc, edt, ebar, fc, gains, *self_arrays, *arrays, *back_arrays],
        [SM] + [VM] * 11 + [ANY] * (n0 + n + n2),
        [(rows, BF)] * 5 + [((1, D), F32)] * 2 + [(part, BF)] * 2, [VM] * 7 + [ANY] * 2,
        [pltpu.VMEM((2 * D, D), BF), pltpu.VMEM((4 * D, D), BF), pltpu.VMEM((FF, D), BF), pltpu.VMEM((2, D, D), BF),
         pltpu.SemaphoreType.DMA((4,))],
        flops=2e9, bytes_=14e6,
    )


def halves(w_query, w_key, w_value, w_out, w_in, w_back):
    ins = [w_in[:, b * D : (b + 1) * D] for b in range(4)]
    backs = [w_back[b * GROUP : (b + 1) * GROUP] for b in range(4)]
    first = [w_query, w_out, ins[0], ins[1], backs[0], backs[1]]
    second = [w_key, w_value, ins[2], ins[3], backs[2], backs[3]]
    return jnp.stack(first), jnp.stack(second)


def per_device(
    enc_in, dec_in, segment, d_out, attn_gain, w_query, w_key, w_value, w_out, ffn_gain, w_in, w_back,
    self_gain, self_value, self_out, rel_table,
):
    core, chip = lax.axis_index("section"), lax.axis_index("dp")
    chips = lax.axis_size("dp")
    rows = w_query.shape[1]
    first = core == 0
    meta = jnp.stack([chip >> low_bits(rows), chip >> low_bits(self_value.shape[0]), core]).astype(jnp.int32)

    small = jnp.stack([
        jnp.pad(v.astype(BF), (0, TILE - v.shape[0])) for v in (attn_gain[0], ffn_gain[0], self_gain)
    ])
    gathered = small[None]
    bits = chips.bit_length() - 1
    for bit in range(bits):
        gathered = jnp.concatenate([gathered, along(gathered, bit)], axis=0)
    places = jnp.bitwise_xor(jnp.arange(chips), chip)
    gathered = jnp.take(gathered, places, axis=0)
    both = jnp.stack([gathered, across(gathered)])
    both = jnp.where(first, both, both[::-1])
    attn_all, ffn_all = both[:, :, 0, :rows].reshape(2, D), both[:, :, 1, :rows].reshape(2, D)
    self_all = both[:, :, 2, : self_gain.shape[0]].reshape(1, D)
    gains = jnp.concatenate(
        [attn_all[0:1], ffn_all[0:1], attn_all[1:2], ffn_all[1:2], self_all, jnp.zeros((3, D), BF)]
    ).astype(F32)

    pre = low_bits(rows)
    own_first, own_second = halves(
        *[filled(w[0], pre, chip, 0) for w in (w_query, w_key, w_value, w_out, w_in, w_back)]
    )
    swapped = across(jnp.where(first, own_second, own_first))
    enc_blocks = jnp.where(first, own_first, swapped)
    dec_blocks = jnp.where(first, swapped, own_second)
    zzxy, zzyx = (2, 3, 0, 1), (2, 3, 1, 0)

    def gather(blocks, order, pre=pre):
        return on_both(gather_groups(blocks, order, pre))

    enc_square = gather(enc_blocks[0:2], zzxy)
    enc_w_in = gather(enc_blocks[2:4], zzyx)
    enc_w_back = gather(enc_blocks[4:6], zzxy)
    self_pre = low_bits(self_value.shape[0])
    self_own = filled(jnp.stack([self_value, self_out]), self_pre, chip, 1)
    self_sets = gather(self_own, (1, 2, 0), self_pre)
    dec_square = gather(dec_blocks[0:2], zzyx)
    dec_w_in = gather(dec_blocks[2:4], zzxy)
    dec_w_back = gather(dec_blocks[4:6], zzyx)

    windows = jnp.einsum(
        "adtb,bh->hadt", window_onehots(), rel_table, precision=lax.Precision.HIGHEST
    ).reshape(HEADS, 6, 2 * TILE)

    x = lax.dynamic_index_in_dim(enc_in, core, 0, False)
    seg = lax.dynamic_index_in_dim(segment, core, 0, False)
    segr, segc = seg[None, :], seg[:, None]

    n1, q, k, v, c, h1, n2, lse = enc_attention(meta, x, gains, segr, segc, windows, enc_square)
    f, slope, e = enc_ffn(meta, h1, n2, enc_w_in, enc_w_back)

    m1, sv, z1, m2, qc, qk = dec_before(meta, dec_in, gains, self_sets, dec_square)
    gm, gw = dec_grad_hidden(meta, d_out, dec_w_back)
    de, cc, z2, m3, fc, duc, da2, dz2, dcc, edt, ebar, dg_ffn1 = dec_core(
        meta, e, segr, qk, z1, gm, gw, gains, dec_square, dec_w_in
    )

    du, back_mine, back_theirs = enc_ffn_back_out(meta, de, f, slope, enc_w_back, zzxy[::-1])
    dh1, da, dg_ffn0, in_mine, in_theirs = enc_ffn_back_in(meta, du, n2, h1, de, gains, enc_w_in, zzyx[::-1])
    dqc, ds1, dsv, dec_grad, dec_out, dg_attn1, dg_self, kv_mine, kv_theirs = dec_after(
        meta, dec_in, sv, z1, z2, dz2, qc, dcc, edt, ebar, fc, gains, self_sets, dec_square, dec_w_back, zzxy[::-1]
    )
    g_out, dq, dk, dv, diag = enc_attention_back(meta, da, c, q, k, v, lse, segr, segc, windows, enc_square)
    sq_mine, sq_theirs = enc_square_grads(meta, n1, dq, dk, dv, g_out, zzyx[::-1])
    keep, send, dg_attn0 = enc_input_grad(meta, dq, dk, dv, x, dh1, gains, enc_square)

    back_sum = scatter_groups(back_mine, back_theirs, zzxy[::-1], pre)
    in_sum = scatter_groups(in_mine, in_theirs, zzyx[::-1], pre)
    kv_sum = scatter_groups(kv_mine, kv_theirs, zzxy[::-1], pre)
    sq_sum = scatter_groups(sq_mine, sq_theirs, zzyx[::-1], pre)

    own = (jnp.arange(8)[:, None] // 4) == core
    acts = jnp.concatenate([m1, sv, m2, cc, m3, dsv, ds1, dqc, da2, fc, gm, duc], axis=1)
    acts = jnp.where(own, acts, jnp.zeros_like(acts))
    acts = acts + across(acts)
    width = acts.shape[1] // 2
    part = lax.dynamic_slice_in_dim(acts, core * width, width, 1)
    for bit in range(bits):
        part = jnp.concatenate([part, along(part, bit)], axis=0)
    other = across(part)
    acts = jnp.concatenate([jnp.where(first, part, other), jnp.where(first, other, part)], axis=1)
    a_m1, a_sv, a_m2, a_cc, a_m3, a_dsv, a_ds1, a_dqc, a_da2 = [acts[:, i * D : (i + 1) * D] for i in range(9)]
    a_fc, a_g, a_duc = acts[:, 9 * D : 13 * D], acts[:, 13 * D : 14 * D], acts[:, 14 * D :]

    def grad_rows(left, right, at, count):
        return tn(lax.dynamic_slice_in_dim(left, at, count, 1), right)

    mine = chip * rows
    dec_q = grad_rows(a_m2, a_dqc, mine, rows)
    dec_o = grad_rows(a_cc, a_da2, mine, rows)
    dec_i = grad_rows(a_m3, a_duc, mine, rows)
    dec_b = grad_rows(a_fc, a_g, 4 * mine, 4 * rows)
    own_self = self_value.shape[0]
    at_self = (core * chips + chip) * own_self
    g_self_value = grad_rows(a_m1, a_dsv, at_self, own_self)
    g_self_out = grad_rows(a_sv, a_ds1, at_self, own_self)

    table = jnp.einsum("hdt,dtb->bh", diag, diagonal_onehots(), precision=lax.Precision.HIGHEST)
    little = jnp.concatenate([
        dg_attn0, dg_ffn0, dg_attn1, dg_ffn1, dg_self,
        jnp.pad(table.reshape(1, -1), ((0, 0), (0, D - BUCKETS * HEADS))), jnp.zeros((2, D), F32),
    ])
    little = little + across(little)
    for bit in range(bits):
        little = little + along(little, bit)
    g_rel_table = little[5, : BUCKETS * HEADS].reshape(BUCKETS, HEADS)

    def cut(index, at, count):
        return lax.dynamic_slice_in_dim(little[index], at, count, 0)

    g_attn_gain = cut(jnp.where(first, 0, 2), mine, rows)[None]
    g_ffn_gain = cut(jnp.where(first, 1, 3), mine, rows)[None]
    g_self_gain = cut(4, at_self, own_self)

    enc_share = jnp.concatenate([sq_sum, in_sum, back_sum]).astype(BF)
    got = across(enc_share)
    got_kv = across(kv_sum)

    def placed(enc_value, dec_value):
        return jnp.where(first, narrowed(enc_value, pre, chip), dec_value)[None]

    g_w_query = placed(sq_sum[0], dec_q)
    g_w_out = placed(sq_sum[1], dec_o)
    g_w_key = narrowed(jnp.where(first, got[0].astype(F32), got_kv[0]), pre, chip)[None]
    g_w_value = narrowed(jnp.where(first, got[1].astype(F32), kv_sum[0]), pre, chip)[None]
    wide = jnp.concatenate([in_sum[0], in_sum[1], got[2].astype(F32), got[3].astype(F32)], axis=1)
    g_w_in = placed(wide, dec_i)
    tall = jnp.concatenate([back_sum[0], back_sum[1], got[4].astype(F32), got[5].astype(F32)], axis=0)
    g_w_back = placed(tall, dec_b)

    other_half = across(send)
    enc_in_grad = jnp.where(first, jnp.stack([keep, other_half]), jnp.stack([other_half, keep]))
    dec_out = dec_out + across(dec_out)
    dec_grad = dec_grad + across(dec_grad)
    half = D // 2
    dec_out = jnp.where(first, dec_out[:, :half], dec_out[:, half:])
    dec_in_grad = jnp.where(first, dec_grad[:, :half], dec_grad[:, half:])
    return (
        dec_out, enc_in_grad, dec_in_grad, g_attn_gain, g_w_query, g_w_key, g_w_value, g_w_out, g_ffn_gain,
        g_w_in, g_w_back, g_self_gain, g_self_value, g_self_out, g_rel_table,
    )


def solution(mesh):
    return jax.shard_map(
        per_device,
        mesh=mesh,
        in_specs=(
            P("dp", None, None),
            P("dp", None),
            P("dp", None),
            P("dp", None),
            P("section", "dp"),
            P("section", "dp", None),
            P("section", "dp", None),
            P("section", "dp", None),
            P("section", "dp", None),
            P("section", "dp"),
            P("section", "dp", None),
            P("section", "dp", None),
            P(("section", "dp")),
            P(("section", "dp"), None),
            P(("section", "dp"), None),
            P(),
        ),
        out_specs=(
            P("dp", "section"),
            P("dp", None, "section"),
            P("dp", "section"),
            P("section", "dp"),
            P("section", "dp", None),
            P("section", "dp", None),
            P("section", "dp", None),
            P("section", "dp", None),
            P("section", "dp"),
            P("section", "dp", None),
            P("section", "dp", None),
            P(("section", "dp")),
            P(("section", "dp"), None),
            P(("section", "dp"), None),
            P(),
        ),
        check_vma=False,
    )
```

```python
import functools

import jax
import jax.numpy as jnp
import numpy as np
from jax import lax
from jax.experimental import pallas as pl
from jax.experimental.pallas import tpu as pltpu
from jax.sharding import PartitionSpec as P

D = 768
HEADS = 12
HEAD_DIM = 64
FF = 3072
BUCKETS = 32
MAX_DIST = 128
ROW_LEN = 512
SEGS = 4
GROUP = 48
GROUPS = D // GROUP
X, Y, Z0, Z1 = 0, 1, 2, 3
TILE = 128
EPS = 1e-06
MASKED = -1000000000.0
BF = jnp.bfloat16
F32 = jnp.float32
VMEM_LIMIT = 58 * 1024 * 1024


def bucket_of(offset):
    half, exact = BUCKETS // 2, BUCKETS // 4
    exponent, growth = half - exact, MAX_DIST // exact
    distance = abs(offset)
    if distance < exact:
        level = distance
    else:
        k = 0
        while k < exponent and exact**exponent * growth ** (k + 1) <= distance**exponent:
            k += 1
        level = min(exact + k, half - 1)
    return (half if offset > 0 else 0) + level


def window_onehots():
    table = np.zeros((2, 3, 2 * TILE, BUCKETS), np.float32)
    for d in range(3):
        for t in range(2 * TILE):
            table[0, d, t, bucket_of(TILE * (d - 1) - TILE + t)] = 1.0
            table[1, d, t, bucket_of(TILE * (d - 1) + TILE - t)] = 1.0
    return table


def diagonal_onehots():
    table = np.zeros((5, 2 * TILE, BUCKETS), np.float32)
    table[1:4] = window_onehots()[1]
    table[0, :, bucket_of(-TILE - 1)] = 1.0
    table[4, :, bucket_of(TILE + 1)] = 1.0
    return table


def across(value):
    return lax.ppermute(value, "section", [(0, 1), (1, 0)])


def along(value, bit):
    count = lax.axis_size("dp")
    return lax.ppermute(value, "dp", [(i, i ^ (1 << bit)) for i in range(count)])


def bit_of(index, bit):
    return lax.rem(lax.div(index, 1 << bit), 2)


def low_bits(rows):
    count = 0
    while rows < GROUP:
        rows *= 2
        count += 1
    return count


def filled(piece, pre, chip, axis):
    for bit in range(pre):
        other = along(piece, bit)
        upper = bit_of(chip, bit) == 1
        first = jnp.where(upper, other, piece)
        second = jnp.where(upper, piece, other)
        piece = jnp.concatenate([first, second], axis=axis)
    return piece


def narrowed(total, pre, chip):
    for bit in reversed(range(pre)):
        length = total.shape[0] // 2
        upper = bit_of(chip, bit)
        kept = lax.dynamic_slice_in_dim(total, upper * length, length, 0)
        sent = lax.dynamic_slice_in_dim(total, (1 - upper) * length, length, 0)
        total = added(kept, along(sent.astype(BF), bit), F32)
    return total


def gate(after, *values):
    out = lax.optimization_barrier((tuple(values), tuple(after)))[0]
    return out[0] if len(values) == 1 else out


class Chain:
    def __init__(self, piece, pre):
        self.held, self.ids, self.pre = piece[None], [0], pre

    def split(self, at):
        parts = []
        for held in (self.held[:, :at], self.held[:, at:]):
            part = Chain(held[0], self.pre)
            part.held, part.ids = held, self.ids
            parts.append(part)
        return parts

    def step(self, bit):
        got = along(self.held, bit + self.pre)
        self.held = jnp.concatenate([self.held, got], axis=0)
        self.ids = self.ids + [g ^ (1 << bit) for g in self.ids]
        return [got]

    def last(self, bit):
        self.last_got = along(self.held, bit + self.pre)
        self.last_ids = [g ^ (1 << bit) for g in self.ids]
        return [self.last_got]

    def cross(self):
        self.other = across(self.held)
        return [self.other]

    def cross_last(self):
        self.other_last = across(self.last_got)
        return [self.other_last]

    def sets(self):
        return [
            (self.held, self.ids, 0), (self.last_got, self.last_ids, 0),
            (self.other, self.ids, 1), (self.other_last, self.last_ids, 1),
        ]


def gate_chains(after, *chains):
    held = lax.optimization_barrier((tuple(c.held for c in chains), tuple(after)))[0]
    for chain, value in zip(chains, held):
        chain.held = value


def added(left, right, kind=BF):
    return (left.astype(F32) + right.astype(F32)).astype(kind)


class Sum:
    def __init__(self, keep, send, pre):
        self.mine, self.send, self.got, self.pre = keep, send, None, pre

    def step(self, bit):
        if self.got is not None:
            half = self.mine.shape[0] // 2
            self.send = added(self.mine[half:], self.got[half:])
            self.mine = added(self.mine[:half], self.got[:half])
        self.got = along(self.send, bit + self.pre)
        return [self.got]

    def total(self):
        return added(self.mine[0], self.got[0], F32)


def merged(sums):
    one = Sum(jnp.concatenate([part.mine for part in sums], axis=1), None, sums[0].pre)
    one.got = jnp.concatenate([part.got for part in sums], axis=1)
    return one


def nn(a, b):
    return lax.dot_general(a, b, (((1,), (0,)), ((), ())), preferred_element_type=F32)


def nt(a, b):
    return lax.dot_general(a, b, (((1,), (1,)), ((), ())), preferred_element_type=F32)


def tn(a, b):
    return lax.dot_general(a, b, (((0,), (0,)), ((), ())), preferred_element_type=F32)


def rms(v, gain):
    return v * lax.rsqrt(jnp.mean(v * v, axis=-1, keepdims=True) + EPS) * gain


def rms_back(v, gain, dy):
    r = lax.rsqrt(jnp.mean(v * v, axis=-1, keepdims=True) + EPS)
    dgain = jnp.sum(dy * v * r, axis=0, keepdims=True)
    dyg = dy * gain
    dv = r * dyg - v * (r * r * r) * jnp.mean(v * dyg, axis=-1, keepdims=True)
    return dv, dgain


def gelu_both(u):
    c = 0.7978845608028654
    t = jnp.tanh(c * (u + 0.044715 * u * u * u))
    value = 0.5 * u * (1.0 + t)
    slope = 0.5 * (1.0 + t) + (0.5 * c) * u * (1.0 - t * t) * (1.0 + 3 * 0.044715 * u * u)
    return value, slope


def square_row(b):
    return lambda core, g: (core * 2 + b) * D + GROUP * g


def back_row(b):
    return lambda core, g: 4 * GROUP * g + GROUP * (2 * core + b)


def in_items(first):
    return [(first + GROUP * b, GROUP, square_row(b), lambda core, g, b=b: 2 * core + b) for b in range(2)]


def back_items(first):
    return [(first, 2 * GROUP, back_row(0), lambda core, g: g // 4)]


def start_fetch(meta, refs, plan, items, dst, sem, only=None):
    if only is not None:
        for other in range(2):
            part = [(ref, entry) for ref, entry in zip(refs, plan) if entry[1] == other]

            @pl.when(jnp.bitwise_xor(meta[1], other) == only)
            def _():
                start_fetch(meta, [r for r, e in part], [e for r, e in part], items, dst, sem)

        return
    me, core = meta[0], meta[1]
    for first, count, row_of, *sem_of in items:
        for ref, (ids, other) in zip(refs, plan):
            source = 1 - core if other else core
            for slot, rel in enumerate(ids):
                group = jnp.bitwise_xor(me, rel)
                off = pl.multiple_of(row_of(source, group), 16)
                at = sem.at[sem_of[0](source, group)] if sem_of else sem
                pltpu.make_async_copy(ref.at[slot, pl.ds(first, count)], dst.at[pl.ds(off, count)], at).start()


def drain(ref, sem):
    pltpu.make_async_copy(ref, ref, sem).wait()


def slot_of(meta, group, b):
    rel = jnp.bitwise_xor(meta[0], group)
    x, y, z0, z1 = [jnp.bitwise_and(rel // (1 << bit), 1) for bit in range(4)]
    return (8 * y + 4 * x if b == 0 else 8 * x + 4 * y) + 2 * z0 + z1


def start_store(meta, src, group, b, keep, send, sem, cols=None):
    slot = slot_of(meta, group, b)
    at = () if cols is None else (slice(None), cols)

    @pl.when(slot < GROUPS // 2)
    def _():
        pltpu.make_async_copy(src, keep.at[(slot,) + at], sem).start()

    @pl.when(slot >= GROUPS // 2)
    def _():
        pltpu.make_async_copy(src, send.at[(slot - GROUPS // 2,) + at], sem).start()


def head_lanes(h):
    lane = lax.broadcasted_iota(jnp.int32, (1, D), 1)
    return (lane >= h * HEAD_DIM) & (lane < (h + 1) * HEAD_DIM)


def pair_lanes(hh):
    lane = lax.broadcasted_iota(jnp.int32, (1, TILE), 1)
    return (lane < HEAD_DIM) if hh == 0 else (lane >= HEAD_DIM)


def masked(value, lanes):
    return jnp.where(lanes, value, jnp.zeros_like(value))


def fill_bias(window_ref, tiles, transposed):
    part = 1 if transposed else 0

    def one(h, carry):
        for d in range(3):
            row = jnp.broadcast_to(window_ref[h, pl.ds(part * 3 + d, 1), :], (TILE, 2 * TILE))
            rolled = pltpu.roll(row, TILE, 1, stride=1, stride_axis=0)
            tiles[h, d + 1] = rolled[:, :TILE]
        low = window_ref[h, pl.ds(0, 1), pl.ds(0, 1)]
        high = window_ref[h, pl.ds(2, 1), pl.ds(2 * TILE - 1, 1)]
        tiles[h, 0] = jnp.broadcast_to(low, (TILE, TILE))
        tiles[h, 4] = jnp.broadcast_to(high, (TILE, TILE))
        return carry

    lax.fori_loop(0, HEADS, one, 0)


def whole(space=pltpu.VMEM):
    return pl.BlockSpec(memory_space=space)


def call(body, name, ins, spaces, outs, out_spaces, scratch, us):
    return pl.pallas_call(
        body,
        name=name,
        in_specs=[whole(s) for s in spaces],
        out_specs=[whole(s) for s in out_spaces],
        out_shape=[jax.ShapeDtypeStruct(s, k) for s, k in outs],
        scratch_shapes=scratch,
        compiler_params=pltpu.CompilerParams(vmem_limit_bytes=VMEM_LIMIT),
        cost_estimate=pl.CostEstimate(flops=int(us * 1.1e9), bytes_accessed=int(us * 1e6), transcendentals=0),
    )(*ins)


VM, SM, ANY = pltpu.VMEM, pltpu.SMEM, pl.ANY


def plan_of(sets):
    return [part for part, ids, other in sets], [(ids, other) for part, ids, other in sets]


def enc_attention(meta, x, gains, segr, segc, windows, a_sets, b_sets):
    a_arrays, a_plan = plan_of(a_sets)
    b_arrays, b_plan = plan_of(b_sets)
    n = len(a_arrays)

    def body(meta, x, gains, segr, segc, windows, *rest):
        a_parts, b_parts, rest = rest[:n], rest[n : 2 * n], rest[2 * n :]
        n1, q, k, v, c, h1, n2, lse, w, tiles, lcol, sems = rest
        start_fetch(meta, a_parts, a_plan, [(0, GROUP, square_row(0))], w, sems.at[0])
        start_fetch(meta, b_parts, b_plan, [(0, GROUP, square_row(1))], w, sems.at[0])
        fill_bias(windows, tiles, False)
        xf = x[...].astype(F32)
        n1[...] = rms(xf, gains[0:1, :]).astype(BF)
        drain(w, sems.at[0])
        for ref, at in ((q, 0), (k, 2), (v, 3)):
            ref[...] = nn(n1[...], w[at * D : (at + 1) * D, :]).astype(BF)
        lane = lax.broadcasted_iota(jnp.int32, (1, TILE), 1)
        lcol[...] = jnp.zeros_like(lcol)

        def pair(pr, carry):
            cols = pl.ds(pl.multiple_of(pr * TILE, TILE), TILE)
            kp, vp = k[:, cols], v[:, cols]
            for ib in range(ROW_LEN // TILE):
                rows = slice(ib * TILE, (ib + 1) * TILE)
                same = segc[rows, :] == segr[...]
                qp = q[rows, cols]
                total = jnp.zeros((TILE, TILE), F32)
                for hh in range(2):
                    h = 2 * pr + hh
                    lanes = pair_lanes(hh)
                    bias = jnp.concatenate(
                        [tiles[h, min(max(jb - ib, -2), 2) + 2] for jb in range(ROW_LEN // TILE)], axis=1
                    )
                    s = jnp.where(same, nt(masked(qp, lanes), kp) + bias, MASKED)
                    top = jnp.max(s, axis=-1, keepdims=True)
                    ex = jnp.exp(s - top)
                    tot = jnp.sum(ex, axis=-1, keepdims=True)
                    p = (ex * (1.0 / tot)).astype(BF)
                    total = total + nn(p, masked(vp, lanes))
                    lcol[rows, :] = jnp.where(lane == h, top + jnp.log(tot), lcol[rows, :])
                c[rows, cols] = total.astype(BF)
            return carry

        lax.fori_loop(0, HEADS // 2, pair, 0)
        lse[...] = lcol[...].T
        res = x[...].astype(F32) + nn(c[...], w[D : 2 * D, :])
        h1[...] = res
        n2[...] = rms(res, gains[1:2, :]).astype(BF)

    rows = (ROW_LEN, D)
    return call(
        body, "enc_attention", [meta, x, gains, segr, segc, windows, *a_arrays, *b_arrays],
        [SM, VM, VM, VM, VM, VM] + [ANY] * (2 * n),
        [(rows, BF)] * 5 + [(rows, F32), (rows, BF), ((TILE, ROW_LEN), F32), ], [VM] * 8,
        [pltpu.VMEM((4 * D, D), BF), pltpu.VMEM((HEADS, 5, TILE, TILE), F32), pltpu.VMEM((ROW_LEN, TILE), F32), pltpu.SemaphoreType.DMA((2,))],
        us=20,
    )


def enc_ffn(meta, h1, n2, in_sets, back_sets):
    in_arrays, in_plan = plan_of(in_sets)
    back_arrays, back_plan = plan_of(back_sets)
    n = len(in_arrays)

    def body(meta, h1, n2, *rest):
        ins, backs, rest = rest[:n], rest[n : 2 * n], rest[2 * n :]
        f, slope, e, w_in, w_back, acc, sems = rest
        start_fetch(meta, ins, in_plan, in_items(0), w_in, sems)
        start_fetch(meta, backs, back_plan, back_items(0), w_back, sems.at[pl.ds(4, 4)])
        acc[...] = h1[...]

        def block(b, carry):
            rows = pl.ds(pl.multiple_of(b * D, D), D)

            drain(w_in.at[rows], sems.at[b])
            value, grad = gelu_both(nn(n2[...], w_in[rows, :]))
            fb = value.astype(BF)
            f[:, rows] = fb
            slope[:, rows] = grad.astype(BF)
            drain(w_back.at[rows], sems.at[4 + b])
            acc[...] += nn(fb, w_back[rows, :])
            return carry

        lax.fori_loop(0, FF // D, block, 0)
        e[...] = acc[...].astype(BF)

    return call(
        body, "enc_ffn", [meta, h1, n2, *in_arrays, *back_arrays], [SM, VM, VM] + [ANY] * (2 * n),
        [((ROW_LEN, FF), BF), ((ROW_LEN, FF), BF), ((ROW_LEN, D), BF)], [VM] * 3,
        [pltpu.VMEM((FF, D), BF), pltpu.VMEM((FF, D), BF), pltpu.VMEM((ROW_LEN, D), F32),
         pltpu.SemaphoreType.DMA((8,))],
        us=15,
    )


PART = (GROUPS // 2, GROUP, D)


def enc_hidden_grad(meta, de, slope, back_sets):
    arrays, plan = plan_of(back_sets)
    n = len(arrays)

    def body(meta, de, slope, *rest):
        parts, rest = rest[:n], rest[n:]
        du, other, w, sems = rest
        start_fetch(meta, parts, plan, back_items(0), w, sems)
        for b in range(FF // D):
            cols = slice(b * D, (b + 1) * D)
            drain(w.at[cols], sems.at[b])
            value = (slope[:, cols].astype(F32) * nt(de[...], w[cols, :])).astype(BF)
            du[:, cols] = value

            @pl.when(meta[1] != b // 2)
            def _():
                other[:, (b % 2) * D : (b % 2 + 1) * D] = value

    return call(
        body, "enc_hidden_grad", [meta, de, slope, *arrays], [SM, VM, VM] + [ANY] * n,
        [((ROW_LEN, FF), BF), ((ROW_LEN, FF // 2), BF)], [VM, VM],
        [pltpu.VMEM((FF, D), BF), pltpu.SemaphoreType.DMA((4,))],
        us=8,
    )


def enc_w_back_grad(meta, de, de_got, f, f_got):
    half = D // 2

    def body(meta, de, de_got, f, f_got, keep_a, send_a, keep_b, send_b, mine, buf, sems):
        mine[...] = de[:, pl.ds(pl.multiple_of(meta[1] * half, TILE), half)]
        for b in range(FF // D):
            cols = slice(b * D, (b + 1) * D)
            at = b % 2
            if b >= 2:
                drain(buf.at[at], sems.at[at])
            buf[at] = (tn(f[:, cols], mine[...]) + tn(f_got[:, cols], de_got[...])).astype(BF)
            for k in range(D // GROUP):
                group, piece = b * (D // GROUP // 4) + k // 4, k % 4
                keep, send = (keep_a, send_a) if piece < 2 else (keep_b, send_b)
                start_store(meta, buf.at[at, pl.ds(k * GROUP, GROUP)], group, piece // 2, keep, send, sems.at[at],
                            pl.ds((piece % 2) * half, half))
        drain(buf.at[0], sems.at[0])
        drain(buf.at[1], sems.at[1])

    return call(
        body, "enc_w_back_grad", [meta, de, de_got, f, f_got], [SM] + [VM] * 4,
        [(PART, BF)] * 4, [ANY] * 4,
        [pltpu.VMEM((ROW_LEN, half), BF), pltpu.VMEM((2, D, half), BF), pltpu.SemaphoreType.DMA((2,))],
        us=7,
    )


def enc_w_in_grad(meta, du, du_got, n2, n2_got):
    def body(meta, du, du_got, n2, n2_got, keep_a, send_a, keep_b, send_b, buf, sems):
        for b in range(2):
            cols = pl.ds(pl.multiple_of(meta[1] * (FF // 2) + b * D, TILE), D)
            buf[b] = (tn(n2[...], du[:, cols]) + tn(n2_got[...], du_got[:, b * D : (b + 1) * D])).astype(BF)
            keep, send = (keep_a, send_a) if b == 0 else (keep_b, send_b)
            for g in range(GROUPS):
                start_store(meta, buf.at[b, pl.ds(g * GROUP, GROUP)], g, b, keep, send, sems.at[b])
        drain(buf.at[0], sems.at[0])
        drain(buf.at[1], sems.at[1])

    return call(
        body, "enc_w_in_grad", [meta, du, du_got, n2, n2_got], [SM] + [VM] * 4,
        [(PART, BF)] * 4, [ANY] * 4,
        [pltpu.VMEM((2, D, D), BF), pltpu.SemaphoreType.DMA((2,))],
        us=7,
    )


def enc_ffn_back(meta, du, h1, de, gains, in_sets):
    arrays, plan = plan_of(in_sets)
    n = len(arrays)

    def body(meta, du, h1, de, gains, *rest):
        parts, rest = rest[:n], rest[n:]
        dh1, da, dgain, w, acc, sems = rest
        start_fetch(meta, parts, plan, in_items(0), w, sems)
        for k, b in enumerate((0, 2, 1, 3)):
            cols = slice(b * D, (b + 1) * D)
            drain(w.at[cols], sems.at[b])
            part = nt(du[:, cols], w[cols, :])
            acc[...] = part if k == 0 else acc[...] + part
        dv, dg = rms_back(h1[...], gains[1:2, :], acc[...])
        total = de[...].astype(F32) + dv
        dh1[...] = total
        da[...] = total.astype(BF)
        dgain[...] = dg

    rows = (ROW_LEN, D)
    return call(
        body, "enc_ffn_back", [meta, du, h1, de, gains, *arrays], [SM, VM, VM, VM, VM] + [ANY] * n,
        [(rows, F32), (rows, BF), ((1, D), F32)], [VM, VM, VM],
        [pltpu.VMEM((FF, D), BF), pltpu.VMEM(rows, F32), pltpu.SemaphoreType.DMA((4,))],
        us=8,
    )


def enc_attention_back(meta, da, q, k, v, lse, segr, segc, windows, sets):
    arrays, plan = plan_of(sets)
    n = len(arrays)
    wide = 2 * TILE

    def body(meta, da, q, k, v, lse, segr, segc, windows, *rest):
        parts, rest = rest[:n], rest[n:]
        dq, dk, dv, diag, other, w, dc, tiles, sums, kacc, vacc, sem = rest
        start_fetch(meta, parts, plan, [(0, GROUP, lambda core, g: GROUP * g)], w, sem, only=0)
        fill_bias(windows, tiles, True)
        drain(w, sem)
        dc[...] = nt(da[...], w[...]).astype(BF)
        row = lax.broadcasted_iota(jnp.int32, (TILE, TILE), 0)
        col = lax.broadcasted_iota(jnp.int32, (TILE, TILE), 1)
        flip = (row + col == TILE - 1).astype(F32)

        def pair(pr, carry):
            cols = pl.ds(pl.multiple_of(pr * TILE, TILE), TILE)
            for hh in range(2):
                h = 2 * pr + hh
                lanes = pair_lanes(hh)
                km, vm = masked(k[:, cols], lanes), masked(v[:, cols], lanes)
                sums[...] = jnp.zeros_like(sums)
                for ib in range(ROW_LEN // wide):
                    rows = slice(ib * wide, (ib + 1) * wide)
                    same = segc[...] == segr[:, rows]
                    qp, dcp = q[rows, cols], dc[rows, cols]
                    bias = jnp.concatenate([
                        jnp.concatenate([
                            tiles[h, min(max(jb - (2 * ib + i), -2), 2) + 2] for i in range(2)
                        ], axis=1) for jb in range(ROW_LEN // TILE)
                    ], axis=0)
                    s = jnp.where(same, nt(km, qp) + bias, MASKED)
                    prob = jnp.exp(s - lse[pl.ds(h, 1), rows])
                    dprob = nt(vm, dcp)
                    inner = jnp.sum(prob * dprob, axis=0, keepdims=True)
                    ds = (prob * (dprob - inner)).astype(BF)
                    dvp = nn(prob.astype(BF), masked(dcp, lanes))
                    dkp = nn(ds, masked(qp, lanes))
                    dqp = tn(ds, km)
                    if hh == 0 and ib == 0:
                        vacc[...], kacc[...] = dvp, dkp
                    else:
                        vacc[...] += dvp
                        kacc[...] += dkp
                    if hh == 0:
                        dq[rows, cols] = dqp.astype(BF)
                    else:
                        dq[rows, cols] = dq[rows, cols] + dqp.astype(BF)
                    for jb in range(ROW_LEN // TILE):
                        for i in range(2):
                            d = min(max(jb - (2 * ib + i), -2), 2) + 2
                            sums[d] += ds[jb * TILE : (jb + 1) * TILE, i * TILE : (i + 1) * TILE].astype(F32)
                for d in range(5):
                    if d in (0, 4):
                        line = jnp.sum(sums[d], axis=0, keepdims=True)
                        diag[h, d : d + 1, :] = jnp.concatenate([line, jnp.zeros_like(line)], axis=1)
                    else:
                        turned = lax.dot_general(
                            flip, sums[d], (((1,), (0,)), ((), ())),
                            precision=lax.Precision.HIGHEST, preferred_element_type=F32,
                        )
                        wider = jnp.concatenate([turned, jnp.zeros_like(turned)], axis=1)
                        rolled = pltpu.roll(wider, 1, 1, stride=1, stride_axis=0)
                        diag[h, d : d + 1, :] = jnp.sum(rolled, axis=0, keepdims=True)
            dk[:, cols] = kacc[...].astype(BF)
            dv[:, cols] = vacc[...].astype(BF)
            return carry

        lax.fori_loop(0, HEADS // 2, pair, 0)

        @pl.when(meta[1] == 0)
        def _():
            other[0] = dk[...]
            other[1] = dv[...]

        @pl.when(meta[1] != 0)
        def _():
            other[0] = dq[...]
            other[1] = da[...]

    rows = (ROW_LEN, D)
    return call(
        body, "enc_attention_back", [meta, da, q, k, v, lse, segr, segc, windows, *arrays],
        [SM] + [VM] * 8 + [ANY] * n,
        [(rows, BF), (rows, BF), (rows, BF), ((HEADS, 5, 2 * TILE), F32), ((2,) + rows, BF)], [VM] * 5,
        [pltpu.VMEM((D, D), BF), pltpu.VMEM(rows, BF), pltpu.VMEM((HEADS, 5, TILE, TILE), F32),
         pltpu.VMEM((5, TILE, TILE), F32), pltpu.VMEM((ROW_LEN, TILE), F32), pltpu.VMEM((ROW_LEN, TILE), F32),
         pltpu.SemaphoreType.DMA],
        us=25,
    )


def enc_square_grads(meta, n1, n1_got, c, c_got, dq, dk, dv, da, got):
    def body(meta, n1, n1_got, c, c_got, dq, dk, dv, da, got, keep_a, send_a, keep_b, send_b, buf, sems):
        for core, (one, left, left_got, two) in enumerate(((dq, c, c_got, da), (dk, n1, n1_got, dv))):

            @pl.when(meta[1] == core)
            def _():
                buf[0] = (tn(n1[...], one[...]) + tn(n1_got[...], got[0])).astype(BF)
                for g in range(GROUPS):
                    start_store(meta, buf.at[0, pl.ds(g * GROUP, GROUP)], g, 0, keep_a, send_a, sems.at[0])
                buf[1] = (tn(left[...], two[...]) + tn(left_got[...], got[1])).astype(BF)
                for g in range(GROUPS):
                    start_store(meta, buf.at[1, pl.ds(g * GROUP, GROUP)], g, 1, keep_b, send_b, sems.at[1])

        drain(buf.at[0], sems.at[0])
        drain(buf.at[1], sems.at[1])

    return call(
        body, "enc_square_grads", [meta, n1, n1_got, c, c_got, dq, dk, dv, da, got], [SM] + [VM] * 9,
        [(PART, BF)] * 4, [ANY] * 4,
        [pltpu.VMEM((2, D, D), BF), pltpu.SemaphoreType.DMA((2,))],
        us=6,
    )


def enc_input_grad(meta, dq, dk, dv, x, dh1, gains, a_sets, b_sets):
    a_arrays, a_plan = plan_of(a_sets)
    b_arrays, b_plan = plan_of(b_sets)
    n = len(a_arrays)

    def body(meta, dq, dk, dv, x, dh1, gains, *rest):
        a_parts, b_parts, rest = rest[:n], rest[n : 2 * n], rest[2 * n :]
        keep, send, dgain, w, sem = rest
        start_fetch(meta, a_parts, a_plan, [(0, GROUP, lambda core, g: core * D + GROUP * g)], w, sem)
        start_fetch(meta, b_parts, b_plan, [(0, GROUP, lambda core, g: 2 * D + GROUP * g)], w, sem, only=1)
        drain(w, sem)
        total = nt(dq[...], w[0:D, :]) + nt(dk[...], w[D : 2 * D, :]) + nt(dv[...], w[2 * D :, :])
        dx, dg = rms_back(x[...].astype(F32), gains[0:1, :], total)
        out = (dh1[...] + dx).astype(BF)
        dgain[...] = dg
        half = D // 2

        @pl.when(meta[1] == 0)
        def _():
            keep[...] = out[:, :half]
            send[...] = out[:, half:]

        @pl.when(meta[1] != 0)
        def _():
            keep[...] = out[:, half:]
            send[...] = out[:, :half]

    return call(
        body, "enc_input_grad", [meta, dq, dk, dv, x, dh1, gains, *a_arrays, *b_arrays],
        [SM] + [VM] * 6 + [ANY] * (2 * n),
        [((ROW_LEN, D // 2), BF), ((ROW_LEN, D // 2), BF), ((1, D), F32)], [VM] * 3,
        [pltpu.VMEM((3 * D, D), BF), pltpu.SemaphoreType.DMA],
        us=8,
    )


def spread_heads(value):
    return jnp.concatenate([masked(value, head_lanes(h)) for h in range(HEADS)], axis=0)


def join_heads(value):
    total = jnp.zeros((8, D), F32)
    for h in range(HEADS):
        total = total + masked(value[8 * h : 8 * h + 8, :], head_lanes(h))
    return total


def own_rows(meta):
    row = lax.broadcasted_iota(jnp.int32, (8, 1), 0)
    return (row >= 4 * meta[1]) & (row < 4 * meta[1] + 4)


def start_self(meta, own, got, dst, sem):
    half = D // 2
    pltpu.make_async_copy(own, dst.at[pl.ds(pl.multiple_of(meta[1] * half, 16), half)], sem).start()
    pltpu.make_async_copy(got, dst.at[pl.ds(pl.multiple_of((1 - meta[1]) * half, 16), half)], sem).start()


def dec_before(meta, z, d_out, gains, self_own, self_got, sets):
    arrays, plan = plan_of(sets)
    n = len(arrays)

    def body(meta, z, d_out, gains, self_own, self_got, *rest):
        parts, rest = rest[:n], rest[n:]
        m1, sv, z1, m2, qc, qk, gm, w_self, w, sems = rest
        start_self(meta, self_own, self_got, w_self, sems.at[0])
        start_fetch(meta, parts, plan, [(0, GROUP, lambda core, g: core * D + GROUP * g)], w, sems.at[1])
        zf = z[...].astype(F32)
        gm[...] = jnp.where(own_rows(meta), d_out[...].astype(F32), 0.0).astype(BF)
        m1v = rms(zf, gains[2:3, :]).astype(BF)
        drain(w_self, sems.at[0])
        drain(w, sems.at[1])
        svv = nn(m1v, w_self[:, :D]).astype(BF)
        z1v = zf + nn(svv, w_self[:, D:])
        m2v = rms(z1v, gains[0:1, :]).astype(BF)
        qcv = nn(m2v, w[0:D, :]).astype(BF)
        qk[...] = nt(spread_heads(qcv), w[D:, :]).astype(BF)
        m1[...], sv[...], z1[...], m2[...], qc[...] = m1v, svv, z1v, m2v, qcv

    rows = (8, D)
    return call(
        body, "dec_before", [meta, z, d_out, gains, self_own, self_got, *arrays],
        [SM, VM, VM, VM, ANY, ANY] + [ANY] * n,
        [(rows, BF), (rows, BF), (rows, F32), (rows, BF), (rows, BF), ((8 * HEADS, D), BF), (rows, BF)], [VM] * 7,
        [pltpu.VMEM((D, 2 * D), BF), pltpu.VMEM((2 * D, D), BF), pltpu.SemaphoreType.DMA((2,))],
        us=6,
    )


def dec_core(meta, e, segr, qk, qc, z1, g, gw, gains, sets, in_sets, in_sets_b):
    arrays, plan = plan_of(sets)
    in_arrays, in_plan = plan_of(in_sets)
    in_arrays_b, in_plan_b = plan_of(in_sets_b)
    n = len(arrays)

    def body(meta, e, segr, qk, qc, z1, g, gw, gains, *rest):
        parts, ins, ins_b, rest = rest[:n], rest[n : 2 * n], rest[2 * n : 3 * n], rest[3 * n :]
        de, cc, z2, m3, fc, duc, da2, dz2, dcc, edt, ebar, dgain, de_other, pairs_other, w, w_in, sems = rest
        start_fetch(meta, parts, plan, [(0, GROUP, lambda core, g: core * D + GROUP * g)], w, sems.at[0])
        start_fetch(meta, ins, in_plan, [(GROUP, GROUP, square_row(0))], w_in, sems.at[1])
        start_fetch(meta, ins_b, in_plan_b, [(GROUP, GROUP, square_row(1))], w_in, sems.at[1])
        pairs = lax.broadcasted_iota(jnp.int32, (8 * HEADS, 1), 0)
        owner = segr[...] == jnp.bitwise_and(pairs, 7) - 4 * meta[1]
        t = jnp.where(owner, nt(qk[...], e[...]), MASKED)
        ex = jnp.where(owner, jnp.exp(t - jnp.max(t, axis=-1, keepdims=True)), 0.0)
        tot = jnp.sum(ex, axis=-1, keepdims=True)
        prob = ex * (1.0 / jnp.where(tot > 0.0, tot, 1.0))
        pc = prob.astype(BF)
        ebv = nn(pc, e[...]).astype(BF)
        ebar[...] = ebv
        drain(w, sems.at[0])
        ccv = join_heads(nn(ebv, w[D:, :])).astype(BF)
        z2v = z1[...] + nn(ccv, w[0:D, :])
        m3v = rms(z2v, gains[1:2, :]).astype(BF)
        drain(w_in, sems.at[1])
        dm3 = jnp.zeros((8, D), F32)
        own = own_rows(meta)
        for b in range(FF // D):
            cols = slice(b * D, (b + 1) * D)
            value, slope = gelu_both(nn(m3v, w_in[cols, :]))
            fc[:, cols] = jnp.where(own, value, 0.0).astype(BF)
            ducv = jnp.where(own, slope * gw[:, cols].astype(F32), 0.0).astype(BF)
            duc[:, cols] = ducv
            dm3 = dm3 + nt(ducv, w_in[cols, :])
        back, dg = rms_back(z2v, gains[1:2, :], dm3)
        dz2v = g[...].astype(F32) + back
        da2v = dz2v.astype(BF)
        dccv = nt(da2v, w[0:D, :]).astype(BF)
        dvw = nt(spread_heads(dccv), w[D:, :]).astype(BF)
        dprob = nt(dvw, e[...])
        dt = (prob * (dprob - jnp.sum(prob * dprob, axis=-1, keepdims=True))).astype(BF)
        de[...] = tn(jnp.concatenate([pc, dt], axis=0), jnp.concatenate([dvw, qk[...]], axis=0)).astype(BF)
        edt[...] = nn(dt, e[...]).astype(BF)
        cc[...], m3[...], da2[...], dz2[...], dcc[...], dgain[...] = ccv, m3v, da2v, dz2v, dccv, dg
        z2[...] = jnp.where(own, z2v, 0.0)
        half = D // 2
        pairs_other[8 * HEADS + 8 :, :] = jnp.zeros((8, D), BF)

        @pl.when(meta[1] == 0)
        def _():
            de_other[...] = de[:, half:]
            pairs_other[: 8 * HEADS, :] = ebv
            pairs_other[8 * HEADS : 8 * HEADS + 8, :] = dccv

        @pl.when(meta[1] != 0)
        def _():
            de_other[...] = de[:, :half]
            pairs_other[: 8 * HEADS, :] = edt[...]
            pairs_other[8 * HEADS : 8 * HEADS + 8, :] = qc[...]

    rows, spread = (8, D), (8 * HEADS, D)
    return call(
        body, "dec_core", [meta, e, segr, qk, qc, z1, g, gw, gains, *arrays, *in_arrays, *in_arrays_b],
        [SM] + [VM] * 8 + [ANY] * (3 * n),
        [((ROW_LEN, D), BF), (rows, BF), (rows, F32), (rows, BF), ((8, FF), BF), ((8, FF), BF), (rows, BF),
         (rows, F32), (rows, BF), (spread, BF), (spread, BF), ((1, D), F32),
         ((ROW_LEN, D // 2), BF), ((8 * HEADS + 16, D), BF)], [VM] * 14,
        [pltpu.VMEM((2 * D, D), BF), pltpu.VMEM((FF, D), BF), pltpu.SemaphoreType.DMA((2,))],
        us=10,
    )


def dec_after(meta, z, z1, dz2, qc, dcc, edt, ebar, got, gains, self_own, self_got, sets):
    arrays, plan = plan_of(sets)
    n = len(arrays)

    def body(meta, z, z1, dz2, qc, dcc, edt, ebar, got, gains, self_own, self_got, *rest):
        parts, rest = rest[:n], rest[n:]
        dqc, ds1, dsv, dec_grad, dg_attn, dg_self, keep, send, w_self, w, buf, sems = rest
        start_fetch(meta, parts, plan, [(0, GROUP, lambda core, g: core * D + GROUP * g)], w, sems.at[1])
        start_self(meta, self_own, self_got, w_self, sems.at[0])
        zero = meta[1] == 0
        left = jnp.concatenate([jnp.where(zero, edt[...], ebar[...]), got[: 8 * HEADS, :]], axis=0)
        right = jnp.where(zero, qc[...], dcc[...])
        right = jnp.concatenate([spread_heads(right), spread_heads(got[8 * HEADS : 8 * HEADS + 8, :])], axis=0)
        buf[...] = tn(left, right).astype(BF)
        for grp in range(GROUPS):
            start_store(meta, buf.at[pl.ds(grp * GROUP, GROUP)], grp, 0, keep, send, sems.at[3])
        drain(w, sems.at[1])
        dqv = join_heads(nn(edt[...], w[D:, :])).astype(BF)
        back, dg = rms_back(z1[...], gains[0:1, :], nt(dqv, w[0:D, :]))
        dz1 = dz2[...] + back
        ds1v = dz1.astype(BF)
        drain(w_self, sems.at[0])
        dsvv = nt(ds1v, w_self[:, D:]).astype(BF)
        back0, dg0 = rms_back(z[...].astype(F32), gains[2:3, :], nt(dsvv, w_self[:, :D]))
        own = own_rows(meta)
        dec_grad[...] = jnp.where(own, dz1 + back0, 0.0).astype(BF)
        dqc[...], ds1[...], dsv[...], dg_attn[...], dg_self[...] = dqv, ds1v, dsvv, dg, dg0
        drain(buf, sems.at[3])

    rows = (8, D)
    return call(
        body, "dec_after",
        [meta, z, z1, dz2, qc, dcc, edt, ebar, got, gains, self_own, self_got, *arrays],
        [SM] + [VM] * 9 + [ANY] * (2 + n),
        [(rows, BF)] * 4 + [((1, D), F32)] * 2 + [(PART, BF)] * 2, [VM] * 6 + [ANY] * 2,
        [pltpu.VMEM((D, 2 * D), BF), pltpu.VMEM((2 * D, D), BF), pltpu.VMEM((D, D), BF),
         pltpu.SemaphoreType.DMA((4,))],
        us=6,
    )


def dec_weight_grads(place, left, right, g_all, w_back, rows, self_rows):
    def body(place, left, right, g_all, w_back, dec_q, dec_o, dec_i, dec_b, self_v, self_o, y):
        half = left.shape[1]
        chip, core = place[0], place[1]
        chips = D // rows

        def cut(at, width):
            parts = []
            while width:
                ref, first = (left, at) if at < half else (right, at - half)
                count = min(width, half - first)
                parts.append(ref[:, first : first + count])
                at, width = at + count, width - count
            return parts[0] if len(parts) == 1 else jnp.concatenate(parts, axis=1)

        def picked(at, first, count, width=D):
            row = lax.broadcasted_iota(jnp.int32, (count, width), 0) + first
            col = lax.broadcasted_iota(jnp.int32, (count, width), 1)
            return nt((row == col).astype(F32).astype(BF), cut(at * D, width)).astype(BF)

        first, first_self = chip * rows, (core * chips + chip) * self_rows
        m1, sv, m2, cc, m3, da2, dqc, ds1, dsv, duc, fc = list(range(10)) + [13]
        dec_q[...] = nn(picked(m2, first, rows), cut(dqc * D, D))
        dec_o[...] = nn(picked(cc, first, rows), cut(da2 * D, D))
        dec_i[...] = nn(picked(m3, first, rows), cut(duc * D, FF))
        self_v[...] = nn(picked(m1, first_self, self_rows), cut(dsv * D, D))
        self_o[...] = nn(picked(sv, first_self, self_rows), cut(ds1 * D, D))
        hidden = picked(fc, 4 * first, 4 * rows, FF)
        dec_b[...] = nn(hidden, g_all[...])
        y[...] = tn(hidden, w_back[...]).astype(BF)

    return call(
        body, "dec_weight_grads", [place, left, right, g_all, w_back], [SM, VM, VM, VM, VM],
        [((rows, D), F32), ((rows, D), F32), ((rows, FF), F32), ((4 * rows, D), F32), ((self_rows, D), F32),
         ((self_rows, D), F32), (g_all.shape, BF)], [VM] * 7,
        [], us=5,
    )


def pieces(w_query, w_key, w_value, w_out, w_in, w_back):
    ins = [w_in[:, b * D : (b + 1) * D] for b in range(4)]
    backs = [w_back[b * GROUP : (b + 1) * GROUP] for b in range(4)]
    return jnp.stack([
        jnp.concatenate([w_query, w_out] + ins[:2] + backs[:2]), jnp.concatenate([w_key, w_value] + ins[2:] + backs[2:])
    ])


def per_device(
    enc_in, dec_in, segment, d_out, attn_gain, w_query, w_key, w_value, w_out, ffn_gain, w_in, w_back,
    self_gain, self_value, self_out, rel_table,
):
    core, chip = lax.axis_index("section"), lax.axis_index("dp")
    chips = lax.axis_size("dp")
    rows = w_query.shape[1]
    first = core == 0
    pre = low_bits(rows)
    meta = jnp.stack([chip >> pre, core]).astype(jnp.int32)
    self_rows = self_value.shape[0]
    at_self = (core * chips + chip) * self_rows

    small = jnp.zeros((8, D), BF)
    small = lax.dynamic_update_slice(small, jnp.concatenate([attn_gain, ffn_gain]), (0, chip * rows))
    small = lax.dynamic_update_slice(small, self_gain[None], (2, at_self))
    small = jnp.concatenate([jnp.concatenate([self_value, self_out], axis=1), jnp.concatenate([d_out, small], axis=1)])
    small = lax.all_gather(small, "dp")

    both = pieces(*[filled(w[0], pre, chip, 0) for w in (w_query, w_key, w_value, w_out, w_in, w_back)])
    kept = lax.dynamic_index_in_dim(both, core, 0, False)
    got = across(lax.dynamic_index_in_dim(both, 1 - core, 0, False))
    enc_piece, dec_piece = jnp.where(first, kept, got), jnp.where(first, got, kept)

    def block(piece, *numbers):
        return jnp.concatenate([piece[k * GROUP : (k + 1) * GROUP] for k in numbers])

    sq, wide = Chain(enc_piece[: 2 * GROUP], pre), Chain(enc_piece[2 * GROUP :], pre)
    dec = Chain(block(dec_piece, 0, 2, 1, 3), pre)

    windows = jnp.einsum(
        "adtb,bh->hadt", window_onehots(), rel_table, precision=lax.Precision.HIGHEST
    ).reshape(HEADS, 6, 2 * TILE)
    x = lax.dynamic_index_in_dim(enc_in, core, 0, False)
    seg = lax.dynamic_index_in_dim(segment, core, 0, False)
    segr, segc = seg[None, :], seg[:, None]

    sq.step(Z1)
    done = sq.step(Z0)
    sa, sb = sq.split(GROUP)
    gate_chains(done, sa, sb, wide)
    done = sa.step(X) + sb.step(Y) + wide.step(Z1)
    gate_chains(done, sa, sb, wide)
    done = sa.last(Y) + sb.last(X) + wide.step(Z0) + sa.cross() + sb.cross()
    wa, wb = wide.split(2 * GROUP)
    gate_chains(done, wa, wb, dec)
    done = wa.step(X) + wb.step(Y) + dec.step(Z1) + sa.cross_last() + sb.cross_last()
    wa.held, wb.held, dec.held, x = gate(done, wa.held, wb.held, dec.held, x)

    g_all = small[:, self_rows:, :D].reshape(8 * chips, D)
    gw = lax.all_gather(nt(w_back[0], g_all), "dp").reshape(FF, 8 * chips)
    gw = lax.dynamic_slice_in_dim(gw, 8 * chip, 8, 1).T
    gw_got = across(gw)
    gw = jnp.where(first, gw_got, gw)
    self_own = small[:, :self_rows].reshape(chips * self_rows, 2 * D)
    gains_own = jnp.sum(small[:, self_rows:, D:].astype(F32), axis=0)
    self_got, gains_got = across(self_own), across(gains_own)
    gains0, gains1 = jnp.where(first, gains_own, gains_got), jnp.where(first, gains_got, gains_own)
    gains1 = jnp.where(jnp.arange(8)[:, None] == 2, gains0 + gains1, gains1)

    n1, q, k, v, c, h1, n2, lse = enc_attention(meta, x, gains0, segr, segc, windows, sa.sets(), sb.sets())
    done = wa.last(Y) + wb.last(X) + dec.step(Z0) + wa.cross() + wb.cross() + [h1]
    da_, db_ = dec.split(2 * GROUP)
    da_.held, db_.held, wa.last_got, wb.last_got, n1, c, n2 = gate(
        done, da_.held, db_.held, wa.last_got, wb.last_got, n1, c, n2
    )
    n1_got, c_got, n2_got = across(n1), across(c), across(n2)
    done = da_.step(X) + db_.step(Y) + wa.cross_last() + wb.cross_last() + [n1_got, c_got, n2_got]
    da_.held, db_.held, h1 = gate(done, da_.held, db_.held, h1)
    f, slope, e = enc_ffn(meta, h1, n2, wa.sets(), wb.sets())
    done = da_.last(Y) + db_.last(X) + da_.cross() + db_.cross() + [e, gw]
    da_.last_got, db_.last_got = gate(done, da_.last_got, db_.last_got)
    f_got = across(f)
    z = gate(da_.cross_last() + db_.cross_last(), dec_in)
    d1a, d1b = da_.sets(), db_.sets()
    m1, sv, z1, m2, qc, qk, gm = dec_before(meta, z, d_out, gains1, self_own, self_got, d1a)
    de, cc, z2, m3, fc, duc, da2, dz2, dcc, edt, ebar, dg_ffn1, de_other, pairs_other = dec_core(
        meta, e, segr, qk, qc, z1, gm, gw, gains1, d1b, d1a, d1b
    )

    def two(parts):
        return Sum(parts[0], parts[1], pre), Sum(parts[2], parts[3], pre)

    de_got, pairs_got = across(de_other), across(pairs_other)
    du, du_other = enc_hidden_grad(meta, de, slope, wb.sets())
    de_got, pairs_got, du_other = gate([de_got, pairs_got, du], de_got, pairs_got, du_other)
    du_got = across(du_other)
    back_a, back_b = two(enc_w_back_grad(meta, de, de_got, f, f_got))
    edt, back_a.send, back_b.send = gate([back_a.mine], edt, back_a.send, back_b.send)
    done = back_a.step(Y) + back_b.step(X)
    dqc, ds1, dsv, dec_grad, dg_attn1, dg_self, k_keep, k_send = dec_after(
        meta, dec_in, z1, dz2, qc, dcc, edt, ebar, pairs_got, gains1, self_own, self_got, d1a
    )
    h1, dqc = gate([dqc], h1, dqc)
    acts = jnp.concatenate([m1, sv, m2, cc, m3, da2, dqc, ds1, dsv, duc, fc], axis=1)
    width = acts.shape[1] // 2
    acts_got = across(lax.dynamic_slice_in_dim(acts, (1 - core) * width, width, 1))
    own = (jnp.arange(8)[:, None] // 4) == core
    acts = jnp.where(own, lax.dynamic_slice_in_dim(acts, core * width, width, 1), acts_got)
    acts = lax.all_gather(acts, "dp").reshape(8 * chips, width)
    dh1, da, dg_ffn0 = enc_ffn_back(meta, du, h1, de, gains0, wa.sets())
    n2, back_a.mine, back_b.mine = gate(done + [da, du_got], n2, back_a.mine, back_b.mine)
    done = back_a.step(X) + back_b.step(Y)
    in_a, in_b = two(enc_w_in_grad(meta, du, du_got, n2, n2_got))
    in_a.mine, in_a.send = jnp.concatenate([in_a.mine, k_keep], axis=1), jnp.concatenate([in_a.send, k_send], axis=1)
    da, in_a.send, in_b.send = gate([in_a.mine], da, in_a.send, in_b.send)
    done += in_a.step(Y) + in_b.step(X)
    dq, dk, dv, diag, other = enc_attention_back(meta, da, q, k, v, lse, segr, segc, windows, sb.sets())
    backs = merged([back_a, back_b])
    dq, other, in_a.mine, in_b.mine, backs.mine = gate(done + [dq], dq, other, in_a.mine, in_b.mine, backs.mine)
    got = across(other)
    done = in_a.step(X) + in_b.step(Y) + backs.step(Z0)
    keep, send, dg_attn0 = enc_input_grad(meta, dq, dk, dv, x, dh1, gains0, sa.sets(), sb.sets())
    dq, got = gate([got, dg_attn0], dq, got)
    square_a, square_b = two(enc_square_grads(meta, n1, n1_got, c, c_got, dq, dk, dv, da, got))
    ins = merged([in_a, in_b])
    acts, send, z2, ins.mine, backs.mine, square_a.send, square_b.send = gate(
        done + [square_a.mine], acts, send, z2, ins.mine, backs.mine, square_a.send, square_b.send
    )
    done = square_a.step(Y) + square_b.step(X) + ins.step(Z0) + backs.step(Z1)

    theirs = across(acts)
    dec_q, dec_o, dec_i, dec_b, g_self_value, g_self_out, y = dec_weight_grads(
        jnp.stack([chip, core]), jnp.where(first, acts, theirs), jnp.where(first, theirs, acts),
        g_all, w_back[0], rows, self_rows,
    )
    z2 = z2 + across(z2)
    square_a.mine, square_b.mine, ins.mine, y = gate(done + [dec_q], square_a.mine, square_b.mine, ins.mine, y)
    done = square_a.step(X) + square_b.step(Y) + ins.step(Z1)
    squares = merged([square_a, square_b])
    squares.mine = gate(done, squares.mine)
    done = squares.step(Z0)
    y = jnp.sum(lax.all_to_all(y.reshape(chips, 8, D), "dp", 0, 0).astype(F32), axis=0)
    squares.mine = gate(done, squares.mine)
    squares.step(Z1)
    backs_sum, ins_sum, square_sum = backs.total(), ins.total(), squares.total()
    dec_out = (z2 + y).astype(BF)
    dec_out = jnp.where(first, across(dec_out), dec_out)
    mine = chip * rows

    table = jnp.einsum("hdt,dtb->bh", diag, diagonal_onehots(), precision=lax.Precision.HIGHEST)
    little = jnp.concatenate([
        dg_attn0, dg_ffn0, dg_attn1, dg_ffn1, dg_self,
        jnp.pad(table.reshape(1, -1), ((0, 0), (0, D - BUCKETS * HEADS))), jnp.zeros((18, D), F32),
    ])
    little = jnp.sum(gate(done, lax.all_gather(little + across(little), "dp")), axis=0)
    g_rel_table = little[5, : BUCKETS * HEADS].reshape(BUCKETS, HEADS)

    def cut(index, at, count):
        return lax.dynamic_slice_in_dim(little[index], at, count, 0)

    g_attn_gain = cut(jnp.where(first, 0, 2), mine, rows)[None]
    g_ffn_gain = cut(jnp.where(first, 1, 3), mine, rows)[None]
    g_self_gain = cut(4, at_self, self_rows)

    backs_got, ins_got, square_got = [across(v.astype(BF)).astype(F32) for v in (backs_sum, ins_sum, square_sum)]

    def group(value, index):
        return value[index * GROUP : (index + 1) * GROUP]

    def placed(enc_value, dec_value):
        return jnp.where(first, narrowed(enc_value, pre, chip), dec_value)[None]

    g_w_query = placed(group(square_sum, 0), dec_q)
    g_w_out = placed(group(square_sum, 1), dec_o)
    g_w_key = narrowed(jnp.where(first, group(square_got, 0), group(ins_got, 1)), pre, chip)[None]
    g_w_value = narrowed(jnp.where(first, group(square_got, 1), group(ins_sum, 1)), pre, chip)[None]
    g_w_in = placed(
        jnp.concatenate([group(ins_sum, 0), group(ins_sum, 2), group(ins_got, 0), group(ins_got, 2)], axis=1), dec_i
    )
    half = D // 2
    tall = [
        jnp.concatenate([group(v, i)[:, j * half : (j + 1) * half] for i in range(2) for j in range(2)])
        for v in (backs_sum, backs_got)
    ]
    g_w_back = placed(jnp.concatenate(tall, axis=1), dec_b)

    other_half = across(send)
    enc_in_grad = jnp.where(first, jnp.stack([keep, other_half]), jnp.stack([other_half, keep]))
    dec_grad = dec_grad + across(dec_grad)
    half = D // 2
    dec_out = jnp.where(first, dec_out[:, :half], dec_out[:, half:])
    dec_in_grad = jnp.where(first, dec_grad[:, :half], dec_grad[:, half:])
    return (
        dec_out, enc_in_grad, dec_in_grad, g_attn_gain, g_w_query, g_w_key, g_w_value, g_w_out, g_ffn_gain,
        g_w_in, g_w_back, g_self_gain, g_self_value, g_self_out, g_rel_table,
    )


def solution(mesh):
    return jax.shard_map(
        per_device,
        mesh=mesh,
        in_specs=(
            P("dp", None, None),
            P("dp", None),
            P("dp", None),
            P("dp", None),
            P("section", "dp"),
            P("section", "dp", None),
            P("section", "dp", None),
            P("section", "dp", None),
            P("section", "dp", None),
            P("section", "dp"),
            P("section", "dp", None),
            P("section", "dp", None),
            P(("section", "dp")),
            P(("section", "dp"), None),
            P(("section", "dp"), None),
            P(),
        ),
        out_specs=(
            P("dp", "section"),
            P("dp", None, "section"),
            P("dp", "section"),
            P("section", "dp"),
            P("section", "dp", None),
            P("section", "dp", None),
            P("section", "dp", None),
            P("section", "dp", None),
            P("section", "dp"),
            P("section", "dp", None),
            P("section", "dp", None),
            P(("section", "dp")),
            P(("section", "dp"), None),
            P(("section", "dp"), None),
            P(),
        ),
        check_vma=False,
    )
```

```python
import functools

import jax
import jax.numpy as jnp
import numpy as np
from jax import lax
from jax.experimental import pallas as pl
from jax.experimental.pallas import tpu as pltpu
from jax.sharding import PartitionSpec as P

D = 768
HEADS = 12
HEAD_DIM = 64
FF = 3072
BUCKETS = 32
MAX_DIST = 128
ROW_LEN = 512
SEGS = 4
GROUP = 48
GROUPS = D // GROUP
X, Y, Z0, Z1 = 0, 1, 2, 3
TILE = 128
EPS = 1e-06
MASKED = -1000000000.0
BF = jnp.bfloat16
F32 = jnp.float32
SPEED = 0.25
VMEM_LIMIT = 58 * 1024 * 1024


def bucket_of(offset):
    half, exact = BUCKETS // 2, BUCKETS // 4
    exponent, growth = half - exact, MAX_DIST // exact
    distance = abs(offset)
    if distance < exact:
        level = distance
    else:
        k = 0
        while k < exponent and exact**exponent * growth ** (k + 1) <= distance**exponent:
            k += 1
        level = min(exact + k, half - 1)
    return (half if offset > 0 else 0) + level


def window_onehots():
    table = np.zeros((2, 3, 2 * TILE, BUCKETS), np.float32)
    for d in range(3):
        for t in range(2 * TILE):
            table[0, d, t, bucket_of(TILE * (d - 1) - TILE + t)] = 1.0
            table[1, d, t, bucket_of(TILE * (d - 1) + TILE - t)] = 1.0
    return table


def diagonal_onehots():
    table = np.zeros((5, 2 * TILE, BUCKETS), np.float32)
    table[1:4] = window_onehots()[1]
    table[0, :, bucket_of(-TILE - 1)] = 1.0
    table[4, :, bucket_of(TILE + 1)] = 1.0
    return table


def across(value):
    return lax.ppermute(value, "section", [(0, 1), (1, 0)])


def along(value, bit):
    count = lax.axis_size("dp")
    return lax.ppermute(value, "dp", [(i, i ^ (1 << bit)) for i in range(count)])


def bit_of(index, bit):
    return lax.rem(lax.div(index, 1 << bit), 2)


def low_bits(rows):
    count = 0
    while rows < GROUP:
        rows *= 2
        count += 1
    return count


def filled(piece, pre, chip, axis):
    for bit in range(pre):
        other = along(piece, bit)
        upper = bit_of(chip, bit) == 1
        first = jnp.where(upper, other, piece)
        second = jnp.where(upper, piece, other)
        piece = jnp.concatenate([first, second], axis=axis)
    return piece


def narrowed(total, pre, chip):
    for bit in reversed(range(pre)):
        length = total.shape[0] // 2
        upper = bit_of(chip, bit)
        kept = lax.dynamic_slice_in_dim(total, upper * length, length, 0)
        sent = lax.dynamic_slice_in_dim(total, (1 - upper) * length, length, 0)
        total = added(kept, along(sent.astype(BF), bit), F32)
    return total


def phase(*things):
    tree = [thing.arrays() if isinstance(thing, (Chain, Sum)) else thing for thing in things]
    out = []
    for thing, value in zip(things, lax.optimization_barrier(tree)):
        if isinstance(thing, (Chain, Sum)):
            thing.replace(value)
        else:
            out.append(value)
    return out[0] if len(out) == 1 else out


class Chain:
    def __init__(self, parts, ids, pre):
        self.parts, self.ids, self.pre = parts, ids, pre

    def arrays(self):
        return list(self.parts)

    def replace(self, values):
        self.parts = values

    def split(self, at):
        cut = [[part[:, :at] for part in self.parts], [part[:, at:] for part in self.parts]]
        return [Chain(parts, self.ids, self.pre) for parts in cut]

    def step(self, bit):
        held = self.parts[0] if len(self.parts) == 1 else jnp.concatenate(self.parts, axis=0)
        self.parts = [held, along(held, bit + self.pre)]
        self.old_ids = self.ids
        self.ids = self.ids + [g ^ (1 << bit) for g in self.ids]

    def sets(self, others):
        first, last = self.old_ids, self.ids[len(self.old_ids) :]
        return [(self.parts[0], first, 0), (self.parts[1], last, 0), (others[0], first, 1), (others[1], last, 1)]


def added(left, right, kind=BF):
    return (left.astype(F32) + right.astype(F32)).astype(kind)


class Sum:
    def __init__(self, keep, send, pre):
        self.mine, self.other, self.pre, self.fresh = keep, send, pre, True

    def arrays(self):
        return [self.mine, self.other]

    def replace(self, values):
        self.mine, self.other = values

    def step(self, bit):
        if self.fresh:
            send, self.fresh = self.other, False
        else:
            half = self.mine.shape[0] // 2
            send = added(self.mine[half:], self.other[half:])
            self.mine = added(self.mine[:half], self.other[:half])
        self.other = along(send, bit + self.pre)

    def total(self):
        return added(self.mine[0], self.other[0], F32)


def merged(sums):
    one = Sum(
        jnp.concatenate([part.mine for part in sums], axis=1),
        jnp.concatenate([part.other for part in sums], axis=1),
        sums[0].pre,
    )
    one.fresh = False
    return one


def nn(a, b):
    return lax.dot_general(a, b, (((1,), (0,)), ((), ())), preferred_element_type=F32)


def nt(a, b):
    return lax.dot_general(a, b, (((1,), (1,)), ((), ())), preferred_element_type=F32)


def tn(a, b):
    return lax.dot_general(a, b, (((0,), (0,)), ((), ())), preferred_element_type=F32)


def rms(v, gain):
    return v * lax.rsqrt(jnp.mean(v * v, axis=-1, keepdims=True) + EPS) * gain


def rms_back(v, gain, dy):
    r = lax.rsqrt(jnp.mean(v * v, axis=-1, keepdims=True) + EPS)
    dgain = jnp.sum(dy * v * r, axis=0, keepdims=True)
    dyg = dy * gain
    dv = r * dyg - v * (r * r * r) * jnp.mean(v * dyg, axis=-1, keepdims=True)
    return dv, dgain


def gelu_both(u):
    c = 0.7978845608028654
    t = jnp.tanh(c * (u + 0.044715 * u * u * u))
    value = 0.5 * u * (1.0 + t)
    slope = 0.5 * (1.0 + t) + (0.5 * c) * u * (1.0 - t * t) * (1.0 + 3 * 0.044715 * u * u)
    return value, slope


def square_row(b):
    return lambda core, g: (core * 2 + b) * D + GROUP * g


def back_row(b):
    return lambda core, g: 4 * GROUP * g + GROUP * (2 * core + b)


def in_items(first):
    return [(first + GROUP * b, GROUP, square_row(b), lambda core, g, b=b: 2 * core + b) for b in range(2)]


def in_sources(a_sets, b_sets):
    cut = 2 * GROUP // 3
    later = lambda core, g: square_row(1)(core, g) + cut
    block = lambda core, g: 2 * core + 1
    return [
        (a_sets, [(0, GROUP, square_row(0), lambda core, g: 2 * core), (GROUP, cut, square_row(1), block)]),
        (b_sets, [(GROUP, GROUP - cut, later, block)]),
    ]


def back_sources(b_sets, shared, first, got):
    quarter = lambda core, g: g // 4
    return [
        (b_sets, [(0, GROUP, back_row(0), quarter)]),
        ([(shared, None, 0)], [(first, GROUP, back_row(1), quarter)]),
        ([(got, None, 1)], [(0, GROUP, back_row(1), quarter)]),
    ]


def arrays_of(sources):
    return [part for sets, items in sources for part, ids, other in sets]


def start_sources(meta, refs, sources, dst, sems):
    at = 0
    for sets, items in sources:
        plan = [(ids, other) for part, ids, other in sets]
        start_fetch(meta, refs[at : at + len(plan)], plan, items, dst, sems)
        at += len(plan)


def start_fetch(meta, refs, plan, items, dst, sem, only=None):
    if only is not None:
        for other in range(2):
            part = [(ref, entry) for ref, entry in zip(refs, plan) if entry[1] == other]

            @pl.when(jnp.bitwise_xor(meta[1], other) == only)
            def _():
                start_fetch(meta, [r for r, e in part], [e for r, e in part], items, dst, sem)

        return
    me, core = meta[0], meta[1]
    for first, count, row_of, *sem_of in items:
        for ref, (ids, other) in zip(refs, plan):
            source = 1 - core if other else core
            for slot in range(ref.shape[0]):
                group = jnp.int32(slot) if ids is None else jnp.bitwise_xor(me, ids[slot])
                off = pl.multiple_of(row_of(source, group), 16)
                at = sem.at[sem_of[0](source, group)] if sem_of else sem
                pltpu.make_async_copy(ref.at[slot, pl.ds(first, count)], dst.at[pl.ds(off, count)], at).start()


def drain(ref, sem):
    pltpu.make_async_copy(ref, ref, sem).wait()


def slot_of(meta, group, b):
    rel = jnp.bitwise_xor(meta[0], group)
    x, y, z0, z1 = [jnp.bitwise_and(rel // (1 << bit), 1) for bit in range(4)]
    return (8 * y + 4 * x if b == 0 else 8 * x + 4 * y) + 2 * z0 + z1


def start_store(meta, src, group, b, keep, send, sem, rows=slice(None), cols=slice(None)):
    slot = slot_of(meta, group, b)
    at = (rows, cols)

    @pl.when(slot < GROUPS // 2)
    def _():
        pltpu.make_async_copy(src, keep.at[(slot,) + at], sem).start()

    @pl.when(slot >= GROUPS // 2)
    def _():
        pltpu.make_async_copy(src, send.at[(slot - GROUPS // 2,) + at], sem).start()


def head_lanes(h):
    lane = lax.broadcasted_iota(jnp.int32, (1, D), 1)
    return (lane >= h * HEAD_DIM) & (lane < (h + 1) * HEAD_DIM)


def pair_lanes(hh):
    lane = lax.broadcasted_iota(jnp.int32, (1, TILE), 1)
    return (lane < HEAD_DIM) if hh == 0 else (lane >= HEAD_DIM)


def masked(value, lanes):
    return jnp.where(lanes, value, jnp.zeros_like(value))


def fill_bias(window_ref, tiles, transposed):
    part = 1 if transposed else 0

    def one(h, carry):
        for d in range(3):
            row = jnp.broadcast_to(window_ref[h, pl.ds(part * 3 + d, 1), :], (TILE, 2 * TILE))
            rolled = pltpu.roll(row, TILE, 1, stride=1, stride_axis=0)
            tiles[h, d + 1] = rolled[:, :TILE]
        low = window_ref[h, pl.ds(0, 1), pl.ds(0, 1)]
        high = window_ref[h, pl.ds(2, 1), pl.ds(2 * TILE - 1, 1)]
        tiles[h, 0] = jnp.broadcast_to(low, (TILE, TILE))
        tiles[h, 4] = jnp.broadcast_to(high, (TILE, TILE))
        return carry

    lax.fori_loop(0, HEADS, one, 0)


def whole(space=pltpu.VMEM):
    return pl.BlockSpec(memory_space=space)


def call(body, name, ins, spaces, outs, out_spaces, scratch, us, aliases={}):
    return pl.pallas_call(
        body,
        name=name,
        in_specs=[whole(s) for s in spaces],
        out_specs=[whole(s) for s in out_spaces],
        out_shape=[jax.ShapeDtypeStruct(s, k) for s, k in outs],
        scratch_shapes=scratch,
        input_output_aliases=aliases,
        compiler_params=pltpu.CompilerParams(vmem_limit_bytes=VMEM_LIMIT),
        cost_estimate=pl.CostEstimate(flops=int(us * SPEED * 1.1e9), bytes_accessed=int(us * SPEED * 1e6), transcendentals=0),
    )(*ins)


VM, SM, ANY = pltpu.VMEM, pltpu.SMEM, pl.ANY


def plan_of(sets):
    return [part for part, ids, other in sets], [(ids, other) for part, ids, other in sets]


def enc_attention(meta, x, gains, segr, segc, windows, a_sets, b_sets):
    a_arrays, a_plan = plan_of(a_sets)
    b_arrays, b_plan = plan_of(b_sets)
    n = len(a_arrays)

    def body(meta, x, gains, segr, segc, windows, *rest):
        a_parts, b_parts, rest = rest[:n], rest[n : 2 * n], rest[2 * n :]
        n1, q, k, v, c, h1, n2, lse, w, tiles, lcol, sems = rest
        start_fetch(meta, a_parts, a_plan, [(0, GROUP, square_row(0))], w, sems.at[0])
        start_fetch(meta, b_parts, b_plan, [(0, GROUP, square_row(1))], w, sems.at[0])
        fill_bias(windows, tiles, False)
        xf = x[...].astype(F32)
        n1[...] = rms(xf, gains[0:1, :]).astype(BF)
        drain(w, sems.at[0])
        for ref, at in ((q, 0), (k, 2), (v, 3)):
            ref[...] = nn(n1[...], w[at * D : (at + 1) * D, :]).astype(BF)
        lane = lax.broadcasted_iota(jnp.int32, (1, TILE), 1)
        lcol[...] = jnp.zeros_like(lcol)

        def pair(pr, carry):
            cols = pl.ds(pl.multiple_of(pr * TILE, TILE), TILE)
            kp, vp = k[:, cols], v[:, cols]
            for ib in range(ROW_LEN // TILE):
                rows = slice(ib * TILE, (ib + 1) * TILE)
                same = segc[rows, :] == segr[...]
                qp = q[rows, cols]
                total = jnp.zeros((TILE, TILE), F32)
                for hh in range(2):
                    h = 2 * pr + hh
                    lanes = pair_lanes(hh)
                    bias = jnp.concatenate(
                        [tiles[h, min(max(jb - ib, -2), 2) + 2] for jb in range(ROW_LEN // TILE)], axis=1
                    )
                    s = jnp.where(same, nt(masked(qp, lanes), kp) + bias, MASKED)
                    top = jnp.max(s, axis=-1, keepdims=True)
                    ex = jnp.exp(s - top)
                    tot = jnp.sum(ex, axis=-1, keepdims=True)
                    p = (ex * (1.0 / tot)).astype(BF)
                    total = total + nn(p, masked(vp, lanes))
                    lcol[rows, :] = jnp.where(lane == h, top + jnp.log(tot), lcol[rows, :])
                c[rows, cols] = total.astype(BF)
            return carry

        lax.fori_loop(0, HEADS // 2, pair, 0)
        lse[...] = lcol[...].T
        res = x[...].astype(F32) + nn(c[...], w[D : 2 * D, :])
        h1[...] = res
        n2[...] = rms(res, gains[1:2, :]).astype(BF)

    rows = (ROW_LEN, D)
    return call(
        body, "enc_attention", [meta, x, gains, segr, segc, windows, *a_arrays, *b_arrays],
        [SM, VM, VM, VM, VM, VM] + [ANY] * (2 * n),
        [(rows, BF)] * 5 + [(rows, F32), (rows, BF), ((TILE, ROW_LEN), F32), ], [VM] * 8,
        [pltpu.VMEM((4 * D, D), BF), pltpu.VMEM((HEADS, 5, TILE, TILE), F32), pltpu.VMEM((ROW_LEN, TILE), F32), pltpu.SemaphoreType.DMA((2,))],
        us=20,
    )


def enc_ffn(meta, h1, n2, w_in_from, w_back_from):
    in_arrays, back_arrays = arrays_of(w_in_from), arrays_of(w_back_from)
    n, m = len(in_arrays), len(back_arrays)

    def body(meta, h1, n2, *rest):
        ins, backs, rest = rest[:n], rest[n : n + m], rest[n + m :]
        f, slope, e, w_in, w_back, acc, sems = rest
        start_sources(meta, ins, w_in_from, w_in, sems)
        start_sources(meta, backs, w_back_from, w_back, sems.at[pl.ds(4, 4)])
        acc[...] = h1[...]

        def block(b, carry):
            rows = pl.ds(pl.multiple_of(b * D, D), D)

            drain(w_in.at[rows], sems.at[b])
            value, grad = gelu_both(nn(n2[...], w_in[rows, :]))
            fb = value.astype(BF)
            f[:, rows] = fb
            slope[:, rows] = grad.astype(BF)
            drain(w_back.at[rows], sems.at[4 + b])
            acc[...] += nn(fb, w_back[rows, :])
            return carry

        lax.fori_loop(0, FF // D, block, 0)
        e[...] = acc[...].astype(BF)

    return call(
        body, "enc_ffn", [meta, h1, n2, *in_arrays, *back_arrays], [SM, VM, VM] + [ANY] * (n + m),
        [((ROW_LEN, FF), BF), ((ROW_LEN, FF), BF), ((ROW_LEN, D), BF)], [VM] * 3,
        [pltpu.VMEM((FF, D), BF), pltpu.VMEM((FF, D), BF), pltpu.VMEM((ROW_LEN, D), F32),
         pltpu.SemaphoreType.DMA((8,))],
        us=15,
    )


PART = (GROUPS // 2, GROUP, D)
WIDE_PART = (GROUPS // 2, 2 * GROUP, D)


def enc_hidden_grad(meta, de, slope, w_back_from):
    arrays = arrays_of(w_back_from)
    n = len(arrays)

    def body(meta, de, slope, *rest):
        parts, rest = rest[:n], rest[n:]
        du, other, w, sems = rest
        start_sources(meta, parts, w_back_from, w, sems)
        for b in range(FF // D):
            cols = slice(b * D, (b + 1) * D)
            drain(w.at[cols], sems.at[b])
            value = (slope[:, cols].astype(F32) * nt(de[...], w[cols, :])).astype(BF)
            du[:, cols] = value

            @pl.when(meta[1] != b // 2)
            def _():
                other[:, (b % 2) * D : (b % 2 + 1) * D] = value

    return call(
        body, "enc_hidden_grad", [meta, de, slope, *arrays], [SM, VM, VM] + [ANY] * n,
        [((ROW_LEN, FF), BF), ((ROW_LEN, FF // 2), BF)], [VM, VM],
        [pltpu.VMEM((FF, D), BF), pltpu.SemaphoreType.DMA((4,))],
        us=8,
    )


def enc_w_back_grad(meta, de, de_got, f, f_got):
    half = D // 2

    def body(meta, de, de_got, f, f_got, keep_a, send_a, keep_b, send_b, mine, buf, sems):
        mine[...] = de[:, pl.ds(pl.multiple_of(meta[1] * half, TILE), half)]
        for b in range(FF // D):
            cols = slice(b * D, (b + 1) * D)
            at = b % 2
            if b >= 2:
                drain(buf.at[at], sems.at[at])
            buf[at] = (tn(f[:, cols], mine[...]) + tn(f_got[:, cols], de_got[...])).astype(BF)
            for k in range(D // GROUP):
                group, piece = b * (D // GROUP // 4) + k // 4, k % 4
                keep, send = (keep_a, send_a) if piece < 2 else (keep_b, send_b)
                start_store(meta, buf.at[at, pl.ds(k * GROUP, GROUP)], group, piece // 2, keep, send, sems.at[at],
                            cols=pl.ds((piece % 2) * half, half))
        drain(buf.at[0], sems.at[0])
        drain(buf.at[1], sems.at[1])

    return call(
        body, "enc_w_back_grad", [meta, de, de_got, f, f_got], [SM] + [VM] * 4,
        [(PART, BF)] * 4, [ANY] * 4,
        [pltpu.VMEM((ROW_LEN, half), BF), pltpu.VMEM((2, D, half), BF), pltpu.SemaphoreType.DMA((2,))],
        us=7,
    )


def enc_w_in_grad(meta, du, du_got, n2, n2_got, wide_keep, wide_send):
    def body(meta, du, du_got, n2, n2_got, wide_keep, wide_send, keep_a, send_a, keep_b, send_b, buf, sems):
        for b in range(2):
            cols = pl.ds(pl.multiple_of(meta[1] * (FF // 2) + b * D, TILE), D)
            buf[b] = (tn(n2[...], du[:, cols]) + tn(n2_got[...], du_got[:, b * D : (b + 1) * D])).astype(BF)
            keep, send = (keep_a, send_a) if b == 0 else (keep_b, send_b)
            for g in range(GROUPS):
                rows = pl.ds(0, GROUP)
                start_store(meta, buf.at[b, pl.ds(g * GROUP, GROUP)], g, b, keep, send, sems.at[b], rows)
        drain(buf.at[0], sems.at[0])
        drain(buf.at[1], sems.at[1])

    return call(
        body, "enc_w_in_grad", [meta, du, du_got, n2, n2_got, wide_keep, wide_send], [SM] + [VM] * 4 + [ANY] * 2,
        [(WIDE_PART, BF), (WIDE_PART, BF), (PART, BF), (PART, BF)], [ANY] * 4,
        [pltpu.VMEM((2, D, D), BF), pltpu.SemaphoreType.DMA((2,))],
        us=7, aliases={5: 0, 6: 1},
    )


def enc_ffn_back(meta, du, h1, de, gains, w_in_from):
    arrays = arrays_of(w_in_from)
    n = len(arrays)

    def body(meta, du, h1, de, gains, *rest):
        parts, rest = rest[:n], rest[n:]
        dh1, da, dgain, w, acc, sems = rest
        start_sources(meta, parts, w_in_from, w, sems)
        for k, b in enumerate((0, 2, 1, 3)):
            cols = slice(b * D, (b + 1) * D)
            drain(w.at[cols], sems.at[b])
            part = nt(du[:, cols], w[cols, :])
            acc[...] = part if k == 0 else acc[...] + part
        dv, dg = rms_back(h1[...], gains[1:2, :], acc[...])
        total = de[...].astype(F32) + dv
        dh1[...] = total
        da[...] = total.astype(BF)
        dgain[...] = dg

    rows = (ROW_LEN, D)
    return call(
        body, "enc_ffn_back", [meta, du, h1, de, gains, *arrays], [SM, VM, VM, VM, VM] + [ANY] * n,
        [(rows, F32), (rows, BF), ((1, D), F32)], [VM, VM, VM],
        [pltpu.VMEM((FF, D), BF), pltpu.VMEM(rows, F32), pltpu.SemaphoreType.DMA((4,))],
        us=8,
    )


def enc_attention_back(meta, da, q, k, v, lse, segr, segc, windows, sets):
    arrays, plan = plan_of(sets)
    n = len(arrays)
    wide = 2 * TILE

    def body(meta, da, q, k, v, lse, segr, segc, windows, *rest):
        parts, rest = rest[:n], rest[n:]
        dq, dk, dv, diag, other, w, dc, tiles, sums, kacc, vacc, sem = rest
        start_fetch(meta, parts, plan, [(0, GROUP, lambda core, g: GROUP * g)], w, sem, only=0)
        fill_bias(windows, tiles, True)
        drain(w, sem)
        dc[...] = nt(da[...], w[...]).astype(BF)
        row = lax.broadcasted_iota(jnp.int32, (TILE, TILE), 0)
        col = lax.broadcasted_iota(jnp.int32, (TILE, TILE), 1)
        flip = (row + col == TILE - 1).astype(F32)

        def pair(pr, carry):
            cols = pl.ds(pl.multiple_of(pr * TILE, TILE), TILE)
            for hh in range(2):
                h = 2 * pr + hh
                lanes = pair_lanes(hh)
                km, vm = masked(k[:, cols], lanes), masked(v[:, cols], lanes)
                sums[...] = jnp.zeros_like(sums)
                for ib in range(ROW_LEN // wide):
                    rows = slice(ib * wide, (ib + 1) * wide)
                    same = segc[...] == segr[:, rows]
                    qp, dcp = q[rows, cols], dc[rows, cols]
                    bias = jnp.concatenate([
                        jnp.concatenate([
                            tiles[h, min(max(jb - (2 * ib + i), -2), 2) + 2] for i in range(2)
                        ], axis=1) for jb in range(ROW_LEN // TILE)
                    ], axis=0)
                    s = jnp.where(same, nt(km, qp) + bias, MASKED)
                    prob = jnp.exp(s - lse[pl.ds(h, 1), rows])
                    dprob = nt(vm, dcp)
                    inner = jnp.sum(prob * dprob, axis=0, keepdims=True)
                    ds = (prob * (dprob - inner)).astype(BF)
                    dvp = nn(prob.astype(BF), masked(dcp, lanes))
                    dkp = nn(ds, masked(qp, lanes))
                    dqp = tn(ds, km)
                    if hh == 0 and ib == 0:
                        vacc[...], kacc[...] = dvp, dkp
                    else:
                        vacc[...] += dvp
                        kacc[...] += dkp
                    if hh == 0:
                        dq[rows, cols] = dqp.astype(BF)
                    else:
                        dq[rows, cols] = dq[rows, cols] + dqp.astype(BF)
                    for jb in range(ROW_LEN // TILE):
                        for i in range(2):
                            d = min(max(jb - (2 * ib + i), -2), 2) + 2
                            sums[d] += ds[jb * TILE : (jb + 1) * TILE, i * TILE : (i + 1) * TILE].astype(F32)
                for d in range(5):
                    if d in (0, 4):
                        line = jnp.sum(sums[d], axis=0, keepdims=True)
                        diag[h, d : d + 1, :] = jnp.concatenate([line, jnp.zeros_like(line)], axis=1)
                    else:
                        turned = lax.dot_general(
                            flip, sums[d], (((1,), (0,)), ((), ())),
                            precision=lax.Precision.HIGHEST, preferred_element_type=F32,
                        )
                        wider = jnp.concatenate([turned, jnp.zeros_like(turned)], axis=1)
                        rolled = pltpu.roll(wider, 1, 1, stride=1, stride_axis=0)
                        diag[h, d : d + 1, :] = jnp.sum(rolled, axis=0, keepdims=True)
            dk[:, cols] = kacc[...].astype(BF)
            dv[:, cols] = vacc[...].astype(BF)
            return carry

        lax.fori_loop(0, HEADS // 2, pair, 0)

        @pl.when(meta[1] == 0)
        def _():
            other[0] = dk[...]
            other[1] = dv[...]

        @pl.when(meta[1] != 0)
        def _():
            other[0] = dq[...]
            other[1] = da[...]

    rows = (ROW_LEN, D)
    return call(
        body, "enc_attention_back", [meta, da, q, k, v, lse, segr, segc, windows, *arrays],
        [SM] + [VM] * 8 + [ANY] * n,
        [(rows, BF), (rows, BF), (rows, BF), ((HEADS, 5, 2 * TILE), F32), ((2,) + rows, BF)], [VM] * 5,
        [pltpu.VMEM((D, D), BF), pltpu.VMEM(rows, BF), pltpu.VMEM((HEADS, 5, TILE, TILE), F32),
         pltpu.VMEM((5, TILE, TILE), F32), pltpu.VMEM((ROW_LEN, TILE), F32), pltpu.VMEM((ROW_LEN, TILE), F32),
         pltpu.SemaphoreType.DMA],
        us=25,
    )


def enc_square_grads(meta, n1, n1_got, c, c_got, dq, dk, dv, da, got):
    def body(meta, n1, n1_got, c, c_got, dq, dk, dv, da, got, keep_a, send_a, keep_b, send_b, buf, sems):
        for core, (one, left, left_got, two) in enumerate(((dq, c, c_got, da), (dk, n1, n1_got, dv))):

            @pl.when(meta[1] == core)
            def _():
                buf[0] = (tn(n1[...], one[...]) + tn(n1_got[...], got[0])).astype(BF)
                for g in range(GROUPS):
                    start_store(meta, buf.at[0, pl.ds(g * GROUP, GROUP)], g, 0, keep_a, send_a, sems.at[0])
                buf[1] = (tn(left[...], two[...]) + tn(left_got[...], got[1])).astype(BF)
                for g in range(GROUPS):
                    start_store(meta, buf.at[1, pl.ds(g * GROUP, GROUP)], g, 1, keep_b, send_b, sems.at[1])

        drain(buf.at[0], sems.at[0])
        drain(buf.at[1], sems.at[1])

    return call(
        body, "enc_square_grads", [meta, n1, n1_got, c, c_got, dq, dk, dv, da, got], [SM] + [VM] * 9,
        [(PART, BF)] * 4, [ANY] * 4,
        [pltpu.VMEM((2, D, D), BF), pltpu.SemaphoreType.DMA((2,))],
        us=6,
    )


def enc_input_grad(meta, dq, dk, dv, x, dh1, gains, a_sets, b_sets):
    a_arrays, a_plan = plan_of(a_sets)
    b_arrays, b_plan = plan_of(b_sets)
    n = len(a_arrays)

    def body(meta, dq, dk, dv, x, dh1, gains, *rest):
        a_parts, b_parts, rest = rest[:n], rest[n : 2 * n], rest[2 * n :]
        keep, send, dgain, w, sem = rest
        start_fetch(meta, a_parts, a_plan, [(0, GROUP, lambda core, g: core * D + GROUP * g)], w, sem)
        start_fetch(meta, b_parts, b_plan, [(0, GROUP, lambda core, g: 2 * D + GROUP * g)], w, sem, only=1)
        drain(w, sem)
        total = nt(dq[...], w[0:D, :]) + nt(dk[...], w[D : 2 * D, :]) + nt(dv[...], w[2 * D :, :])
        dx, dg = rms_back(x[...].astype(F32), gains[0:1, :], total)
        out = (dh1[...] + dx).astype(BF)
        dgain[...] = dg
        half = D // 2

        @pl.when(meta[1] == 0)
        def _():
            keep[...] = out[:, :half]
            send[...] = out[:, half:]

        @pl.when(meta[1] != 0)
        def _():
            keep[...] = out[:, half:]
            send[...] = out[:, :half]

    return call(
        body, "enc_input_grad", [meta, dq, dk, dv, x, dh1, gains, *a_arrays, *b_arrays],
        [SM] + [VM] * 6 + [ANY] * (2 * n),
        [((ROW_LEN, D // 2), BF), ((ROW_LEN, D // 2), BF), ((1, D), F32)], [VM] * 3,
        [pltpu.VMEM((3 * D, D), BF), pltpu.SemaphoreType.DMA],
        us=8,
    )


def spread_heads(value):
    return jnp.concatenate([masked(value, head_lanes(h)) for h in range(HEADS)], axis=0)


def join_heads(value):
    total = jnp.zeros((8, D), F32)
    for h in range(HEADS):
        total = total + masked(value[8 * h : 8 * h + 8, :], head_lanes(h))
    return total


def own_rows(meta):
    row = lax.broadcasted_iota(jnp.int32, (8, 1), 0)
    return (row >= 4 * meta[1]) & (row < 4 * meta[1] + 4)


def start_self(meta, own, got, dst, sem):
    half = D // 2
    pltpu.make_async_copy(own, dst.at[pl.ds(pl.multiple_of(meta[1] * half, 16), half)], sem).start()
    pltpu.make_async_copy(got, dst.at[pl.ds(pl.multiple_of((1 - meta[1]) * half, 16), half)], sem).start()


def dec_before(meta, z, d_out, gains, self_own, self_got, sets):
    arrays, plan = plan_of(sets)
    n = len(arrays)

    def body(meta, z, d_out, gains, self_own, self_got, *rest):
        parts, rest = rest[:n], rest[n:]
        m1, sv, z1, m2, qc, qk, gm, w_self, w, sems = rest
        start_self(meta, self_own, self_got, w_self, sems.at[0])
        start_fetch(meta, parts, plan, [(0, GROUP, lambda core, g: core * D + GROUP * g)], w, sems.at[1])
        zf = z[...].astype(F32)
        gm[...] = jnp.where(own_rows(meta), d_out[...].astype(F32), 0.0).astype(BF)
        m1v = rms(zf, gains[2:3, :]).astype(BF)
        drain(w_self, sems.at[0])
        drain(w, sems.at[1])
        svv = nn(m1v, w_self[:, :D]).astype(BF)
        z1v = zf + nn(svv, w_self[:, D:])
        m2v = rms(z1v, gains[0:1, :]).astype(BF)
        qcv = nn(m2v, w[0:D, :]).astype(BF)
        qk[...] = nt(spread_heads(qcv), w[D:, :]).astype(BF)
        m1[...], sv[...], z1[...], m2[...], qc[...] = m1v, svv, z1v, m2v, qcv

    rows = (8, D)
    return call(
        body, "dec_before", [meta, z, d_out, gains, self_own, self_got, *arrays],
        [SM, VM, VM, VM, ANY, ANY] + [ANY] * n,
        [(rows, BF), (rows, BF), (rows, F32), (rows, BF), (rows, BF), ((8 * HEADS, D), BF), (rows, BF)], [VM] * 7,
        [pltpu.VMEM((D, 2 * D), BF), pltpu.VMEM((2 * D, D), BF), pltpu.SemaphoreType.DMA((2,))],
        us=6,
    )


def dec_core(meta, e, segr, qk, qc, z1, g, gw, gains, sets):
    arrays, plan = plan_of(sets)
    n = len(arrays)

    def body(meta, e, segr, qk, qc, z1, g, gw, gains, *rest):
        parts, rest = rest[:n], rest[n:]
        de, cc, z2, m3, fc, duc, da2, dz2, dcc, edt, ebar, dgain, de_other, pairs_other, w, w_in, sems = rest
        start_fetch(meta, parts, plan, [(GROUP, GROUP, lambda core, g: core * D + GROUP * g)], w, sems.at[0])
        start_fetch(meta, parts, plan, in_items(2 * GROUP), w_in, sems.at[pl.ds(1, 4)])
        pairs = lax.broadcasted_iota(jnp.int32, (8 * HEADS, 1), 0)
        owner = segr[...] == jnp.bitwise_and(pairs, 7) - 4 * meta[1]
        t = jnp.where(owner, nt(qk[...], e[...]), MASKED)
        ex = jnp.where(owner, jnp.exp(t - jnp.max(t, axis=-1, keepdims=True)), 0.0)
        tot = jnp.sum(ex, axis=-1, keepdims=True)
        prob = ex * (1.0 / jnp.where(tot > 0.0, tot, 1.0))
        pc = prob.astype(BF)
        ebv = nn(pc, e[...]).astype(BF)
        ebar[...] = ebv
        drain(w, sems.at[0])
        ccv = join_heads(nn(ebv, w[D:, :])).astype(BF)
        z2v = z1[...] + nn(ccv, w[0:D, :])
        m3v = rms(z2v, gains[1:2, :]).astype(BF)
        dm3 = jnp.zeros((8, D), F32)
        own = own_rows(meta)
        for b in (0, 2, 1, 3):
            cols = slice(b * D, (b + 1) * D)
            drain(w_in.at[cols], sems.at[1 + b])
            value, slope = gelu_both(nn(m3v, w_in[cols, :]))
            fc[:, cols] = jnp.where(own, value, 0.0).astype(BF)
            ducv = jnp.where(own, slope * gw[:, cols].astype(F32), 0.0).astype(BF)
            duc[:, cols] = ducv
            dm3 = dm3 + nt(ducv, w_in[cols, :])
        back, dg = rms_back(z2v, gains[1:2, :], dm3)
        dz2v = g[...].astype(F32) + back
        da2v = dz2v.astype(BF)
        dccv = nt(da2v, w[0:D, :]).astype(BF)
        dvw = nt(spread_heads(dccv), w[D:, :]).astype(BF)
        dprob = nt(dvw, e[...])
        dt = (prob * (dprob - jnp.sum(prob * dprob, axis=-1, keepdims=True))).astype(BF)
        de[...] = tn(jnp.concatenate([pc, dt], axis=0), jnp.concatenate([dvw, qk[...]], axis=0)).astype(BF)
        edt[...] = nn(dt, e[...]).astype(BF)
        cc[...], m3[...], da2[...], dz2[...], dcc[...], dgain[...] = ccv, m3v, da2v, dz2v, dccv, dg
        z2[...] = jnp.where(own, z2v, 0.0)
        half = D // 2
        pairs_other[8 * HEADS + 8 :, :] = jnp.zeros((8, D), BF)

        @pl.when(meta[1] == 0)
        def _():
            de_other[...] = de[:, half:]
            pairs_other[: 8 * HEADS, :] = ebv
            pairs_other[8 * HEADS : 8 * HEADS + 8, :] = dccv

        @pl.when(meta[1] != 0)
        def _():
            de_other[...] = de[:, :half]
            pairs_other[: 8 * HEADS, :] = edt[...]
            pairs_other[8 * HEADS : 8 * HEADS + 8, :] = qc[...]

    rows, spread = (8, D), (8 * HEADS, D)
    return call(
        body, "dec_core", [meta, e, segr, qk, qc, z1, g, gw, gains, *arrays],
        [SM] + [VM] * 8 + [ANY] * n,
        [((ROW_LEN, D), BF), (rows, BF), (rows, F32), (rows, BF), ((8, FF), BF), ((8, FF), BF), (rows, BF),
         (rows, F32), (rows, BF), (spread, BF), (spread, BF), ((1, D), F32),
         ((ROW_LEN, D // 2), BF), ((8 * HEADS + 16, D), BF)], [VM] * 14,
        [pltpu.VMEM((2 * D, D), BF), pltpu.VMEM((FF, D), BF), pltpu.SemaphoreType.DMA((5,))],
        us=10,
    )


def dec_after(meta, z, z1, dz2, qc, dcc, edt, ebar, got, gains, self_own, self_got, sets):
    arrays, plan = plan_of(sets)
    n = len(arrays)

    def body(meta, z, z1, dz2, qc, dcc, edt, ebar, got, gains, self_own, self_got, *rest):
        parts, rest = rest[:n], rest[n:]
        dqc, ds1, dsv, dec_grad, dg_attn, dg_self, keep, send, w_self, w, buf, sems = rest
        start_fetch(meta, parts, plan, [(0, GROUP, lambda core, g: core * D + GROUP * g)], w, sems.at[1])
        start_self(meta, self_own, self_got, w_self, sems.at[0])
        zero = meta[1] == 0
        left = jnp.concatenate([jnp.where(zero, edt[...], ebar[...]), got[: 8 * HEADS, :]], axis=0)
        right = jnp.where(zero, qc[...], dcc[...])
        right = jnp.concatenate([spread_heads(right), spread_heads(got[8 * HEADS : 8 * HEADS + 8, :])], axis=0)
        buf[...] = tn(left, right).astype(BF)
        for grp in range(GROUPS):
            start_store(meta, buf.at[pl.ds(grp * GROUP, GROUP)], grp, 0, keep, send, sems.at[3], pl.ds(GROUP, GROUP))
        drain(w, sems.at[1])
        dqv = join_heads(nn(edt[...], w[D:, :])).astype(BF)
        back, dg = rms_back(z1[...], gains[0:1, :], nt(dqv, w[0:D, :]))
        dz1 = dz2[...] + back
        ds1v = dz1.astype(BF)
        drain(w_self, sems.at[0])
        dsvv = nt(ds1v, w_self[:, D:]).astype(BF)
        back0, dg0 = rms_back(z[...].astype(F32), gains[2:3, :], nt(dsvv, w_self[:, :D]))
        own = own_rows(meta)
        dec_grad[...] = jnp.where(own, dz1 + back0, 0.0).astype(BF)
        dqc[...], ds1[...], dsv[...], dg_attn[...], dg_self[...] = dqv, ds1v, dsvv, dg, dg0
        drain(buf, sems.at[3])

    rows = (8, D)
    return call(
        body, "dec_after",
        [meta, z, z1, dz2, qc, dcc, edt, ebar, got, gains, self_own, self_got, *arrays],
        [SM] + [VM] * 9 + [ANY] * (2 + n),
        [(rows, BF)] * 4 + [((1, D), F32)] * 2 + [(WIDE_PART, BF)] * 2, [VM] * 6 + [ANY] * 2,
        [pltpu.VMEM((D, 2 * D), BF), pltpu.VMEM((2 * D, D), BF), pltpu.VMEM((D, D), BF),
         pltpu.SemaphoreType.DMA((4,))],
        us=6,
    )


def dec_weight_grads(place, own, got, g_all, w_back, rows, self_rows):
    def body(place, own, got, *rest):
        for core, (left, right) in enumerate(((own, got), (got, own))):
            pl.when(place[1] == core)(functools.partial(halves, place, left, right, *rest))

    def halves(place, left, right, g_all, w_back, dec_q, dec_o, dec_i, dec_b, self_v, self_o, y):
        half = left.shape[1]
        chip, core = place[0], place[1]
        chips = D // rows

        def cut(at, width):
            parts = []
            while width:
                ref, first = (left, at) if at < half else (right, at - half)
                count = min(width, half - first)
                parts.append(ref[:, first : first + count])
                at, width = at + count, width - count
            return parts[0] if len(parts) == 1 else jnp.concatenate(parts, axis=1)

        def picked(at, first, count, width=D):
            row = lax.broadcasted_iota(jnp.int32, (count, width), 0) + first
            col = lax.broadcasted_iota(jnp.int32, (count, width), 1)
            return nt((row == col).astype(F32).astype(BF), cut(at * D, width)).astype(BF)

        first, first_self = chip * rows, (core * chips + chip) * self_rows
        m1, sv, m2, cc, m3, da2, dqc, ds1, dsv, duc, fc = list(range(10)) + [13]
        dec_q[...] = nn(picked(m2, first, rows), cut(dqc * D, D))
        dec_o[...] = nn(picked(cc, first, rows), cut(da2 * D, D))
        dec_i[...] = nn(picked(m3, first, rows), cut(duc * D, FF))
        self_v[...] = nn(picked(m1, first_self, self_rows), cut(dsv * D, D))
        self_o[...] = nn(picked(sv, first_self, self_rows), cut(ds1 * D, D))
        hidden = picked(fc, 4 * first, 4 * rows, FF)
        dec_b[...] = nn(hidden, g_all[...])
        y[...] = tn(hidden, w_back[...]).astype(BF)

    return call(
        body, "dec_weight_grads", [place, own, got, g_all, w_back], [SM, VM, VM, VM, VM],
        [((rows, D), F32), ((rows, D), F32), ((rows, FF), F32), ((4 * rows, D), F32), ((self_rows, D), F32),
         ((self_rows, D), F32), (g_all.shape, BF)], [VM] * 7,
        [], us=5,
    )


def pieces(w_query, w_key, w_value, w_out, w_in, w_back):
    ins = [w_in[:, b * D : (b + 1) * D] for b in range(4)]
    backs = [w_back[b * GROUP : (b + 1) * GROUP] for b in range(4)]
    return jnp.stack([
        jnp.concatenate([w_query, w_out] + ins[:2] + backs[:2]), jnp.concatenate([w_key, w_value] + ins[2:] + backs[2:])
    ])


def dec_pieces(w_query, w_key, w_value, w_out, w_in):
    ins = [w_in[:, b * D : (b + 1) * D] for b in range(4)]
    return jnp.stack([jnp.concatenate([w_query, w_out] + ins[:2]), jnp.concatenate([w_key, w_value] + ins[2:])])


def by_group(pieces_of, pre):
    one = pieces_of.reshape(GROUPS, 2**pre, 4, GROUP // 2**pre, D)
    return one.transpose(0, 2, 1, 3, 4).reshape(GROUPS, 4 * GROUP, D)


def per_device(
    enc_in, dec_in, segment, d_out, attn_gain, w_query, w_key, w_value, w_out, ffn_gain, w_in, w_back,
    self_gain, self_value, self_out, rel_table,
):
    core, chip = lax.axis_index("section"), lax.axis_index("dp")
    chips = lax.axis_size("dp")
    rows = w_query.shape[1]
    first = core == 0
    pre = low_bits(rows)
    meta = jnp.stack([chip >> pre, core]).astype(jnp.int32)
    self_rows = self_value.shape[0]
    at_self = (core * chips + chip) * self_rows

    weights = [w[0] for w in (w_query, w_key, w_value, w_out, w_in, w_back)]
    enc_both = pieces(*[filled(w, pre, chip, 0) for w in weights])
    dec_both = dec_pieces(*weights[:5])
    sent = jnp.zeros(enc_both.shape[1:], BF)
    sent = lax.dynamic_update_slice(sent, dec_both[0], (0, 0))
    got = across(jnp.where(first, enc_both[1], sent))
    enc_piece = jnp.where(first, enc_both[0], got)
    dec_piece = jnp.where(first, got[: dec_both.shape[1]], dec_both[1])

    shared = lax.all_gather(jnp.concatenate([dec_piece, self_value, self_out, enc_piece[5 * GROUP :]]), "dp")

    gains = jnp.zeros((8, D), BF)
    gains = lax.dynamic_update_slice(gains, jnp.concatenate([attn_gain, ffn_gain]), (0, chip * rows))
    gains = lax.dynamic_update_slice(gains, self_gain[None], (2, at_self))
    little = Chain([jnp.concatenate([gains, d_out])[None]], [0], 0)
    for bit in range(pre):
        little.step(bit)

    def chain(*parts):
        return Chain([jnp.concatenate(parts)[None]], [0], pre)

    cut = 3 * GROUP + 2 * GROUP // 3
    sq = chain(enc_piece[: 2 * GROUP])
    wide = chain(enc_piece[2 * GROUP : cut], enc_piece[4 * GROUP : 5 * GROUP], enc_piece[cut : 4 * GROUP])

    windows = jnp.einsum(
        "adtb,bh->hadt", window_onehots(), rel_table, precision=lax.Precision.HIGHEST
    ).reshape(HEADS, 6, 2 * TILE)
    x = lax.dynamic_index_in_dim(enc_in, core, 0, False)
    seg = lax.dynamic_index_in_dim(segment, core, 0, False)
    segr, segc = seg[None, :], seg[:, None]

    sq.step(Z1), little.step(X + pre)
    phase(sq, little)
    sq.step(Z0), little.step(Y + pre)
    phase(sq, wide, little)
    sa, sb = sq.split(GROUP)
    sa.step(X), sb.step(Y), wide.step(Z1), little.step(Z0 + pre)
    phase(sa, sb, wide, little)
    sa.step(Y), sb.step(X), wide.step(Z0), little.step(Z1 + pre)
    sa_got, sb_got = [across(sa.parts[0])], [across(sb.parts[0])]
    x = phase(sa, sb, wide, little, x)
    wa, wb = wide.split(cut - 2 * GROUP)
    wa.step(X), wb.step(Y)
    sa_got += [across(sa.parts[1])]
    sb_got += [across(sb.parts[1])]

    order = np.argsort(np.array(little.ids))
    places = jnp.take(jnp.asarray(order, jnp.int32), jnp.bitwise_xor(jnp.arange(chips), chip))
    little = jnp.concatenate(little.parts)
    gains = jnp.sum(little[:, :8].astype(F32), axis=0)
    gains_got = across(gains)
    gains0, gains1 = jnp.where(first, gains, gains_got), jnp.where(first, gains_got, gains)
    gains1 = jnp.where(jnp.arange(8)[:, None] == 2, gains0 + gains1, gains1)

    n1, q, k, v, c, h1, n2, lse = enc_attention(meta, x, gains0, segr, segc, windows, sa.sets(sa_got), sb.sets(sb_got))
    h1, little = phase(wa, wb, h1, little)
    wa.step(Y), wb.step(X)
    wa_got, wb_got = [across(wa.parts[0])], [across(wb.parts[0])]

    g_all = jnp.take(little[:, 8:], places, axis=0).reshape(8 * chips, D)
    lanes = -(-4 * rows // TILE) * TILE
    gw = jnp.pad(nt(g_all, w_back[0]).astype(BF), ((0, 0), (0, lanes - 4 * rows))).reshape(chips, 8, lanes)
    gw = lax.all_to_all(gw, "dp", 0, 0)
    h1, shared, gw = phase(wa, wb, h1, shared, gw)
    wa_got += [across(wa.parts[1])]
    wb_got += [across(wb.parts[1])]
    count = dec_both.shape[1]
    shared_back = shared[:: 2**pre, count + 2 * self_rows :]
    back_got = across(shared_back)
    wa_got, wb_got, back_got, h1, n1, c, n2, shared = phase(wa_got, wb_got, back_got, h1, n1, c, n2, shared)
    shared_got, n1_got, c_got, n2_got = across(shared), across(n1), across(c), across(n2)
    w_in_from = in_sources(wa.sets(wa_got), wb.sets(wb_got))
    w_back_from = back_sources(wb.sets(wb_got), shared_back if pre else shared, 0 if pre else count + 2 * self_rows, back_got)
    f, slope, e = enc_ffn(meta, h1, n2, w_in_from, w_back_from)
    e, shared_got, n1_got, c_got, n2_got = phase(e, shared_got, n1_got, c_got, n2_got)
    self_own, self_got = [
        jnp.concatenate([v[:, count + i * self_rows : count + (i + 1) * self_rows].reshape(D // 2, D) for i in range(2)], axis=1)
        for v in (shared, shared_got)
    ]
    dec_sets = [(by_group(v[:, :count], pre) if pre else v, None, other) for other, v in enumerate((shared, shared_got))]
    gw = gw[:, :, : 4 * rows].transpose(1, 0, 2).reshape(8, FF)
    gw_got = across(gw)
    gw = jnp.where(first, gw_got, gw)
    m1, sv, z1, m2, qc, qk, gm = dec_before(meta, dec_in, d_out, gains1, self_own, self_got, dec_sets)
    f, qk = phase(f, qk)
    f_got = across(f)
    de, cc, z2, m3, fc, duc, da2, dz2, dcc, edt, ebar, dg_ffn1, de_other, pairs_other = dec_core(
        meta, e, segr, qk, qc, z1, gm, gw, gains1, dec_sets
    )

    def two(parts):
        return Sum(parts[0], parts[1], pre), Sum(parts[2], parts[3], pre)

    de_got, pairs_got = across(de_other), across(pairs_other)
    du, du_other = enc_hidden_grad(meta, de, slope, w_back_from)
    de_got, pairs_got, du, du_other = phase(de_got, pairs_got, du, du_other)
    du_got = across(du_other)
    back_a, back_b = two(enc_w_back_grad(meta, de, de_got, f, f_got))
    edt = phase(back_a, back_b, edt)
    back_a.step(Y), back_b.step(X)
    dqc, ds1, dsv, dec_grad, dg_attn1, dg_self, k_keep, k_send = dec_after(
        meta, dec_in, z1, dz2, qc, dcc, edt, ebar, pairs_got, gains1, self_own, self_got, dec_sets
    )
    n2, dqc, du_got = phase(n2, dqc, du_got)
    acts = jnp.concatenate([m1, sv, m2, cc, m3, da2, dqc, ds1, dsv, duc, fc], axis=1)
    width = acts.shape[1] // 2
    acts_got = across(lax.dynamic_slice_in_dim(acts, (1 - core) * width, width, 1))
    own = (jnp.arange(8)[:, None] // 4) == core
    acts = jnp.where(own, lax.dynamic_slice_in_dim(acts, core * width, width, 1), acts_got)
    acts = lax.all_gather(acts, "dp").reshape(8 * chips, width)
    in_a, in_b = two(enc_w_in_grad(meta, du, du_got, n2, n2_got, k_keep, k_send))
    h1 = phase(back_a, back_b, in_a, in_b, h1)
    in_a.step(Y), in_b.step(X), back_a.step(X), back_b.step(Y)
    dh1, da, dg_ffn0 = enc_ffn_back(meta, du, h1, de, gains0, w_in_from)
    dq, dk, dv, diag, other = enc_attention_back(meta, da, q, k, v, lse, segr, segc, windows, sb.sets(sb_got))
    dq, other = phase(back_a, back_b, in_a, in_b, dq, other)
    got = across(other)
    in_a.step(X), in_b.step(Y)
    backs = merged([back_a, back_b])
    backs.step(Z0)
    keep, send, dg_attn0 = enc_input_grad(meta, dq, dk, dv, x, dh1, gains0, sa.sets(sa_got), sb.sets(sb_got))
    got, dq, dg_attn0, acts = phase(got, dq, dg_attn0, acts)
    theirs = across(acts)
    square_a, square_b = two(enc_square_grads(meta, n1, n1_got, c, c_got, dq, dk, dv, da, got))
    table = jnp.einsum("hdt,dtb->bh", diag, diagonal_onehots(), precision=lax.Precision.HIGHEST)
    little = jnp.concatenate([
        dg_attn0, dg_ffn0, dg_attn1, dg_ffn1, dg_self,
        jnp.pad(table.reshape(1, -1), ((0, 0), (0, D - BUCKETS * HEADS))), jnp.zeros((2, D), F32),
    ])
    little = little + across(little)
    for bit in range(pre):
        little = little + along(little, bit)
    theirs, send, z2, little = phase(square_a, square_b, in_a, in_b, backs, theirs, send, z2, little)
    square_a.step(Y), square_b.step(X)
    ins = merged([in_a, in_b])
    ins.step(Z0), backs.step(Z1)

    dec_q, dec_o, dec_i, dec_b, g_self_value, g_self_out, y = dec_weight_grads(
        jnp.stack([chip, core]), acts, theirs, g_all, w_back[0], rows, self_rows
    )
    z2 = z2 + across(z2)
    other = along(little, X + pre)
    y, other = phase(square_a, square_b, ins, y, other)
    little = little + other
    square_a.step(X), square_b.step(Y), ins.step(Z1)
    other = along(little, Y + pre)
    y = lax.all_to_all(y.reshape(chips, 8, D), "dp", 0, 0)
    other = phase(square_a, square_b, other)
    little = little + other
    squares = merged([square_a, square_b])
    squares.step(Z0)
    other = along(little, Z0 + pre)
    y, other = phase(squares, ins, backs, y, other)
    little = little + other
    squares.step(Z1)
    little = little + along(little, Z1 + pre)
    backs_sum, ins_sum, square_sum = backs.total(), ins.total(), squares.total()
    dec_out = (z2 + jnp.sum(y.astype(F32), axis=0)).astype(BF)
    dec_out = jnp.where(first, across(dec_out), dec_out)
    mine = chip * rows

    g_rel_table = little[5, : BUCKETS * HEADS].reshape(BUCKETS, HEADS)

    def cut(index, at, count):
        return lax.dynamic_slice_in_dim(little[index], at, count, 0)

    g_attn_gain = cut(jnp.where(first, 0, 2), mine, rows)[None]
    g_ffn_gain = cut(jnp.where(first, 1, 3), mine, rows)[None]
    g_self_gain = cut(4, at_self, self_rows)

    backs_got, ins_got, square_got = [across(v.astype(BF)).astype(F32) for v in (backs_sum, ins_sum, square_sum)]

    def group(value, index):
        return value[index * GROUP : (index + 1) * GROUP]

    def placed(enc_value, dec_value):
        return jnp.where(first, narrowed(enc_value, pre, chip), dec_value)[None]

    g_w_query = placed(group(square_sum, 0), dec_q)
    g_w_out = placed(group(square_sum, 1), dec_o)
    g_w_key = narrowed(jnp.where(first, group(square_got, 0), group(ins_got, 1)), pre, chip)[None]
    g_w_value = narrowed(jnp.where(first, group(square_got, 1), group(ins_sum, 1)), pre, chip)[None]
    g_w_in = placed(
        jnp.concatenate([group(ins_sum, 0), group(ins_sum, 2), group(ins_got, 0), group(ins_got, 2)], axis=1), dec_i
    )
    half = D // 2
    tall = [
        jnp.concatenate([group(v, i)[:, j * half : (j + 1) * half] for i in range(2) for j in range(2)])
        for v in (backs_sum, backs_got)
    ]
    g_w_back = placed(jnp.concatenate(tall, axis=1), dec_b)

    other_half = across(send)
    enc_in_grad = jnp.where(first, jnp.stack([keep, other_half]), jnp.stack([other_half, keep]))
    dec_grad = dec_grad + across(dec_grad)
    half = D // 2
    dec_out = jnp.where(first, dec_out[:, :half], dec_out[:, half:])
    dec_in_grad = jnp.where(first, dec_grad[:, :half], dec_grad[:, half:])
    return (
        dec_out, enc_in_grad, dec_in_grad, g_attn_gain, g_w_query, g_w_key, g_w_value, g_w_out, g_ffn_gain,
        g_w_in, g_w_back, g_self_gain, g_self_value, g_self_out, g_rel_table,
    )


def solution(mesh):
    return jax.shard_map(
        per_device,
        mesh=mesh,
        in_specs=(
            P("dp", None, None),
            P("dp", None),
            P("dp", None),
            P("dp", None),
            P("section", "dp"),
            P("section", "dp", None),
            P("section", "dp", None),
            P("section", "dp", None),
            P("section", "dp", None),
            P("section", "dp"),
            P("section", "dp", None),
            P("section", "dp", None),
            P(("section", "dp")),
            P(("section", "dp"), None),
            P(("section", "dp"), None),
            P(),
        ),
        out_specs=(
            P("dp", "section"),
            P("dp", None, "section"),
            P("dp", "section"),
            P("section", "dp"),
            P("section", "dp", None),
            P("section", "dp", None),
            P("section", "dp", None),
            P("section", "dp", None),
            P("section", "dp"),
            P("section", "dp", None),
            P("section", "dp", None),
            P(("section", "dp")),
            P(("section", "dp"), None),
            P(("section", "dp"), None),
            P(),
        ),
        check_vma=False,
    )
```

```python
import functools

import jax
import jax.numpy as jnp
import numpy as np
from jax import lax
from jax.experimental import pallas as pl
from jax.experimental.pallas import tpu as pltpu
from jax.sharding import PartitionSpec as P

D = 768
HEADS = 12
HEAD_DIM = 64
FF = 3072
BUCKETS = 32
MAX_DIST = 128
ROW_LEN = 512
SEGS = 4
GROUP = 48
GROUPS = D // GROUP
X, Y, Z0, Z1 = 0, 1, 2, 3
TILE = 128
EPS = 1e-06
MASKED = -1000000000.0
BF = jnp.bfloat16
F32 = jnp.float32
SPEED = 0.25
VMEM_LIMIT = 58 * 1024 * 1024


def bucket_of(offset):
    half, exact = BUCKETS // 2, BUCKETS // 4
    exponent, growth = half - exact, MAX_DIST // exact
    distance = abs(offset)
    if distance < exact:
        level = distance
    else:
        k = 0
        while k < exponent and exact**exponent * growth ** (k + 1) <= distance**exponent:
            k += 1
        level = min(exact + k, half - 1)
    return (half if offset > 0 else 0) + level


def window_onehots():
    table = np.zeros((2, 3, 2 * TILE, BUCKETS), np.float32)
    for d in range(3):
        for t in range(2 * TILE):
            table[0, d, t, bucket_of(TILE * (d - 1) - TILE + t)] = 1.0
            table[1, d, t, bucket_of(TILE * (d - 1) + TILE - t)] = 1.0
    return table


def diagonal_onehots():
    table = np.zeros((5, 2 * TILE, BUCKETS), np.float32)
    table[1:4] = window_onehots()[1]
    table[0, :, bucket_of(-TILE - 1)] = 1.0
    table[4, :, bucket_of(TILE + 1)] = 1.0
    return table


def across(value):
    return lax.ppermute(value, "section", [(0, 1), (1, 0)])


def along(value, bit):
    count = lax.axis_size("dp")
    return lax.ppermute(value, "dp", [(i, i ^ (1 << bit)) for i in range(count)])


def bit_of(index, bit):
    return lax.rem(lax.div(index, 1 << bit), 2)


def low_bits(rows):
    count = 0
    while rows < GROUP:
        rows *= 2
        count += 1
    return count


def filled(piece, pre, chip, axis):
    for bit in range(pre):
        other = along(piece, bit)
        upper = bit_of(chip, bit) == 1
        first = jnp.where(upper, other, piece)
        second = jnp.where(upper, piece, other)
        piece = jnp.concatenate([first, second], axis=axis)
    return piece


def narrowed(total, pre, chip):
    for bit in reversed(range(pre)):
        length = total.shape[0] // 2
        upper = bit_of(chip, bit)
        kept = lax.dynamic_slice_in_dim(total, upper * length, length, 0)
        sent = lax.dynamic_slice_in_dim(total, (1 - upper) * length, length, 0)
        total = added(kept, along(sent.astype(BF), bit), F32)
    return total


def phase(*things):
    tree = [thing.arrays() if isinstance(thing, (Chain, Sum)) else thing for thing in things]
    out = []
    for thing, value in zip(things, lax.optimization_barrier(tree)):
        if isinstance(thing, (Chain, Sum)):
            thing.replace(value)
        else:
            out.append(value)
    return out[0] if len(out) == 1 else out


class Chain:
    def __init__(self, parts, ids, pre):
        self.parts, self.ids, self.pre = parts, ids, pre

    def arrays(self):
        return list(self.parts)

    def replace(self, values):
        self.parts = values

    def split(self, at):
        cut = [[part[:, :at] for part in self.parts], [part[:, at:] for part in self.parts]]
        return [Chain(parts, self.ids, self.pre) for parts in cut]

    def step(self, bit):
        held = self.parts[0] if len(self.parts) == 1 else jnp.concatenate(self.parts, axis=0)
        self.parts = [held, along(held, bit + self.pre)]
        self.old_ids = self.ids
        self.ids = self.ids + [g ^ (1 << bit) for g in self.ids]

    def sets(self, others):
        first, last = self.old_ids, self.ids[len(self.old_ids) :]
        return [(self.parts[0], first, 0), (self.parts[1], last, 0), (others[0], first, 1), (others[1], last, 1)]


def added(left, right, kind=BF):
    return (left.astype(F32) + right.astype(F32)).astype(kind)


class Sum:
    def __init__(self, keep, send, pre):
        self.mine, self.other, self.pre, self.fresh = keep, send, pre, True

    def arrays(self):
        return [self.mine, self.other]

    def replace(self, values):
        self.mine, self.other = values

    def step(self, bit):
        if self.fresh:
            send, self.fresh = self.other, False
        else:
            half = self.mine.shape[0] // 2
            send = added(self.mine[half:], self.other[half:])
            self.mine = added(self.mine[:half], self.other[:half])
        self.other = along(send, bit + self.pre)

    def total(self):
        return added(self.mine[0], self.other[0], F32)


def merged(sums):
    one = Sum(
        jnp.concatenate([part.mine for part in sums], axis=1),
        jnp.concatenate([part.other for part in sums], axis=1),
        sums[0].pre,
    )
    one.fresh = False
    return one


def nn(a, b):
    return lax.dot_general(a, b, (((1,), (0,)), ((), ())), preferred_element_type=F32)


def nt(a, b):
    return lax.dot_general(a, b, (((1,), (1,)), ((), ())), preferred_element_type=F32)


def tn(a, b):
    return lax.dot_general(a, b, (((0,), (0,)), ((), ())), preferred_element_type=F32)


def rms(v, gain):
    return v * lax.rsqrt(jnp.mean(v * v, axis=-1, keepdims=True) + EPS) * gain


def rms_back(v, gain, dy):
    r = lax.rsqrt(jnp.mean(v * v, axis=-1, keepdims=True) + EPS)
    dgain = jnp.sum(dy * v * r, axis=0, keepdims=True)
    dyg = dy * gain
    dv = r * dyg - v * (r * r * r) * jnp.mean(v * dyg, axis=-1, keepdims=True)
    return dv, dgain


def gelu_both(u):
    c = 0.7978845608028654
    t = jnp.tanh(c * (u + 0.044715 * u * u * u))
    value = 0.5 * u * (1.0 + t)
    slope = 0.5 * (1.0 + t) + (0.5 * c) * u * (1.0 - t * t) * (1.0 + 3 * 0.044715 * u * u)
    return value, slope


def square_row(b):
    return lambda core, g: (core * 2 + b) * D + GROUP * g


def back_row(b):
    return lambda core, g: 4 * GROUP * g + GROUP * (2 * core + b)


def in_items(first):
    return [(first + GROUP * b, GROUP, square_row(b), lambda core, g, b=b: 2 * core + b) for b in range(2)]


def in_sources(a_sets, b_sets):
    cut = 2 * GROUP // 3
    later = lambda core, g: square_row(1)(core, g) + cut
    block = lambda core, g: 2 * core + 1
    return [
        (a_sets, [(0, GROUP, square_row(0), lambda core, g: 2 * core), (GROUP, cut, square_row(1), block)]),
        (b_sets, [(GROUP, GROUP - cut, later, block)]),
    ]


def back_sources(b_sets, shared, first, got):
    quarter = lambda core, g: g // 4
    return [
        (b_sets, [(0, GROUP, back_row(0), quarter)]),
        ([(shared, None, 0)], [(first, GROUP, back_row(1), quarter)]),
        ([(got, None, 1)], [(0, GROUP, back_row(1), quarter)]),
    ]


def arrays_of(sources):
    return [part for sets, items in sources for part, ids, other in sets]


def start_sources(meta, refs, sources, dst, sems):
    at = 0
    for sets, items in sources:
        plan = [(ids, other) for part, ids, other in sets]
        start_fetch(meta, refs[at : at + len(plan)], plan, items, dst, sems)
        at += len(plan)


def start_fetch(meta, refs, plan, items, dst, sem, only=None):
    if only is not None:
        for other in range(2):
            part = [(ref, entry) for ref, entry in zip(refs, plan) if entry[1] == other]

            @pl.when(jnp.bitwise_xor(meta[1], other) == only)
            def _():
                start_fetch(meta, [r for r, e in part], [e for r, e in part], items, dst, sem)

        return
    me, core = meta[0], meta[1]
    for first, count, row_of, *sem_of in items:
        for ref, (ids, other) in zip(refs, plan):
            source = 1 - core if other else core
            for slot in range(ref.shape[0]):
                group = jnp.int32(slot) if ids is None else jnp.bitwise_xor(me, ids[slot])
                off = pl.multiple_of(row_of(source, group), 16)
                at = sem.at[sem_of[0](source, group)] if sem_of else sem
                pltpu.make_async_copy(ref.at[slot, pl.ds(first, count)], dst.at[pl.ds(off, count)], at).start()


def drain(ref, sem):
    pltpu.make_async_copy(ref, ref, sem).wait()


def slot_of(meta, group, b):
    rel = jnp.bitwise_xor(meta[0], group)
    x, y, z0, z1 = [jnp.bitwise_and(rel // (1 << bit), 1) for bit in range(4)]
    return (8 * y + 4 * x if b == 0 else 8 * x + 4 * y) + 2 * z0 + z1


def start_store(meta, src, group, b, keep, send, sem, rows=slice(None), cols=slice(None)):
    slot = slot_of(meta, group, b)
    at = (rows, cols)

    @pl.when(slot < GROUPS // 2)
    def _():
        pltpu.make_async_copy(src, keep.at[(slot,) + at], sem).start()

    @pl.when(slot >= GROUPS // 2)
    def _():
        pltpu.make_async_copy(src, send.at[(slot - GROUPS // 2,) + at], sem).start()


def head_lanes(h):
    lane = lax.broadcasted_iota(jnp.int32, (1, D), 1)
    return (lane >= h * HEAD_DIM) & (lane < (h + 1) * HEAD_DIM)


def pair_lanes(hh):
    lane = lax.broadcasted_iota(jnp.int32, (1, TILE), 1)
    return (lane < HEAD_DIM) if hh == 0 else (lane >= HEAD_DIM)


def masked(value, lanes):
    return jnp.where(lanes, value, jnp.zeros_like(value))


def fill_bias(window_ref, tiles, transposed):
    part = 1 if transposed else 0

    def one(h, carry):
        for d in range(3):
            row = jnp.broadcast_to(window_ref[h, pl.ds(part * 3 + d, 1), :], (TILE, 2 * TILE))
            rolled = pltpu.roll(row, TILE, 1, stride=1, stride_axis=0)
            tiles[h, d + 1] = rolled[:, :TILE]
        low = window_ref[h, pl.ds(0, 1), pl.ds(0, 1)]
        high = window_ref[h, pl.ds(2, 1), pl.ds(2 * TILE - 1, 1)]
        tiles[h, 0] = jnp.broadcast_to(low, (TILE, TILE))
        tiles[h, 4] = jnp.broadcast_to(high, (TILE, TILE))
        return carry

    lax.fori_loop(0, HEADS, one, 0)


def spec(space):
    return space if isinstance(space, pl.BlockSpec) else pl.BlockSpec(memory_space=space)


def call(body, name, ins, spaces, outs, out_spaces, scratch, us, aliases={}, grid=()):
    if grid:
        specs = {
            "grid_spec": pltpu.PrefetchScalarGridSpec(
                num_scalar_prefetch=1,
                grid=grid,
                in_specs=[spec(s) for s in spaces[1:]],
                out_specs=[spec(s) for s in out_spaces],
                scratch_shapes=scratch,
            )
        }
    else:
        specs = {
            "in_specs": [spec(s) for s in spaces],
            "out_specs": [spec(s) for s in out_spaces],
            "scratch_shapes": scratch,
        }
    return pl.pallas_call(
        body,
        name=name,
        out_shape=[jax.ShapeDtypeStruct(s, k) for s, k in outs],
        input_output_aliases=aliases,
        compiler_params=pltpu.CompilerParams(vmem_limit_bytes=VMEM_LIMIT),
        cost_estimate=pl.CostEstimate(flops=int(us * SPEED * 1.1e9), bytes_accessed=int(us * SPEED * 1e6), transcendentals=0),
        **specs,
    )(*ins)


VM, SM, ANY = pltpu.VMEM, pltpu.SMEM, pl.ANY


def plan_of(sets):
    return [part for part, ids, other in sets], [(ids, other) for part, ids, other in sets]


def enc_attention(meta, x, gains, segr, segc, windows, a_sets, b_sets):
    a_arrays, a_plan = plan_of(a_sets)
    b_arrays, b_plan = plan_of(b_sets)
    n = len(a_arrays)

    def body(meta, x, gains, segr, segc, windows, *rest):
        a_parts, b_parts, rest = rest[:n], rest[n : 2 * n], rest[2 * n :]
        n1, q, k, v, c, h1, n2, lse, w, tiles, lcol, sems = rest
        start_fetch(meta, a_parts, a_plan, [(0, GROUP, square_row(0))], w, sems.at[0])
        start_fetch(meta, b_parts, b_plan, [(0, GROUP, square_row(1))], w, sems.at[0])
        fill_bias(windows, tiles, False)
        xf = x[...].astype(F32)
        n1[...] = rms(xf, gains[0:1, :]).astype(BF)
        drain(w, sems.at[0])
        for ref, at in ((q, 0), (k, 2), (v, 3)):
            ref[...] = nn(n1[...], w[at * D : (at + 1) * D, :]).astype(BF)
        lane = lax.broadcasted_iota(jnp.int32, (1, TILE), 1)
        lcol[...] = jnp.zeros_like(lcol)

        def pair(pr, carry):
            cols = pl.ds(pl.multiple_of(pr * TILE, TILE), TILE)
            kp, vp = k[:, cols], v[:, cols]
            for ib in range(ROW_LEN // TILE):
                rows = slice(ib * TILE, (ib + 1) * TILE)
                same = segc[rows, :] == segr[...]
                qp = q[rows, cols]
                total = jnp.zeros((TILE, TILE), F32)
                for hh in range(2):
                    h = 2 * pr + hh
                    lanes = pair_lanes(hh)
                    bias = jnp.concatenate(
                        [tiles[h, min(max(jb - ib, -2), 2) + 2] for jb in range(ROW_LEN // TILE)], axis=1
                    )
                    s = jnp.where(same, nt(masked(qp, lanes), kp) + bias, MASKED)
                    top = jnp.max(s, axis=-1, keepdims=True)
                    ex = jnp.exp(s - top)
                    tot = jnp.sum(ex, axis=-1, keepdims=True)
                    p = (ex * (1.0 / tot)).astype(BF)
                    total = total + nn(p, masked(vp, lanes))
                    lcol[rows, :] = jnp.where(lane == h, top + jnp.log(tot), lcol[rows, :])
                c[rows, cols] = total.astype(BF)
            return carry

        lax.fori_loop(0, HEADS // 2, pair, 0)
        lse[...] = lcol[...].T
        res = x[...].astype(F32) + nn(c[...], w[D : 2 * D, :])
        h1[...] = res
        n2[...] = rms(res, gains[1:2, :]).astype(BF)

    rows = (ROW_LEN, D)
    return call(
        body, "enc_attention", [meta, x, gains, segr, segc, windows, *a_arrays, *b_arrays],
        [SM, VM, VM, VM, VM, VM] + [ANY] * (2 * n),
        [(rows, BF)] * 5 + [(rows, F32), (rows, BF), ((TILE, ROW_LEN), F32), ], [VM] * 8,
        [pltpu.VMEM((4 * D, D), BF), pltpu.VMEM((HEADS, 5, TILE, TILE), F32), pltpu.VMEM((ROW_LEN, TILE), F32), pltpu.SemaphoreType.DMA((2,))],
        us=20,
    )


PART = (GROUPS // 2, GROUP, D)
WIDE_PART = (GROUPS // 2, 2 * GROUP, D)
BLOCKS = FF // D


def enc_ffn(meta, h1, n2, w_in_from, w_back_from):
    in_arrays, back_arrays = arrays_of(w_in_from), arrays_of(w_back_from)
    n, m = len(in_arrays), len(back_arrays)

    def body(meta, h1, n2, *rest):
        ins, backs, rest = rest[:n], rest[n : n + m], rest[n + m :]
        f, slope, e, w_in, w_back, acc, sems = rest
        start_sources(meta, ins, w_in_from, w_in, sems)
        start_sources(meta, backs, w_back_from, w_back, sems.at[pl.ds(4, 4)])
        acc[...] = h1[...]

        def block(b, carry):
            rows = pl.ds(pl.multiple_of(b * D, D), D)

            drain(w_in.at[rows], sems.at[b])
            value, grad = gelu_both(nn(n2[...], w_in[rows, :]))
            fb = value.astype(BF)
            f[:, rows] = fb
            slope[:, rows] = grad.astype(BF)
            drain(w_back.at[rows], sems.at[4 + b])
            acc[...] += nn(fb, w_back[rows, :])
            return carry

        lax.fori_loop(0, FF // D, block, 0)
        e[...] = acc[...].astype(BF)

    return call(
        body, "enc_ffn", [meta, h1, n2, *in_arrays, *back_arrays], [SM, VM, VM] + [ANY] * (n + m),
        [((ROW_LEN, FF), BF), ((ROW_LEN, FF), BF), ((ROW_LEN, D), BF)], [VM] * 3,
        [pltpu.VMEM((FF, D), BF), pltpu.VMEM((FF, D), BF), pltpu.VMEM((ROW_LEN, D), F32),
         pltpu.SemaphoreType.DMA((8,))],
        us=15,
    )


def enc_hidden_grad(meta, de, slope, w_back_from):
    arrays = arrays_of(w_back_from)
    n = len(arrays)

    def body(meta, de, slope, *rest):
        parts, rest = rest[:n], rest[n:]
        du, other, w, sems = rest
        b = pl.program_id(0)

        @pl.when(b == 0)
        def _():
            start_sources(meta, parts, w_back_from, w, sems)

        rows = pl.ds(pl.multiple_of(b * D, D), D)
        drain(w.at[rows], sems.at[b])
        value = (slope[...].astype(F32) * nt(de[...], w[rows, :])).astype(BF)
        du[...] = value

        @pl.when(meta[1] != b // 2)
        def _():
            other[:, pl.ds(pl.multiple_of(b % 2 * D, D), D)] = value

    block = pl.BlockSpec((ROW_LEN, D), lambda b, meta: (0, b))
    return call(
        body, "enc_hidden_grad", [meta, de, slope, *arrays], [SM, VM, block] + [ANY] * n,
        [((ROW_LEN, FF), BF), ((ROW_LEN, FF // 2), BF)], [block, VM],
        [pltpu.VMEM((FF, D), BF), pltpu.SemaphoreType.DMA((4,))],
        us=8, grid=(BLOCKS,),
    )


def enc_w_back_grad(meta, de, de_got, f, f_got):
    half = D // 2

    def body(meta, de, de_got, f, f_got, keep_a, send_a, keep_b, send_b, mine, buf, sems):
        mine[...] = de[:, pl.ds(pl.multiple_of(meta[1] * half, TILE), half)]
        for b in range(FF // D):
            cols = slice(b * D, (b + 1) * D)
            at = b % 2
            if b >= 2:
                drain(buf.at[at], sems.at[at])
            buf[at] = (tn(f[:, cols], mine[...]) + tn(f_got[:, cols], de_got[...])).astype(BF)
            for k in range(D // GROUP):
                group, piece = b * (D // GROUP // 4) + k // 4, k % 4
                keep, send = (keep_a, send_a) if piece < 2 else (keep_b, send_b)
                start_store(meta, buf.at[at, pl.ds(k * GROUP, GROUP)], group, piece // 2, keep, send, sems.at[at],
                            cols=pl.ds((piece % 2) * half, half))
        drain(buf.at[0], sems.at[0])
        drain(buf.at[1], sems.at[1])

    return call(
        body, "enc_w_back_grad", [meta, de, de_got, f, f_got], [SM] + [VM] * 4,
        [(PART, BF)] * 4, [ANY] * 4,
        [pltpu.VMEM((ROW_LEN, half), BF), pltpu.VMEM((2, D, half), BF), pltpu.SemaphoreType.DMA((2,))],
        us=7,
    )


def enc_w_in_grad(meta, du, du_got, n2, n2_got, wide_keep, wide_send):
    def body(meta, du, du_got, n2, n2_got, wide_keep, wide_send, keep_a, send_a, keep_b, send_b, buf, sems):
        for b in range(2):
            cols = pl.ds(pl.multiple_of(meta[1] * (FF // 2) + b * D, TILE), D)
            buf[b] = (tn(n2[...], du[:, cols]) + tn(n2_got[...], du_got[:, b * D : (b + 1) * D])).astype(BF)
            keep, send = (keep_a, send_a) if b == 0 else (keep_b, send_b)
            for g in range(GROUPS):
                rows = pl.ds(0, GROUP)
                start_store(meta, buf.at[b, pl.ds(g * GROUP, GROUP)], g, b, keep, send, sems.at[b], rows)
        drain(buf.at[0], sems.at[0])
        drain(buf.at[1], sems.at[1])

    return call(
        body, "enc_w_in_grad", [meta, du, du_got, n2, n2_got, wide_keep, wide_send], [SM] + [VM] * 4 + [ANY] * 2,
        [(WIDE_PART, BF), (WIDE_PART, BF), (PART, BF), (PART, BF)], [ANY] * 4,
        [pltpu.VMEM((2, D, D), BF), pltpu.SemaphoreType.DMA((2,))],
        us=7, aliases={5: 0, 6: 1},
    )


def enc_ffn_back(meta, du, h1, de, gains, w_in_from):
    arrays = arrays_of(w_in_from)
    n = len(arrays)

    def body(meta, du, h1, de, gains, *rest):
        parts, rest = rest[:n], rest[n:]
        dh1, da, dgain, w, acc, sems = rest
        start_sources(meta, parts, w_in_from, w, sems)
        for k, b in enumerate((0, 2, 1, 3)):
            cols = slice(b * D, (b + 1) * D)
            drain(w.at[cols], sems.at[b])
            part = nt(du[:, cols], w[cols, :])
            acc[...] = part if k == 0 else acc[...] + part
        dv, dg = rms_back(h1[...], gains[1:2, :], acc[...])
        total = de[...].astype(F32) + dv
        dh1[...] = total
        da[...] = total.astype(BF)
        dgain[...] = dg

    rows = (ROW_LEN, D)
    return call(
        body, "enc_ffn_back", [meta, du, h1, de, gains, *arrays], [SM, VM, VM, VM, VM] + [ANY] * n,
        [(rows, F32), (rows, BF), ((1, D), F32)], [VM, VM, VM],
        [pltpu.VMEM((FF, D), BF), pltpu.VMEM(rows, F32), pltpu.SemaphoreType.DMA((4,))],
        us=8,
    )


def enc_attention_back(meta, da, q, k, v, lse, segr, segc, windows, sets):
    arrays, plan = plan_of(sets)
    n = len(arrays)
    wide = 2 * TILE

    def body(meta, da, q, k, v, lse, segr, segc, windows, *rest):
        parts, rest = rest[:n], rest[n:]
        dq, dk, dv, diag, other, w, dc, tiles, sums, kacc, vacc, sem = rest
        start_fetch(meta, parts, plan, [(0, GROUP, lambda core, g: GROUP * g)], w, sem, only=0)
        fill_bias(windows, tiles, True)
        drain(w, sem)
        dc[...] = nt(da[...], w[...]).astype(BF)
        row = lax.broadcasted_iota(jnp.int32, (TILE, TILE), 0)
        col = lax.broadcasted_iota(jnp.int32, (TILE, TILE), 1)
        flip = (row + col == TILE - 1).astype(F32)

        def pair(pr, carry):
            cols = pl.ds(pl.multiple_of(pr * TILE, TILE), TILE)
            for hh in range(2):
                h = 2 * pr + hh
                lanes = pair_lanes(hh)
                km, vm = masked(k[:, cols], lanes), masked(v[:, cols], lanes)
                sums[...] = jnp.zeros_like(sums)
                for ib in range(ROW_LEN // wide):
                    rows = slice(ib * wide, (ib + 1) * wide)
                    same = segc[...] == segr[:, rows]
                    qp, dcp = q[rows, cols], dc[rows, cols]
                    bias = jnp.concatenate([
                        jnp.concatenate([
                            tiles[h, min(max(jb - (2 * ib + i), -2), 2) + 2] for i in range(2)
                        ], axis=1) for jb in range(ROW_LEN // TILE)
                    ], axis=0)
                    s = jnp.where(same, nt(km, qp) + bias, MASKED)
                    prob = jnp.exp(s - lse[pl.ds(h, 1), rows])
                    dprob = nt(vm, dcp)
                    inner = jnp.sum(prob * dprob, axis=0, keepdims=True)
                    ds = (prob * (dprob - inner)).astype(BF)
                    dvp = nn(prob.astype(BF), masked(dcp, lanes))
                    dkp = nn(ds, masked(qp, lanes))
                    dqp = tn(ds, km)
                    if hh == 0 and ib == 0:
                        vacc[...], kacc[...] = dvp, dkp
                    else:
                        vacc[...] += dvp
                        kacc[...] += dkp
                    if hh == 0:
                        dq[rows, cols] = dqp.astype(BF)
                    else:
                        dq[rows, cols] = dq[rows, cols] + dqp.astype(BF)
                    for jb in range(ROW_LEN // TILE):
                        for i in range(2):
                            d = min(max(jb - (2 * ib + i), -2), 2) + 2
                            sums[d] += ds[jb * TILE : (jb + 1) * TILE, i * TILE : (i + 1) * TILE].astype(F32)
                for d in range(5):
                    if d in (0, 4):
                        line = jnp.sum(sums[d], axis=0, keepdims=True)
                        diag[h, d : d + 1, :] = jnp.concatenate([line, jnp.zeros_like(line)], axis=1)
                    else:
                        turned = lax.dot_general(
                            flip, sums[d], (((1,), (0,)), ((), ())),
                            precision=lax.Precision.HIGHEST, preferred_element_type=F32,
                        )
                        wider = jnp.concatenate([turned, jnp.zeros_like(turned)], axis=1)
                        rolled = pltpu.roll(wider, 1, 1, stride=1, stride_axis=0)
                        diag[h, d : d + 1, :] = jnp.sum(rolled, axis=0, keepdims=True)
            dk[:, cols] = kacc[...].astype(BF)
            dv[:, cols] = vacc[...].astype(BF)
            return carry

        lax.fori_loop(0, HEADS // 2, pair, 0)

        @pl.when(meta[1] == 0)
        def _():
            other[0] = dk[...]
            other[1] = dv[...]

        @pl.when(meta[1] != 0)
        def _():
            other[0] = dq[...]
            other[1] = da[...]

    rows = (ROW_LEN, D)
    return call(
        body, "enc_attention_back", [meta, da, q, k, v, lse, segr, segc, windows, *arrays],
        [SM] + [VM] * 8 + [ANY] * n,
        [(rows, BF), (rows, BF), (rows, BF), ((HEADS, 5, 2 * TILE), F32), ((2,) + rows, BF)], [VM] * 5,
        [pltpu.VMEM((D, D), BF), pltpu.VMEM(rows, BF), pltpu.VMEM((HEADS, 5, TILE, TILE), F32),
         pltpu.VMEM((5, TILE, TILE), F32), pltpu.VMEM((ROW_LEN, TILE), F32), pltpu.VMEM((ROW_LEN, TILE), F32),
         pltpu.SemaphoreType.DMA],
        us=25,
    )


def enc_square_grads(meta, n1, n1_got, c, c_got, dq, dk, dv, da, got):
    def body(meta, n1, n1_got, c, c_got, dq, dk, dv, da, got, keep_a, send_a, keep_b, send_b, buf, sems):
        for core, (one, left, left_got, two) in enumerate(((dq, c, c_got, da), (dk, n1, n1_got, dv))):

            @pl.when(meta[1] == core)
            def _():
                buf[0] = (tn(n1[...], one[...]) + tn(n1_got[...], got[0])).astype(BF)
                for g in range(GROUPS):
                    start_store(meta, buf.at[0, pl.ds(g * GROUP, GROUP)], g, 0, keep_a, send_a, sems.at[0])
                buf[1] = (tn(left[...], two[...]) + tn(left_got[...], got[1])).astype(BF)
                for g in range(GROUPS):
                    start_store(meta, buf.at[1, pl.ds(g * GROUP, GROUP)], g, 1, keep_b, send_b, sems.at[1])

        drain(buf.at[0], sems.at[0])
        drain(buf.at[1], sems.at[1])

    return call(
        body, "enc_square_grads", [meta, n1, n1_got, c, c_got, dq, dk, dv, da, got], [SM] + [VM] * 9,
        [(PART, BF)] * 4, [ANY] * 4,
        [pltpu.VMEM((2, D, D), BF), pltpu.SemaphoreType.DMA((2,))],
        us=1,
    )


def enc_input_grad(meta, dq, dk, dv, x, dh1, gains, a_sets, b_sets):
    a_arrays, a_plan = plan_of(a_sets)
    b_arrays, b_plan = plan_of(b_sets)
    n = len(a_arrays)

    def body(meta, dq, dk, dv, x, dh1, gains, *rest):
        a_parts, b_parts, rest = rest[:n], rest[n : 2 * n], rest[2 * n :]
        keep, send, dgain, w, sem = rest
        start_fetch(meta, a_parts, a_plan, [(0, GROUP, lambda core, g: core * D + GROUP * g)], w, sem)
        start_fetch(meta, b_parts, b_plan, [(0, GROUP, lambda core, g: 2 * D + GROUP * g)], w, sem, only=1)
        drain(w, sem)
        total = nt(dq[...], w[0:D, :]) + nt(dk[...], w[D : 2 * D, :]) + nt(dv[...], w[2 * D :, :])
        dx, dg = rms_back(x[...].astype(F32), gains[0:1, :], total)
        out = (dh1[...] + dx).astype(BF)
        dgain[...] = dg
        half = D // 2

        @pl.when(meta[1] == 0)
        def _():
            keep[...] = out[:, :half]
            send[...] = out[:, half:]

        @pl.when(meta[1] != 0)
        def _():
            keep[...] = out[:, half:]
            send[...] = out[:, :half]

    return call(
        body, "enc_input_grad", [meta, dq, dk, dv, x, dh1, gains, *a_arrays, *b_arrays],
        [SM] + [VM] * 6 + [ANY] * (2 * n),
        [((ROW_LEN, D // 2), BF), ((ROW_LEN, D // 2), BF), ((1, D), F32)], [VM] * 3,
        [pltpu.VMEM((3 * D, D), BF), pltpu.SemaphoreType.DMA],
        us=1,
    )


def spread_heads(value):
    return jnp.concatenate([masked(value, head_lanes(h)) for h in range(HEADS)], axis=0)


def join_heads(value):
    total = jnp.zeros((8, D), F32)
    for h in range(HEADS):
        total = total + masked(value[8 * h : 8 * h + 8, :], head_lanes(h))
    return total


def own_rows(meta):
    row = lax.broadcasted_iota(jnp.int32, (8, 1), 0)
    return (row >= 4 * meta[1]) & (row < 4 * meta[1] + 4)


def start_self(meta, own, got, dst, sem):
    half = D // 2
    pltpu.make_async_copy(own, dst.at[pl.ds(pl.multiple_of(meta[1] * half, 16), half)], sem).start()
    pltpu.make_async_copy(got, dst.at[pl.ds(pl.multiple_of((1 - meta[1]) * half, 16), half)], sem).start()


def dec_before(meta, z, d_out, gains, self_own, self_got, sets):
    arrays, plan = plan_of(sets)
    n = len(arrays)

    def body(meta, z, d_out, gains, self_own, self_got, *rest):
        parts, rest = rest[:n], rest[n:]
        m1, sv, z1, m2, qc, qk, gm, w_self, w, sems = rest
        start_self(meta, self_own, self_got, w_self, sems.at[0])
        start_fetch(meta, parts, plan, [(0, GROUP, lambda core, g: core * D + GROUP * g)], w, sems.at[1])
        zf = z[...].astype(F32)
        gm[...] = jnp.where(own_rows(meta), d_out[...].astype(F32), 0.0).astype(BF)
        m1v = rms(zf, gains[2:3, :]).astype(BF)
        drain(w_self, sems.at[0])
        drain(w, sems.at[1])
        svv = nn(m1v, w_self[:, :D]).astype(BF)
        z1v = zf + nn(svv, w_self[:, D:])
        m2v = rms(z1v, gains[0:1, :]).astype(BF)
        qcv = nn(m2v, w[0:D, :]).astype(BF)
        qk[...] = nt(spread_heads(qcv), w[D:, :]).astype(BF)
        m1[...], sv[...], z1[...], m2[...], qc[...] = m1v, svv, z1v, m2v, qcv

    rows = (8, D)
    return call(
        body, "dec_before", [meta, z, d_out, gains, self_own, self_got, *arrays],
        [SM, VM, VM, VM, ANY, ANY] + [ANY] * n,
        [(rows, BF), (rows, BF), (rows, F32), (rows, BF), (rows, BF), ((8 * HEADS, D), BF), (rows, BF)], [VM] * 7,
        [pltpu.VMEM((D, 2 * D), BF), pltpu.VMEM((2 * D, D), BF), pltpu.SemaphoreType.DMA((2,))],
        us=6,
    )


def dec_core(meta, e, segr, qk, qc, z1, g, gw, gains, sets):
    arrays, plan = plan_of(sets)
    n = len(arrays)

    def body(meta, e, segr, qk, qc, z1, g, gw, gains, *rest):
        parts, rest = rest[:n], rest[n:]
        de, cc, z2, m3, fc, duc, da2, dz2, dcc, edt, ebar, dgain, de_other, pairs_other, w, w_in, sems = rest
        start_fetch(meta, parts, plan, [(GROUP, GROUP, lambda core, g: core * D + GROUP * g)], w, sems.at[0])
        start_fetch(meta, parts, plan, in_items(2 * GROUP), w_in, sems.at[pl.ds(1, 4)])
        pairs = lax.broadcasted_iota(jnp.int32, (8 * HEADS, 1), 0)
        owner = segr[...] == jnp.bitwise_and(pairs, 7) - 4 * meta[1]
        t = jnp.where(owner, nt(qk[...], e[...]), MASKED)
        ex = jnp.where(owner, jnp.exp(t - jnp.max(t, axis=-1, keepdims=True)), 0.0)
        tot = jnp.sum(ex, axis=-1, keepdims=True)
        prob = ex * (1.0 / jnp.where(tot > 0.0, tot, 1.0))
        pc = prob.astype(BF)
        ebv = nn(pc, e[...]).astype(BF)
        ebar[...] = ebv
        drain(w, sems.at[0])
        ccv = join_heads(nn(ebv, w[D:, :])).astype(BF)
        z2v = z1[...] + nn(ccv, w[0:D, :])
        m3v = rms(z2v, gains[1:2, :]).astype(BF)
        dm3 = jnp.zeros((8, D), F32)
        own = own_rows(meta)
        for b in (0, 2, 1, 3):
            cols = slice(b * D, (b + 1) * D)
            drain(w_in.at[cols], sems.at[1 + b])
            value, slope = gelu_both(nn(m3v, w_in[cols, :]))
            fc[:, cols] = jnp.where(own, value, 0.0).astype(BF)
            ducv = jnp.where(own, slope * gw[:, cols].astype(F32), 0.0).astype(BF)
            duc[:, cols] = ducv
            dm3 = dm3 + nt(ducv, w_in[cols, :])
        back, dg = rms_back(z2v, gains[1:2, :], dm3)
        dz2v = g[...].astype(F32) + back
        da2v = dz2v.astype(BF)
        dccv = nt(da2v, w[0:D, :]).astype(BF)
        dvw = nt(spread_heads(dccv), w[D:, :]).astype(BF)
        dprob = nt(dvw, e[...])
        dt = (prob * (dprob - jnp.sum(prob * dprob, axis=-1, keepdims=True))).astype(BF)
        de[...] = tn(jnp.concatenate([pc, dt], axis=0), jnp.concatenate([dvw, qk[...]], axis=0)).astype(BF)
        edt[...] = nn(dt, e[...]).astype(BF)
        cc[...], m3[...], da2[...], dz2[...], dcc[...], dgain[...] = ccv, m3v, da2v, dz2v, dccv, dg
        z2[...] = jnp.where(own, z2v, 0.0)
        half = D // 2
        pairs_other[8 * HEADS + 8 :, :] = jnp.zeros((8, D), BF)

        @pl.when(meta[1] == 0)
        def _():
            de_other[...] = de[:, half:]
            pairs_other[: 8 * HEADS, :] = ebv
            pairs_other[8 * HEADS : 8 * HEADS + 8, :] = dccv

        @pl.when(meta[1] != 0)
        def _():
            de_other[...] = de[:, :half]
            pairs_other[: 8 * HEADS, :] = edt[...]
            pairs_other[8 * HEADS : 8 * HEADS + 8, :] = qc[...]

    rows, spread = (8, D), (8 * HEADS, D)
    return call(
        body, "dec_core", [meta, e, segr, qk, qc, z1, g, gw, gains, *arrays],
        [SM] + [VM] * 8 + [ANY] * n,
        [((ROW_LEN, D), BF), (rows, BF), (rows, F32), (rows, BF), ((8, FF), BF), ((8, FF), BF), (rows, BF),
         (rows, F32), (rows, BF), (spread, BF), (spread, BF), ((1, D), F32),
         ((ROW_LEN, D // 2), BF), ((8 * HEADS + 16, D), BF)], [VM] * 14,
        [pltpu.VMEM((2 * D, D), BF), pltpu.VMEM((FF, D), BF), pltpu.SemaphoreType.DMA((5,))],
        us=10,
    )


def dec_after(meta, z, z1, dz2, qc, dcc, edt, ebar, got, gains, acts, duc, fc, self_own, self_got, sets):
    arrays, plan = plan_of(sets)
    n = len(arrays)

    def body(meta, z, z1, dz2, qc, dcc, edt, ebar, got, gains, *rest):
        acts, rest = rest[:8], rest[8:]
        self_own, self_got, parts, rest = rest[0], rest[1], rest[2 : 2 + n], rest[2 + n :]
        acts_keep, acts_send, dec_grad, dg_attn, dg_self, keep, send, w_self, w, buf, sems = rest
        start_fetch(meta, parts, plan, [(0, GROUP, lambda core, g: core * D + GROUP * g)], w, sems.at[1])
        start_self(meta, self_own, self_got, w_self, sems.at[0])
        zero = meta[1] == 0
        left = jnp.concatenate([jnp.where(zero, edt[...], ebar[...]), got[: 8 * HEADS, :]], axis=0)
        right = jnp.where(zero, qc[...], dcc[...])
        right = jnp.concatenate([spread_heads(right), spread_heads(got[8 * HEADS : 8 * HEADS + 8, :])], axis=0)
        buf[...] = tn(left, right).astype(BF)
        for grp in range(GROUPS):
            start_store(meta, buf.at[pl.ds(grp * GROUP, GROUP)], grp, 0, keep, send, sems.at[3], pl.ds(GROUP, GROUP))
        drain(w, sems.at[1])
        dqv = join_heads(nn(edt[...], w[D:, :])).astype(BF)
        back, dg = rms_back(z1[...], gains[0:1, :], nt(dqv, w[0:D, :]))
        dz1 = dz2[...] + back
        ds1v = dz1.astype(BF)
        drain(w_self, sems.at[0])
        dsvv = nt(ds1v, w_self[:, D:]).astype(BF)
        back0, dg0 = rms_back(z[...].astype(F32), gains[2:3, :], nt(dsvv, w_self[:, :D]))
        own = own_rows(meta)
        dec_grad[...] = jnp.where(own, dz1 + back0, 0.0).astype(BF)
        dg_attn[...], dg_self[...] = dg, dg0
        row = jnp.concatenate([ref[...] for ref in acts[:6]] + [dqv, ds1v, dsvv] + [ref[...] for ref in acts[6:]], axis=1)
        half = row.shape[1] // 2
        for core, (one, two) in enumerate(((acts_keep, acts_send), (acts_send, acts_keep))):

            @pl.when(meta[1] == core)
            def _():
                one[...] = row[:, :half]
                two[...] = row[:, half:]

        drain(buf, sems.at[3])

    rows = (8, D)
    return call(
        body, "dec_after",
        [meta, z, z1, dz2, qc, dcc, edt, ebar, got, gains, *acts, duc, fc, self_own, self_got, *arrays],
        [SM] + [VM] * 17 + [ANY] * (2 + n),
        [((8, (9 * D + 2 * FF) // 2), BF)] * 2 + [(rows, BF)] + [((1, D), F32)] * 2 + [(WIDE_PART, BF)] * 2, [VM] * 5 + [ANY] * 2,
        [pltpu.VMEM((D, 2 * D), BF), pltpu.VMEM((2 * D, D), BF), pltpu.VMEM((D, D), BF),
         pltpu.SemaphoreType.DMA((4,))],
        us=6,
    )


def dec_weight_grads(place, own, got, g_all, w_back, rows, self_rows):
    def body(place, own, got, *rest):
        for core, (left, right) in enumerate(((own, got), (got, own))):
            pl.when(place[1] == core)(functools.partial(halves, place, left, right, *rest))

    def halves(place, left, right, g_all, w_back, dec_q, dec_o, dec_i, dec_b, self_v, self_o, y):
        half = left.shape[1]
        chip, core = place[0], place[1]
        chips = D // rows

        def cut(at, width):
            parts = []
            while width:
                ref, first = (left, at) if at < half else (right, at - half)
                count = min(width, half - first)
                parts.append(ref[:, first : first + count])
                at, width = at + count, width - count
            return parts[0] if len(parts) == 1 else jnp.concatenate(parts, axis=1)

        def picked(at, first, count, width=D):
            row = lax.broadcasted_iota(jnp.int32, (count, width), 0) + first
            col = lax.broadcasted_iota(jnp.int32, (count, width), 1)
            return nt((row == col).astype(F32).astype(BF), cut(at * D, width)).astype(BF)

        first, first_self = chip * rows, (core * chips + chip) * self_rows
        m1, sv, m2, cc, m3, da2, dqc, ds1, dsv, duc, fc = list(range(10)) + [13]
        dec_q[...] = nn(picked(m2, first, rows), cut(dqc * D, D))
        dec_o[...] = nn(picked(cc, first, rows), cut(da2 * D, D))
        dec_i[...] = nn(picked(m3, first, rows), cut(duc * D, FF))
        self_v[...] = nn(picked(m1, first_self, self_rows), cut(dsv * D, D))
        self_o[...] = nn(picked(sv, first_self, self_rows), cut(ds1 * D, D))
        hidden = picked(fc, 4 * first, 4 * rows, FF)
        dec_b[...] = nn(hidden, g_all[...])
        y[...] = tn(hidden, w_back[...]).astype(BF)

    return call(
        body, "dec_weight_grads", [place, own, got, g_all, w_back], [SM, VM, VM, VM, VM],
        [((rows, D), F32), ((rows, D), F32), ((rows, FF), F32), ((4 * rows, D), F32), ((self_rows, D), F32),
         ((self_rows, D), F32), (g_all.shape, BF)], [VM] * 7,
        [], us=5,
    )


def prepare(meta, w_query, w_key, w_value, w_out, w_in, w_back):
    def body(meta, query, key, value, out, w_in, w_back, kept, sent):
        for core, (one, two) in enumerate(((kept, sent), (sent, kept))):

            @pl.when(meta[1] == core)
            def _():
                for half, (dst, squares) in enumerate(((one, (query, out)), (two, (key, value)))):
                    for k in range(2):
                        at = 2 * half + k
                        dst[k * GROUP : (k + 1) * GROUP, :] = squares[k][...]
                        dst[(2 + k) * GROUP : (3 + k) * GROUP, :] = w_in[:, at * D : (at + 1) * D]
                        dst[(4 + k) * GROUP : (5 + k) * GROUP, :] = w_back[at * GROUP : (at + 1) * GROUP, :]

    half = ((6 * GROUP, D), BF)
    return call(
        body, "prepare", [meta, w_query, w_key, w_value, w_out, w_in, w_back], [SM] + [VM] * 6, [half] * 2, [VM] * 2, [], us=2
    )


def per_device(
    enc_in, dec_in, segment, d_out, attn_gain, w_query, w_key, w_value, w_out, ffn_gain, w_in, w_back,
    self_gain, self_value, self_out, rel_table,
):
    core, chip = lax.axis_index("section"), lax.axis_index("dp")
    chips = lax.axis_size("dp")
    rows = w_query.shape[1]
    first = core == 0
    pre = low_bits(rows)
    meta = jnp.stack([chip >> pre, core]).astype(jnp.int32)
    self_rows = self_value.shape[0]
    at_self = (core * chips + chip) * self_rows

    kept, sent = prepare(
        meta, *[filled(w[0], pre, chip, 0) for w in (w_query, w_key, w_value, w_out, w_in, w_back)]
    )
    got = across(sent)
    enc_piece, dec_piece = jnp.where(first, kept, got), jnp.where(first, got, kept)
    count = 4 * GROUP

    shared = lax.all_gather(jnp.concatenate([dec_piece[:count], self_value, self_out, enc_piece[5 * GROUP :]]), "dp")

    gains = jnp.zeros((8, D), BF)
    gains = lax.dynamic_update_slice(gains, jnp.concatenate([attn_gain, ffn_gain]), (0, chip * rows))
    gains = lax.dynamic_update_slice(gains, self_gain[None], (2, at_self))
    little = Chain([jnp.concatenate([gains, d_out])[None]], [0], 0)
    for bit in range(pre):
        little.step(bit)

    def chain(*parts):
        return Chain([jnp.concatenate(parts)[None]], [0], pre)

    cut = 3 * GROUP + 2 * GROUP // 3
    sq = chain(enc_piece[: 2 * GROUP])
    wide = chain(enc_piece[2 * GROUP : cut], enc_piece[4 * GROUP : 5 * GROUP], enc_piece[cut : 4 * GROUP])

    windows = jnp.einsum(
        "adtb,bh->hadt", window_onehots(), rel_table, precision=lax.Precision.HIGHEST
    ).reshape(HEADS, 6, 2 * TILE)
    x = lax.dynamic_index_in_dim(enc_in, core, 0, False)
    seg = lax.dynamic_index_in_dim(segment, core, 0, False)
    segr, segc = seg[None, :], seg[:, None]

    sq.step(Z1), little.step(X + pre)
    phase(sq, little)
    sq.step(Z0), little.step(Y + pre)
    phase(sq, wide, little)
    sa, sb = sq.split(GROUP)
    sa.step(X), sb.step(Y), wide.step(Z1), little.step(Z0 + pre)
    phase(sa, sb, wide, little)
    sa.step(Y), sb.step(X), wide.step(Z0), little.step(Z1 + pre)
    sa_got, sb_got = [across(sa.parts[0])], [across(sb.parts[0])]
    x = phase(sa, sb, wide, little, x)
    wa, wb = wide.split(cut - 2 * GROUP)
    wa.step(X), wb.step(Y)
    sa_got += [across(sa.parts[1])]
    sb_got += [across(sb.parts[1])]

    order = np.argsort(np.array(little.ids))
    places = jnp.take(jnp.asarray(order, jnp.int32), jnp.bitwise_xor(jnp.arange(chips), chip))
    little = jnp.concatenate(little.parts)
    gains = jnp.sum(little[:, :8].astype(F32), axis=0)
    gains_got = across(gains)
    gains0, gains1 = jnp.where(first, gains, gains_got), jnp.where(first, gains_got, gains)
    gains1 = jnp.where(jnp.arange(8)[:, None] == 2, gains0 + gains1, gains1)
    n1, q, k, v, c, h1, n2, lse = enc_attention(meta, x, gains0, segr, segc, windows, sa.sets(sa_got), sb.sets(sb_got))
    h1, little = phase(wa, wb, h1, little)
    wa.step(Y), wb.step(X)
    wa_got, wb_got = [across(wa.parts[0])], [across(wb.parts[0])]

    g_all = jnp.take(little[:, 8:], places, axis=0).reshape(8 * chips, D)
    lanes = -(-4 * rows // TILE) * TILE
    gw = jnp.pad(nt(g_all, w_back[0]).astype(BF), ((0, 0), (0, lanes - 4 * rows))).reshape(chips, 8, lanes)
    gw = lax.all_to_all(gw, "dp", 0, 0)
    h1, shared, gw = phase(wa, wb, h1, shared, gw)
    wa_got += [across(wa.parts[1])]
    wb_got += [across(wb.parts[1])]
    back_at = count + 2 * self_rows
    shared_back = shared[:: 2**pre, back_at:]
    back_got = across(shared_back)

    def self_part(index):
        at = count + index * self_rows
        return shared[:, at : at + self_rows].reshape(D // 2, D)

    self_own = jnp.concatenate([self_part(0), self_part(1)], axis=1)
    gw = gw[:, :, : 4 * rows].transpose(1, 0, 2).reshape(8, FF)
    gw_got = across(gw)
    wa_got, wb_got, back_got, h1, n1, c, n2, shared, self_own, gw, gw_got = phase(
        wa_got, wb_got, back_got, h1, n1, c, n2, shared, self_own, gw, gw_got
    )
    gw = jnp.where(first, gw_got, gw)
    self_got, shared_got = across(self_own), across(shared)
    n1_got, c_got, n2_got = across(n1), across(c), across(n2)
    w_in_from = in_sources(wa.sets(wa_got), wb.sets(wb_got))
    w_back_from = back_sources(wb.sets(wb_got), shared_back if pre else shared, 0 if pre else back_at, back_got)
    f, slope, e = enc_ffn(meta, h1, n2, w_in_from, w_back_from)
    e, shared_got, n1_got, c_got, n2_got, self_got = phase(e, shared_got, n1_got, c_got, n2_got, self_got)
    dec_sets = [(v[:: 2**pre] if pre else v, None, other) for other, v in enumerate((shared, shared_got))]
    m1, sv, z1, m2, qc, qk, gm = dec_before(meta, dec_in, d_out, gains1, self_own, self_got, dec_sets)
    f, qk = phase(f, qk)
    f_got = across(f)
    de, cc, z2, m3, fc, duc, da2, dz2, dcc, edt, ebar, dg_ffn1, de_other, pairs_other = dec_core(
        meta, e, segr, qk, qc, z1, gm, gw, gains1, dec_sets
    )

    def two(parts):
        return Sum(parts[0], parts[1], pre), Sum(parts[2], parts[3], pre)

    de_got, pairs_got = across(de_other), across(pairs_other)
    du, du_other = enc_hidden_grad(meta, de, slope, w_back_from)
    de_got, pairs_got, du, du_other, edt = phase(de_got, pairs_got, du, du_other, edt)
    du_got = across(du_other)
    acts, acts_send, dec_grad, dg_attn1, dg_self, k_keep, k_send = dec_after(
        meta, dec_in, z1, dz2, qc, dcc, edt, ebar, pairs_got, gains1, [m1, sv, m2, cc, m3, da2], duc, fc,
        self_own, self_got, dec_sets,
    )
    acts, acts_send, f, f_got = phase(acts, acts_send, f, f_got)
    acts_got, width = across(acts_send), acts.shape[1]
    own = (jnp.arange(8)[:, None] // 4) == core
    acts = jnp.where(own, acts, acts_got)
    acts = lax.all_gather(acts, "dp").reshape(8 * chips, width)
    back_a, back_b = two(enc_w_back_grad(meta, de, de_got, f, f_got))
    n2, du_got = phase(back_a, back_b, n2, du_got)
    back_a.step(Y), back_b.step(X)
    in_a, in_b = two(enc_w_in_grad(meta, du, du_got, n2, n2_got, k_keep, k_send))
    h1 = phase(in_a, in_b, h1)
    in_a.step(Y), in_b.step(X)
    dh1, da, dg_ffn0 = enc_ffn_back(meta, du, h1, de, gains0, w_in_from)
    da = phase(back_a, back_b, da)
    back_a.step(X), back_b.step(Y)
    dq, dk, dv, diag, other = enc_attention_back(meta, da, q, k, v, lse, segr, segc, windows, sb.sets(sb_got))
    dq, other = phase(back_a, back_b, in_a, in_b, dq, other)
    got = across(other)
    in_a.step(X), in_b.step(Y)
    backs = merged([back_a, back_b])
    backs.step(Z0)
    keep, send, dg_attn0 = enc_input_grad(meta, dq, dk, dv, x, dh1, gains0, sa.sets(sa_got), sb.sets(sb_got))
    got, dq, dg_attn0 = phase(backs, got, dq, dg_attn0)
    backs.step(Z1)
    square_a, square_b = two(enc_square_grads(meta, n1, n1_got, c, c_got, dq, dk, dv, da, got))
    table = jnp.einsum("hdt,dtb->bh", diag, diagonal_onehots(), precision=lax.Precision.HIGHEST)
    little = jnp.concatenate([
        dg_attn0, dg_ffn0, dg_attn1, dg_ffn1, dg_self,
        jnp.pad(table.reshape(1, -1), ((0, 0), (0, D - BUCKETS * HEADS))), jnp.zeros((2, D), F32),
    ])
    little = little + across(little)
    for bit in range(pre):
        little = little + along(little, bit)
    acts, little = phase(square_a, square_b, in_a, in_b, acts, little)
    square_a.step(Y), square_b.step(X)
    theirs = across(acts)
    other = along(little, X + pre)
    ins = merged([in_a, in_b])
    ins.step(Z0)

    dec_q, dec_o, dec_i, dec_b, g_self_value, g_self_out, y = dec_weight_grads(
        jnp.stack([chip, core]), acts, theirs, g_all, w_back[0], rows, self_rows
    )
    other, y = phase(square_a, square_b, ins, backs, other, y)
    little = little + other
    square_a.step(X), square_b.step(Y), ins.step(Z1)
    other = along(little, Y + pre)
    other, y, send, z2 = phase(square_a, square_b, other, y, send, z2)
    little = little + other
    squares = merged([square_a, square_b])
    squares.step(Z0)
    other = along(little, Z0 + pre)
    z2 = z2 + across(z2)
    y = lax.all_to_all(y.reshape(chips, 8, D), "dp", 0, 0)
    other, y = phase(squares, ins, other, y)
    little = little + other
    squares.step(Z1)
    little = little + along(little, Z1 + pre)
    backs_sum, ins_sum, square_sum = backs.total(), ins.total(), squares.total()
    dec_out = (z2 + jnp.sum(y.astype(F32), axis=0)).astype(BF)
    dec_out = jnp.where(first, across(dec_out), dec_out)
    mine = chip * rows

    g_rel_table = little[5, : BUCKETS * HEADS].reshape(BUCKETS, HEADS)

    def cut(index, at, count):
        return lax.dynamic_slice_in_dim(little[index], at, count, 0)

    g_attn_gain = cut(jnp.where(first, 0, 2), mine, rows)[None]
    g_ffn_gain = cut(jnp.where(first, 1, 3), mine, rows)[None]
    g_self_gain = cut(4, at_self, self_rows)

    backs_got, ins_got, square_got = [across(v.astype(BF)).astype(F32) for v in (backs_sum, ins_sum, square_sum)]

    def group(value, index):
        return value[index * GROUP : (index + 1) * GROUP]

    def placed(enc_value, dec_value):
        return jnp.where(first, narrowed(enc_value, pre, chip), dec_value)[None]

    g_w_query = placed(group(square_sum, 0), dec_q)
    g_w_out = placed(group(square_sum, 1), dec_o)
    g_w_key = narrowed(jnp.where(first, group(square_got, 0), group(ins_got, 1)), pre, chip)[None]
    g_w_value = narrowed(jnp.where(first, group(square_got, 1), group(ins_sum, 1)), pre, chip)[None]
    g_w_in = placed(
        jnp.concatenate([group(ins_sum, 0), group(ins_sum, 2), group(ins_got, 0), group(ins_got, 2)], axis=1), dec_i
    )
    half = D // 2
    tall = [
        jnp.concatenate([group(v, i)[:, j * half : (j + 1) * half] for i in range(2) for j in range(2)])
        for v in (backs_sum, backs_got)
    ]
    g_w_back = placed(jnp.concatenate(tall, axis=1), dec_b)

    other_half = across(send)
    enc_in_grad = jnp.where(first, jnp.stack([keep, other_half]), jnp.stack([other_half, keep]))
    dec_grad = dec_grad + across(dec_grad)
    half = D // 2
    dec_out = jnp.where(first, dec_out[:, :half], dec_out[:, half:])
    dec_in_grad = jnp.where(first, dec_grad[:, :half], dec_grad[:, half:])
    return (
        dec_out, enc_in_grad, dec_in_grad, g_attn_gain, g_w_query, g_w_key, g_w_value, g_w_out, g_ffn_gain,
        g_w_in, g_w_back, g_self_gain, g_self_value, g_self_out, g_rel_table,
    )


def solution(mesh):
    return jax.shard_map(
        per_device,
        mesh=mesh,
        in_specs=(
            P("dp", None, None),
            P("dp", None),
            P("dp", None),
            P("dp", None),
            P("section", "dp"),
            P("section", "dp", None),
            P("section", "dp", None),
            P("section", "dp", None),
            P("section", "dp", None),
            P("section", "dp"),
            P("section", "dp", None),
            P("section", "dp", None),
            P(("section", "dp")),
            P(("section", "dp"), None),
            P(("section", "dp"), None),
            P(),
        ),
        out_specs=(
            P("dp", "section"),
            P("dp", None, "section"),
            P("dp", "section"),
            P("section", "dp"),
            P("section", "dp", None),
            P("section", "dp", None),
            P("section", "dp", None),
            P("section", "dp", None),
            P("section", "dp"),
            P("section", "dp", None),
            P("section", "dp", None),
            P(("section", "dp")),
            P(("section", "dp"), None),
            P(("section", "dp"), None),
            P(),
        ),
        check_vma=False,
    )
```

```python
import functools

import jax
import jax.numpy as jnp
import numpy as np
from jax import lax
from jax.experimental import pallas as pl
from jax.experimental.pallas import tpu as pltpu
from jax.sharding import PartitionSpec as P

D = 768
HEADS = 12
HEAD_DIM = 64
FF = 3072
BUCKETS = 32
MAX_DIST = 128
ROW_LEN = 512
SEGS = 4
GROUP = 48
GROUPS = D // GROUP
X, Y, Z0, Z1 = 0, 1, 2, 3
TILE = 128
EPS = 1e-06
MASKED = -1000000000.0
BF = jnp.bfloat16
F32 = jnp.float32
SPEED = 0.25
VMEM_LIMIT = 58 * 1024 * 1024


def bucket_of(offset):
    half, exact = BUCKETS // 2, BUCKETS // 4
    exponent, growth = half - exact, MAX_DIST // exact
    distance = abs(offset)
    if distance < exact:
        level = distance
    else:
        k = 0
        while k < exponent and exact**exponent * growth ** (k + 1) <= distance**exponent:
            k += 1
        level = min(exact + k, half - 1)
    return (half if offset > 0 else 0) + level


def window_onehots():
    table = np.zeros((2, 3, 2 * TILE, BUCKETS), np.float32)
    for d in range(3):
        for t in range(2 * TILE):
            table[0, d, t, bucket_of(TILE * (d - 1) - TILE + t)] = 1.0
            table[1, d, t, bucket_of(TILE * (d - 1) + TILE - t)] = 1.0
    return table


def diagonal_onehots():
    table = np.zeros((5, 2 * TILE, BUCKETS), np.float32)
    table[1:4] = window_onehots()[1]
    table[0, :, bucket_of(-TILE - 1)] = 1.0
    table[4, :, bucket_of(TILE + 1)] = 1.0
    return table


def across(value):
    return lax.ppermute(value, "section", [(0, 1), (1, 0)])


def along(value, bit):
    count = lax.axis_size("dp")
    return lax.ppermute(value, "dp", [(i, i ^ (1 << bit)) for i in range(count)])


def bit_of(index, bit):
    return lax.rem(lax.div(index, 1 << bit), 2)


def low_bits(rows):
    count = 0
    while rows < GROUP:
        rows *= 2
        count += 1
    return count


def filled(piece, pre, chip, axis):
    for bit in range(pre):
        other = along(piece, bit)
        upper = bit_of(chip, bit) == 1
        first = jnp.where(upper, other, piece)
        second = jnp.where(upper, piece, other)
        piece = jnp.concatenate([first, second], axis=axis)
    return piece


def narrowed(total, pre, chip):
    for bit in reversed(range(pre)):
        length = total.shape[0] // 2
        upper = bit_of(chip, bit)
        kept = lax.dynamic_slice_in_dim(total, upper * length, length, 0)
        sent = lax.dynamic_slice_in_dim(total, (1 - upper) * length, length, 0)
        total = added(kept, along(sent.astype(BF), bit), F32)
    return total


def phase(*things):
    tree = [thing.arrays() if isinstance(thing, (Chain, Sum)) else thing for thing in things]
    out = []
    for thing, value in zip(things, lax.optimization_barrier(tree)):
        if isinstance(thing, (Chain, Sum)):
            thing.replace(value)
        else:
            out.append(value)
    return out[0] if len(out) == 1 else out


class Chain:
    def __init__(self, parts, ids, pre):
        self.parts, self.ids, self.pre = parts, ids, pre

    def arrays(self):
        return list(self.parts)

    def replace(self, values):
        self.parts = values

    def split(self, at):
        cut = [[part[:, :at] for part in self.parts], [part[:, at:] for part in self.parts]]
        return [Chain(parts, self.ids, self.pre) for parts in cut]

    def step(self, bit):
        held = self.parts[0] if len(self.parts) == 1 else jnp.concatenate(self.parts, axis=0)
        self.parts = [held, along(held, bit + self.pre)]
        self.old_ids = self.ids
        self.ids = self.ids + [g ^ (1 << bit) for g in self.ids]

    def sets(self, others):
        first, last = self.old_ids, self.ids[len(self.old_ids) :]
        return [(self.parts[0], first, 0), (self.parts[1], last, 0), (others[0], first, 1), (others[1], last, 1)]


def added(left, right, kind=BF):
    return (left.astype(F32) + right.astype(F32)).astype(kind)


class Sum:
    def __init__(self, keep, send, pre):
        self.mine, self.other, self.pre, self.fresh = keep, send, pre, True

    def arrays(self):
        return [self.mine, self.other]

    def replace(self, values):
        self.mine, self.other = values

    def step(self, bit):
        if self.fresh:
            send, self.fresh = self.other, False
        else:
            half = self.mine.shape[0] // 2
            send = added(self.mine[half:], self.other[half:])
            self.mine = added(self.mine[:half], self.other[:half])
        self.other = along(send, bit + self.pre)

    def total(self):
        return added(self.mine[0], self.other[0], F32)


def merged(sums):
    one = Sum(
        jnp.concatenate([part.mine for part in sums], axis=1),
        jnp.concatenate([part.other for part in sums], axis=1),
        sums[0].pre,
    )
    one.fresh = False
    return one


def nn(a, b):
    return lax.dot_general(a, b, (((1,), (0,)), ((), ())), preferred_element_type=F32)


def nt(a, b):
    return lax.dot_general(a, b, (((1,), (1,)), ((), ())), preferred_element_type=F32)


def tn(a, b):
    return lax.dot_general(a, b, (((0,), (0,)), ((), ())), preferred_element_type=F32)


def rms(v, gain):
    return v * lax.rsqrt(jnp.mean(v * v, axis=-1, keepdims=True) + EPS) * gain


def rms_back(v, gain, dy):
    r = lax.rsqrt(jnp.mean(v * v, axis=-1, keepdims=True) + EPS)
    dgain = jnp.sum(dy * v * r, axis=0, keepdims=True)
    dyg = dy * gain
    dv = r * dyg - v * (r * r * r) * jnp.mean(v * dyg, axis=-1, keepdims=True)
    return dv, dgain


def gelu_both(u):
    c = 0.7978845608028654
    square = u * u
    half = 0.5 + 0.5 * jnp.tanh(u * (c + (0.044715 * c) * square))
    value = u * half
    return value, half + value * (1.0 - half) * (2.0 * c + (6.0 * 0.044715 * c) * square)


def square_row(b):
    return lambda core, g: (core * 2 + b) * D + GROUP * g


def back_row(b):
    return lambda core, g: 4 * GROUP * g + GROUP * (2 * core + b)


def in_items(first):
    return [(first + GROUP * b, GROUP, square_row(b), lambda core, g, b=b: 2 * core + b) for b in range(2)]


def in_sources(a_sets, b_sets):
    cut = 2 * GROUP // 3
    later = lambda core, g: square_row(1)(core, g) + cut
    block = lambda core, g: 2 * core + 1
    return [
        (a_sets, [(0, GROUP, square_row(0), lambda core, g: 2 * core), (GROUP, cut, square_row(1), block)]),
        (b_sets, [(GROUP, GROUP - cut, later, block)]),
    ]


def back_sources(b_sets, shared, first, got):
    quarter = lambda core, g: g // 4
    return [
        (b_sets, [(0, GROUP, back_row(0), quarter)]),
        ([(shared, None, 0)], [(first, GROUP, back_row(1), quarter)]),
        ([(got, None, 1)], [(0, GROUP, back_row(1), quarter)]),
    ]


def arrays_of(sources):
    return [part for sets, items in sources for part, ids, other in sets]


def start_sources(meta, refs, sources, dst, sems, turn=None):
    at = 0
    for k, (sets, items) in enumerate(sources):
        plan = [(ids, other) for part, ids, other in sets]
        if turn is not None:
            items = (items[:1] if turn == 0 else items[1:]) if k == 0 else items * turn
        start_fetch(meta, refs[at : at + len(plan)], plan, items, dst, sems)
        at += len(plan)


def start_fetch(meta, refs, plan, items, dst, sem, only=None):
    if only is not None:
        for other in range(2):
            part = [(ref, entry) for ref, entry in zip(refs, plan) if entry[1] == other]

            @pl.when(jnp.bitwise_xor(meta[1], other) == only)
            def _():
                start_fetch(meta, [r for r, e in part], [e for r, e in part], items, dst, sem)

        return
    me, core = meta[0], meta[1]
    for first, count, row_of, *sem_of in items:
        for ref, (ids, other) in zip(refs, plan):
            source = 1 - core if other else core
            for slot in range(ref.shape[0]):
                group = jnp.int32(slot) if ids is None else jnp.bitwise_xor(me, ids[slot])
                off = pl.multiple_of(row_of(source, group), 16)
                at = sem.at[sem_of[0](source, group)] if sem_of else sem
                pltpu.make_async_copy(ref.at[slot, pl.ds(first, count)], dst.at[pl.ds(off, count)], at).start()


def start_copy(src, dst, sem):
    pltpu.make_async_copy(src, dst, sem).start()


def drain(ref, sem):
    pltpu.make_async_copy(ref, ref, sem).wait()


def slot_of(meta, group, b):
    rel = jnp.bitwise_xor(meta[0], group)
    x, y, z0, z1 = [jnp.bitwise_and(rel // (1 << bit), 1) for bit in range(4)]
    return (8 * y + 4 * x if b == 0 else 8 * x + 4 * y) + 2 * z0 + z1


def start_store(meta, src, group, b, keep, send, sem, rows=slice(None), cols=slice(None)):
    slot = slot_of(meta, group, b)
    at = (rows, cols)

    @pl.when(slot < GROUPS // 2)
    def _():
        pltpu.make_async_copy(src, keep.at[(slot,) + at], sem).start()

    @pl.when(slot >= GROUPS // 2)
    def _():
        pltpu.make_async_copy(src, send.at[(slot - GROUPS // 2,) + at], sem).start()


def head_lanes(h):
    lane = lax.broadcasted_iota(jnp.int32, (1, D), 1)
    return (lane >= h * HEAD_DIM) & (lane < (h + 1) * HEAD_DIM)


def pair_lanes(hh):
    lane = lax.broadcasted_iota(jnp.int32, (1, TILE), 1)
    return (lane < HEAD_DIM) if hh == 0 else (lane >= HEAD_DIM)


def masked(value, lanes):
    return jnp.where(lanes, value, jnp.zeros_like(value))


def fill_bias(window_ref, tiles, transposed):
    part = 1 if transposed else 0

    def one(h, carry):
        for d in range(3):
            row = jnp.broadcast_to(window_ref[h, pl.ds(part * 3 + d, 1), :], (TILE, 2 * TILE))
            rolled = pltpu.roll(row, TILE, 1, stride=1, stride_axis=0)
            tiles[h, d + 1] = rolled[:, :TILE]
        low = window_ref[h, pl.ds(0, 1), pl.ds(0, 1)]
        high = window_ref[h, pl.ds(2, 1), pl.ds(2 * TILE - 1, 1)]
        tiles[h, 0] = jnp.broadcast_to(low, (TILE, TILE))
        tiles[h, 4] = jnp.broadcast_to(high, (TILE, TILE))
        return carry

    lax.fori_loop(0, HEADS, one, 0)


def spec(space):
    return space if isinstance(space, pl.BlockSpec) else pl.BlockSpec(memory_space=space)


def call(body, name, ins, spaces, outs, out_spaces, scratch, us, aliases={}, grid=()):
    if grid:
        specs = {
            "grid_spec": pltpu.PrefetchScalarGridSpec(
                num_scalar_prefetch=1,
                grid=grid,
                in_specs=[spec(s) for s in spaces[1:]],
                out_specs=[spec(s) for s in out_spaces],
                scratch_shapes=scratch,
            )
        }
    else:
        specs = {
            "in_specs": [spec(s) for s in spaces],
            "out_specs": [spec(s) for s in out_spaces],
            "scratch_shapes": scratch,
        }
    return pl.pallas_call(
        body,
        name=name,
        out_shape=[jax.ShapeDtypeStruct(s, k) for s, k in outs],
        input_output_aliases=aliases,
        compiler_params=pltpu.CompilerParams(vmem_limit_bytes=VMEM_LIMIT),
        cost_estimate=pl.CostEstimate(flops=int(us * SPEED * 1.1e9), bytes_accessed=int(us * SPEED * 1e6), transcendentals=0),
        **specs,
    )(*ins)


VM, SM, ANY = pltpu.VMEM, pltpu.SMEM, pl.ANY


def plan_of(sets):
    return [part for part, ids, other in sets], [(ids, other) for part, ids, other in sets]


def bias_block(tiles, h, ib):
    return jnp.concatenate([
        jnp.concatenate([tiles[h, min(max(jb - (2 * ib + i), -2), 2) + 2] for i in range(2)], axis=1)
        for jb in range(ROW_LEN // TILE)
    ], axis=0)


def enc_attention(meta, x, gains, segr, segc, windows, a_sets, b_sets):
    a_arrays, a_plan = plan_of(a_sets)
    b_arrays, b_plan = plan_of(b_sets)
    n = len(a_arrays)
    wide = 2 * TILE

    def body(meta, x, gains, segr, segc, windows, *rest):
        a_parts, b_parts, rest = rest[:n], rest[n : 2 * n], rest[2 * n :]
        n1, q, k, v, c, h1, n2, lse, w, tiles, sems = rest
        start_fetch(meta, a_parts, a_plan, [(0, GROUP, square_row(0))], w, sems.at[0])
        start_fetch(meta, b_parts, b_plan, [(0, GROUP, square_row(1))], w, sems.at[0])
        fill_bias(windows, tiles, True)
        xf = x[...].astype(F32)
        n1[...] = rms(xf, gains[0:1, :]).astype(BF)
        drain(w, sems.at[0])
        for ref, at in ((q, 0), (k, 2), (v, 3)):
            ref[...] = nn(n1[...], w[at * D : (at + 1) * D, :]).astype(BF)
        lse[...] = jnp.zeros_like(lse)

        def pair(pr, carry):
            cols = pl.ds(pl.multiple_of(pr * TILE, TILE), TILE)
            for ib in range(ROW_LEN // wide):
                rows = slice(ib * wide, (ib + 1) * wide)
                same = segc[...] == segr[:, rows]
                total = None
                for hh in range(2):
                    h = 2 * pr + hh
                    lanes = pair_lanes(hh)
                    s = nt(masked(k[:, cols], lanes), q[rows, cols]) + bias_block(tiles, h, ib)
                    s = jnp.where(same, s, MASKED)
                    top = jnp.max(s, axis=0, keepdims=True)
                    ex = jnp.exp(s - top)
                    tot = jnp.sum(ex, axis=0, keepdims=True)
                    p = (ex * (1.0 / tot)).astype(BF)
                    part = tn(p, masked(v[:, cols], lanes))
                    total = part if total is None else total + part
                    lse[pl.ds(h, 1), rows] = top + jnp.log(tot)
                c[rows, cols] = total.astype(BF)
            return carry

        lax.fori_loop(0, HEADS // 2, pair, 0)
        res = x[...].astype(F32) + nn(c[...], w[D : 2 * D, :])
        h1[...] = res
        n2[...] = rms(res, gains[1:2, :]).astype(BF)

    rows = (ROW_LEN, D)
    return call(
        body, "enc_attention", [meta, x, gains, segr, segc, windows, *a_arrays, *b_arrays],
        [SM, VM, VM, VM, VM, VM] + [ANY] * (2 * n),
        [(rows, BF)] * 5 + [(rows, F32), (rows, BF), ((TILE, ROW_LEN), F32), ], [VM] * 8,
        [pltpu.VMEM((4 * D, D), BF), pltpu.VMEM((HEADS, 5, TILE, TILE), F32), pltpu.SemaphoreType.DMA((2,))],
        us=20,
    )


PART = (GROUPS // 2, GROUP, D)
WIDE_PART = (GROUPS // 2, 2 * GROUP, D)
BLOCKS = FF // D


def enc_ffn(meta, h1, n2, w_in_from, w_back_from):
    in_arrays, back_arrays = arrays_of(w_in_from), arrays_of(w_back_from)
    n, m = len(in_arrays), len(back_arrays)

    def body(meta, h1, n2, *rest):
        ins, backs, rest = rest[:n], rest[n : n + m], rest[n + m :]
        f_out, slope_out, e, w_in, w_back, acc, normed, f, slope, sems = rest
        start_copy(n2, normed, sems.at[8])
        start_sources(meta, ins, w_in_from, w_in, sems)
        start_copy(h1, acc, sems.at[9])
        start_sources(meta, backs, w_back_from, w_back, sems.at[pl.ds(4, 4)])
        drain(normed, sems.at[8])
        for at, b in enumerate((0, 2, 1, 3)):
            rows = slice(b * D, (b + 1) * D)
            slot = at % 2
            drain(w_in.at[rows], sems.at[b])
            value, grad = gelu_both(nn(normed[...], w_in[rows, :]))
            if at >= 2:
                drain(f.at[slot], sems.at[10 + slot])
                drain(slope.at[slot], sems.at[12 + slot])
            f[slot] = value.astype(BF)
            start_copy(f.at[slot], f_out.at[:, rows], sems.at[10 + slot])
            slope[slot] = grad.astype(BF)
            start_copy(slope.at[slot], slope_out.at[:, rows], sems.at[12 + slot])
            if at == 0:
                drain(acc, sems.at[9])
            drain(w_back.at[rows], sems.at[4 + b])
            acc[...] += nn(f[slot], w_back[rows, :])
        e[...] = acc[...].astype(BF)
        for slot in range(2):
            drain(f.at[slot], sems.at[10 + slot])
            drain(slope.at[slot], sems.at[12 + slot])

    block = (2, ROW_LEN, D)
    return call(
        body, "enc_ffn", [meta, h1, n2, *in_arrays, *back_arrays], [SM, ANY, ANY] + [ANY] * (n + m),
        [((ROW_LEN, FF), BF), ((ROW_LEN, FF), BF), ((ROW_LEN, D), BF)], [ANY, ANY, VM],
        [pltpu.VMEM((FF, D), BF), pltpu.VMEM((FF, D), BF), pltpu.VMEM((ROW_LEN, D), F32), pltpu.VMEM((ROW_LEN, D), BF),
         pltpu.VMEM(block, BF), pltpu.VMEM(block, BF), pltpu.SemaphoreType.DMA((14,))],
        us=15,
    )


PART = (GROUPS // 2, GROUP, D)
WIDE_PART = (GROUPS // 2, 2 * GROUP, D)
BLOCKS = FF // D


def enc_ffn(meta, h1, n2, w_in_from, w_back_from):
    in_arrays, back_arrays = arrays_of(w_in_from), arrays_of(w_back_from)
    n, m = len(in_arrays), len(back_arrays)

    def body(meta, h1, n2, *rest):
        ins, backs, rest = rest[:n], rest[n : n + m], rest[n + m :]
        f, slope, e, w_in, w_back, acc, sems = rest
        start_sources(meta, ins, w_in_from, w_in, sems)
        start_sources(meta, backs, w_back_from, w_back, sems.at[pl.ds(4, 4)])
        acc[...] = h1[...]

        def block(b, carry):
            rows = pl.ds(pl.multiple_of(b * D, D), D)

            drain(w_in.at[rows], sems.at[b])
            value, grad = gelu_both(nn(n2[...], w_in[rows, :]))
            fb = value.astype(BF)
            f[:, rows] = fb
            slope[:, rows] = grad.astype(BF)
            drain(w_back.at[rows], sems.at[4 + b])
            acc[...] += nn(fb, w_back[rows, :])
            return carry

        lax.fori_loop(0, FF // D, block, 0)
        e[...] = acc[...].astype(BF)

    return call(
        body, "enc_ffn", [meta, h1, n2, *in_arrays, *back_arrays], [SM, VM, VM] + [ANY] * (n + m),
        [((ROW_LEN, FF), BF), ((ROW_LEN, FF), BF), ((ROW_LEN, D), BF)], [VM] * 3,
        [pltpu.VMEM((FF, D), BF), pltpu.VMEM((FF, D), BF), pltpu.VMEM((ROW_LEN, D), F32),
         pltpu.SemaphoreType.DMA((8,))],
        us=15,
    )


def enc_hidden_grad(meta, de, slope, w_back_from):
    arrays = arrays_of(w_back_from)
    n = len(arrays)

    def body(meta, de, slope, *rest):
        parts, rest = rest[:n], rest[n:]
        du_out, other, w, slopes, du, sems = rest
        start_sources(meta, parts, w_back_from, w, sems)
        for b in range(BLOCKS):
            start_copy(slope.at[:, b * D : (b + 1) * D], slopes.at[b], sems.at[4 + b])
        for b in range(BLOCKS):
            cols = slice(b * D, (b + 1) * D)
            drain(w.at[cols], sems.at[b])
            drain(slopes.at[b], sems.at[4 + b])
            du[b] = (slopes[b].astype(F32) * nt(de[...], w[cols, :])).astype(BF)
            start_copy(du.at[b], du_out.at[:, cols], sems.at[8])

            @pl.when(meta[1] != b // 2)
            def _():
                start_copy(du.at[b], other.at[:, (b % 2) * D : (b % 2 + 1) * D], sems.at[9])

        drain(du, sems.at[8])
        drain(du.at[pl.ds(0, 2)], sems.at[9])

    block = (BLOCKS, ROW_LEN, D)
    return call(
        body, "enc_hidden_grad", [meta, de, slope, *arrays], [SM, VM, ANY] + [ANY] * n,
        [((ROW_LEN, FF), BF), ((ROW_LEN, FF // 2), BF)], [ANY, ANY],
        [pltpu.VMEM((FF, D), BF), pltpu.VMEM(block, BF), pltpu.VMEM(block, BF), pltpu.SemaphoreType.DMA((10,))],
        us=8,
    )


def enc_w_back_grad(meta, de, de_got, f, f_got):
    half = D // 2

    def body(meta, de, de_got, f, f_got, keep_a, send_a, keep_b, send_b, mine, theirs, fs, buf, sems):
        start_copy(de.at[:, pl.ds(pl.multiple_of(meta[1] * half, TILE), half)], mine, sems.at[2])
        start_copy(de_got, theirs, sems.at[3])
        for b in range(BLOCKS):
            for k, ref in enumerate((f, f_got)):
                start_copy(ref.at[:, b * D : (b + 1) * D], fs.at[b, k], sems.at[4 + b])
        drain(mine, sems.at[2])
        drain(theirs, sems.at[3])
        for b in range(BLOCKS):
            at = b % 2
            if b >= 2:
                drain(buf.at[at], sems.at[at])
            drain(fs.at[b], sems.at[4 + b])
            buf[at] = (tn(fs[b, 0], mine[...]) + tn(fs[b, 1], theirs[...])).astype(BF)
            for k in range(D // GROUP):
                group, piece = b * (D // GROUP // 4) + k // 4, k % 4
                keep, send = (keep_a, send_a) if piece < 2 else (keep_b, send_b)
                start_store(meta, buf.at[at, pl.ds(k * GROUP, GROUP)], group, piece // 2, keep, send, sems.at[at],
                            cols=pl.ds((piece % 2) * half, half))
        drain(buf.at[0], sems.at[0])
        drain(buf.at[1], sems.at[1])

    part = pltpu.VMEM((ROW_LEN, half), BF)
    return call(
        body, "enc_w_back_grad", [meta, de, de_got, f, f_got], [SM] + [ANY] * 4,
        [(PART, BF)] * 4, [ANY] * 4,
        [part, part, pltpu.VMEM((BLOCKS, 2, ROW_LEN, D), BF), pltpu.VMEM((2, D, half), BF), pltpu.SemaphoreType.DMA((8,))],
        us=7,
    )


def enc_w_in_grad(meta, du, du_got, n2, n2_got, wide_keep, wide_send):
    def body(meta, du, du_got, n2, n2_got, wide_keep, wide_send, keep_a, send_a, keep_b, send_b, buf, sems):
        for b in range(2):
            cols = pl.ds(pl.multiple_of(meta[1] * (FF // 2) + b * D, TILE), D)
            buf[b] = (tn(n2[...], du[:, cols]) + tn(n2_got[...], du_got[:, b * D : (b + 1) * D])).astype(BF)
            keep, send = (keep_a, send_a) if b == 0 else (keep_b, send_b)
            for g in range(GROUPS):
                rows = pl.ds(0, GROUP)
                start_store(meta, buf.at[b, pl.ds(g * GROUP, GROUP)], g, b, keep, send, sems.at[b], rows)
        drain(buf.at[0], sems.at[0])
        drain(buf.at[1], sems.at[1])

    return call(
        body, "enc_w_in_grad", [meta, du, du_got, n2, n2_got, wide_keep, wide_send], [SM] + [VM] * 4 + [ANY] * 2,
        [(WIDE_PART, BF), (WIDE_PART, BF), (PART, BF), (PART, BF)], [ANY] * 4,
        [pltpu.VMEM((2, D, D), BF), pltpu.SemaphoreType.DMA((2,))],
        us=7, aliases={5: 0, 6: 1},
    )


def enc_ffn_back(meta, du, h1, de, gains, w_in_from):
    arrays = arrays_of(w_in_from)
    n = len(arrays)

    def body(meta, du, h1, de, gains, *rest):
        parts, rest = rest[:n], rest[n:]
        dh1, da, dgain, w, acc, dus, h1s, des, sems = rest
        for first in range(2):
            for b in (first, first + 2):
                start_copy(du.at[:, b * D : (b + 1) * D], dus.at[b], sems.at[4 + b])
            start_sources(meta, parts, w_in_from, w, sems, first)
        start_copy(h1, h1s, sems.at[8])
        start_copy(de, des, sems.at[9])
        for k, b in enumerate((0, 2, 1, 3)):
            cols = slice(b * D, (b + 1) * D)
            drain(w.at[cols], sems.at[b])
            drain(dus.at[b], sems.at[4 + b])
            part = nt(dus[b], w[cols, :])
            acc[...] = part if k == 0 else acc[...] + part
        drain(h1s, sems.at[8])
        drain(des, sems.at[9])
        dv, dg = rms_back(h1s[...], gains[1:2, :], acc[...])
        total = des[...].astype(F32) + dv
        dh1[...] = total
        da[...] = total.astype(BF)
        dgain[...] = dg

    rows = (ROW_LEN, D)
    return call(
        body, "enc_ffn_back", [meta, du, h1, de, gains, *arrays], [SM, ANY, ANY, ANY, VM] + [ANY] * n,
        [(rows, F32), (rows, BF), ((1, D), F32)], [VM, VM, VM],
        [pltpu.VMEM((FF, D), BF), pltpu.VMEM(rows, F32), pltpu.VMEM((BLOCKS, ROW_LEN, D), BF), pltpu.VMEM(rows, F32),
         pltpu.VMEM(rows, BF), pltpu.SemaphoreType.DMA((10,))],
        us=8,
    )


def enc_attention_back(meta, da, q, k, v, lse, segr, segc, windows, sets):
    arrays, plan = plan_of(sets)
    n = len(arrays)
    wide = 2 * TILE

    def body(meta, da, q_in, k_in, v_in, lse, segr, segc, windows, *rest):
        parts, rest = rest[:n], rest[n:]
        dq_out, dk_out, dv_out, diag, other, w, dc, tiles, sums, kacc, vacc, q, k, v, dq, dk, dv, sems = rest
        sem = sems.at[0]
        start_fetch(meta, parts, plan, [(0, GROUP, lambda core, g: GROUP * g)], w, sem, only=0)
        for at, (src, dst) in enumerate(((q_in, q), (k_in, k), (v_in, v))):
            start_copy(src, dst, sems.at[1 + at])
        fill_bias(windows, tiles, True)
        drain(w, sem)
        dc[...] = nt(da[...], w[...]).astype(BF)
        for at, ref in enumerate((q, k, v)):
            drain(ref, sems.at[1 + at])
        row = lax.broadcasted_iota(jnp.int32, (TILE, TILE), 0)
        col = lax.broadcasted_iota(jnp.int32, (TILE, TILE), 1)
        flip = (row + col == TILE - 1).astype(F32)

        def pair(pr, carry):
            cols = pl.ds(pl.multiple_of(pr * TILE, TILE), TILE)
            for hh in range(2):
                h = 2 * pr + hh
                lanes = pair_lanes(hh)
                km, vm = masked(k[:, cols], lanes), masked(v[:, cols], lanes)
                sums[...] = jnp.zeros_like(sums)
                for ib in range(ROW_LEN // wide):
                    rows = slice(ib * wide, (ib + 1) * wide)
                    same = segc[...] == segr[:, rows]
                    qp, dcp = q[rows, cols], dc[rows, cols]
                    s = jnp.where(same, nt(km, qp) + bias_block(tiles, h, ib), MASKED)
                    prob = jnp.exp(s - lse[pl.ds(h, 1), rows])
                    dprob = nt(vm, dcp)
                    inner = jnp.sum(prob * dprob, axis=0, keepdims=True)
                    ds = (prob * (dprob - inner)).astype(BF)
                    dvp = nn(prob.astype(BF), masked(dcp, lanes))
                    dkp = nn(ds, masked(qp, lanes))
                    dqp = tn(ds, km)
                    if hh == 0 and ib == 0:
                        vacc[...], kacc[...] = dvp, dkp
                    else:
                        vacc[...] += dvp
                        kacc[...] += dkp
                    if hh == 0:
                        dq[rows, cols] = dqp.astype(BF)
                    else:
                        dq[rows, cols] = dq[rows, cols] + dqp.astype(BF)
                    for jb in range(ROW_LEN // TILE):
                        for i in range(2):
                            d = min(max(jb - (2 * ib + i), -2), 2) + 2
                            sums[d] += ds[jb * TILE : (jb + 1) * TILE, i * TILE : (i + 1) * TILE].astype(F32)
                for d in range(5):
                    if d in (0, 4):
                        line = jnp.sum(sums[d], axis=0, keepdims=True)
                        diag[h, d : d + 1, :] = jnp.concatenate([line, jnp.zeros_like(line)], axis=1)
                    else:
                        turned = lax.dot_general(
                            flip, sums[d], (((1,), (0,)), ((), ())),
                            precision=lax.Precision.HIGHEST, preferred_element_type=F32,
                        )
                        wider = jnp.concatenate([turned, jnp.zeros_like(turned)], axis=1)
                        rolled = pltpu.roll(wider, 1, 1, stride=1, stride_axis=0)
                        diag[h, d : d + 1, :] = jnp.sum(rolled, axis=0, keepdims=True)
            dk[:, cols] = kacc[...].astype(BF)
            dv[:, cols] = vacc[...].astype(BF)
            return carry

        lax.fori_loop(0, HEADS // 2, pair, 0)

        for core, (one, two) in enumerate(((dk, dv), (dq, da))):

            @pl.when(meta[1] == core)
            def _():
                start_copy(one, other.at[0], sems.at[1])
                start_copy(two, other.at[1], sems.at[1])

        for src, dst in ((dq, dq_out), (dk, dk_out), (dv, dv_out)):
            start_copy(src, dst, sems.at[2])
        drain(dk, sems.at[1])
        drain(dv, sems.at[1])
        for ref in (dq, dk, dv):
            drain(ref, sems.at[2])

    rows = (ROW_LEN, D)
    return call(
        body, "enc_attention_back", [meta, da, q, k, v, lse, segr, segc, windows, *arrays],
        [SM, VM, ANY, ANY, ANY] + [VM] * 4 + [ANY] * n,
        [(rows, BF), (rows, BF), (rows, BF), ((HEADS, 5, 2 * TILE), F32), ((2,) + rows, BF)], [ANY, ANY, ANY, VM, ANY],
        [pltpu.VMEM((D, D), BF), pltpu.VMEM(rows, BF), pltpu.VMEM((HEADS, 5, TILE, TILE), F32),
         pltpu.VMEM((5, TILE, TILE), F32), pltpu.VMEM((ROW_LEN, TILE), F32), pltpu.VMEM((ROW_LEN, TILE), F32)]
        + [pltpu.VMEM(rows, BF)] * 6 + [pltpu.SemaphoreType.DMA((4,))],
        us=25,
    )


def enc_square_grads(meta, n1, n1_got, c, c_got, dq, dk, dv, da, got):
    def body(meta, n1, n1_got, c, c_got, dq, dk, dv, da, got, keep_a, send_a, keep_b, send_b, buf, sems):
        for core, (one, left, left_got, two) in enumerate(((dq, c, c_got, da), (dk, n1, n1_got, dv))):

            @pl.when(meta[1] == core)
            def _():
                buf[0] = (tn(n1[...], one[...]) + tn(n1_got[...], got[0])).astype(BF)
                for g in range(GROUPS):
                    start_store(meta, buf.at[0, pl.ds(g * GROUP, GROUP)], g, 0, keep_a, send_a, sems.at[0])
                buf[1] = (tn(left[...], two[...]) + tn(left_got[...], got[1])).astype(BF)
                for g in range(GROUPS):
                    start_store(meta, buf.at[1, pl.ds(g * GROUP, GROUP)], g, 1, keep_b, send_b, sems.at[1])

        drain(buf.at[0], sems.at[0])
        drain(buf.at[1], sems.at[1])

    return call(
        body, "enc_square_grads", [meta, n1, n1_got, c, c_got, dq, dk, dv, da, got], [SM] + [VM] * 9,
        [(PART, BF)] * 4, [ANY] * 4,
        [pltpu.VMEM((2, D, D), BF), pltpu.SemaphoreType.DMA((2,))],
        us=1,
    )


def enc_input_grad(meta, dq, dk, dv, x, dh1, gains, a_sets, b_sets):
    a_arrays, a_plan = plan_of(a_sets)
    b_arrays, b_plan = plan_of(b_sets)
    n = len(a_arrays)

    def body(meta, dq, dk, dv, x, dh1, gains, *rest):
        a_parts, b_parts, rest = rest[:n], rest[n : 2 * n], rest[2 * n :]
        keep, send, dgain, w, grads, xs, dh1s, sems = rest
        start_fetch(meta, a_parts, a_plan, [(0, GROUP, lambda core, g: core * D + GROUP * g, lambda core, g: core)], w, sems)
        start_fetch(meta, b_parts, b_plan, [(0, GROUP, lambda core, g: 2 * D + GROUP * g, lambda core, g: 2)], w, sems, only=1)
        for k, ref in enumerate((dq, dk, dv)):
            start_copy(ref, grads.at[k], sems.at[3 + k])
        start_copy(x, xs, sems.at[6])
        start_copy(dh1, dh1s, sems.at[7])
        total = None
        for k in range(3):
            drain(w.at[pl.ds(k * D, D)], sems.at[k])
            drain(grads.at[k], sems.at[3 + k])
            part = nt(grads[k], w[k * D : (k + 1) * D, :])
            total = part if total is None else total + part
        drain(xs, sems.at[6])
        drain(dh1s, sems.at[7])
        dx, dg = rms_back(xs[...].astype(F32), gains[0:1, :], total)
        out = (dh1s[...] + dx).astype(BF)
        dgain[...] = dg
        half = D // 2

        @pl.when(meta[1] == 0)
        def _():
            keep[...] = out[:, :half]
            send[...] = out[:, half:]

        @pl.when(meta[1] != 0)
        def _():
            keep[...] = out[:, half:]
            send[...] = out[:, :half]

    return call(
        body, "enc_input_grad", [meta, dq, dk, dv, x, dh1, gains, *a_arrays, *b_arrays],
        [SM] + [ANY] * 5 + [VM] + [ANY] * (2 * n),
        [((ROW_LEN, D // 2), BF), ((ROW_LEN, D // 2), BF), ((1, D), F32)], [VM] * 3,
        [pltpu.VMEM((3 * D, D), BF), pltpu.VMEM((3, ROW_LEN, D), BF), pltpu.VMEM((ROW_LEN, D), BF),
         pltpu.VMEM((ROW_LEN, D), F32), pltpu.SemaphoreType.DMA((8,))],
        us=1,
    )


def spread_heads(value):
    return jnp.concatenate([masked(value, head_lanes(h)) for h in range(HEADS)], axis=0)


def join_heads(value):
    total = jnp.zeros((8, D), F32)
    for h in range(HEADS):
        total = total + masked(value[8 * h : 8 * h + 8, :], head_lanes(h))
    return total


def own_rows(meta):
    row = lax.broadcasted_iota(jnp.int32, (8, 1), 0)
    return (row >= 4 * meta[1]) & (row < 4 * meta[1] + 4)


def start_self(meta, own, got, dst, sem):
    half = D // 2
    pltpu.make_async_copy(own, dst.at[pl.ds(pl.multiple_of(meta[1] * half, 16), half)], sem).start()
    pltpu.make_async_copy(got, dst.at[pl.ds(pl.multiple_of((1 - meta[1]) * half, 16), half)], sem).start()


def dec_before(meta, z, d_out, gains, self_own, self_got, sets):
    arrays, plan = plan_of(sets)
    n = len(arrays)

    def body(meta, z, d_out, gains, self_own, self_got, *rest):
        parts, rest = rest[:n], rest[n:]
        m1, sv, z1, m2, qc, qk, gm, w_self, w, sems = rest
        start_self(meta, self_own, self_got, w_self, sems.at[0])
        start_fetch(meta, parts, plan, [(0, GROUP, lambda core, g: core * D + GROUP * g)], w, sems.at[1])
        zf = z[...].astype(F32)
        gm[...] = jnp.where(own_rows(meta), d_out[...].astype(F32), 0.0).astype(BF)
        m1v = rms(zf, gains[2:3, :]).astype(BF)
        drain(w_self, sems.at[0])
        drain(w, sems.at[1])
        svv = nn(m1v, w_self[:, :D]).astype(BF)
        z1v = zf + nn(svv, w_self[:, D:])
        m2v = rms(z1v, gains[0:1, :]).astype(BF)
        qcv = nn(m2v, w[0:D, :]).astype(BF)
        qk[...] = nt(spread_heads(qcv), w[D:, :]).astype(BF)
        m1[...], sv[...], z1[...], m2[...], qc[...] = m1v, svv, z1v, m2v, qcv

    rows = (8, D)
    return call(
        body, "dec_before", [meta, z, d_out, gains, self_own, self_got, *arrays],
        [SM, VM, VM, VM, ANY, ANY] + [ANY] * n,
        [(rows, BF), (rows, BF), (rows, F32), (rows, BF), (rows, BF), ((8 * HEADS, D), BF), (rows, BF)], [VM] * 7,
        [pltpu.VMEM((D, 2 * D), BF), pltpu.VMEM((2 * D, D), BF), pltpu.SemaphoreType.DMA((2,))],
        us=6,
    )


def dec_core(meta, e, segr, qk, qc, z1, g, gw, gains, sets):
    arrays, plan = plan_of(sets)
    n = len(arrays)

    def body(meta, e, segr, qk, qc, z1, g, gw, gains, *rest):
        parts, rest = rest[:n], rest[n:]
        de, cc, z2, m3, fc, duc, da2, dz2, dcc, edt, ebar, dgain, de_other, pairs_other, w, w_in, sems = rest
        start_fetch(meta, parts, plan, [(GROUP, GROUP, lambda core, g: core * D + GROUP * g)], w, sems.at[0])
        start_fetch(meta, parts, plan, in_items(2 * GROUP), w_in, sems.at[pl.ds(1, 4)])
        pairs = lax.broadcasted_iota(jnp.int32, (8 * HEADS, 1), 0)
        owner = segr[...] == jnp.bitwise_and(pairs, 7) - 4 * meta[1]
        t = jnp.where(owner, nt(qk[...], e[...]), MASKED)
        ex = jnp.where(owner, jnp.exp(t - jnp.max(t, axis=-1, keepdims=True)), 0.0)
        tot = jnp.sum(ex, axis=-1, keepdims=True)
        prob = ex * (1.0 / jnp.where(tot > 0.0, tot, 1.0))
        pc = prob.astype(BF)
        ebv = nn(pc, e[...]).astype(BF)
        ebar[...] = ebv
        drain(w, sems.at[0])
        ccv = join_heads(nn(ebv, w[D:, :])).astype(BF)
        z2v = z1[...] + nn(ccv, w[0:D, :])
        m3v = rms(z2v, gains[1:2, :]).astype(BF)
        dm3 = jnp.zeros((8, D), F32)
        own = own_rows(meta)
        for b in (0, 2, 1, 3):
            cols = slice(b * D, (b + 1) * D)
            drain(w_in.at[cols], sems.at[1 + b])
            value, slope = gelu_both(nn(m3v, w_in[cols, :]))
            fc[:, cols] = jnp.where(own, value, 0.0).astype(BF)
            ducv = jnp.where(own, slope * gw[:, cols].astype(F32), 0.0).astype(BF)
            duc[:, cols] = ducv
            dm3 = dm3 + nt(ducv, w_in[cols, :])
        back, dg = rms_back(z2v, gains[1:2, :], dm3)
        dz2v = g[...].astype(F32) + back
        da2v = dz2v.astype(BF)
        dccv = nt(da2v, w[0:D, :]).astype(BF)
        dvw = nt(spread_heads(dccv), w[D:, :]).astype(BF)
        dprob = nt(dvw, e[...])
        dt = (prob * (dprob - jnp.sum(prob * dprob, axis=-1, keepdims=True))).astype(BF)
        de[...] = tn(jnp.concatenate([pc, dt], axis=0), jnp.concatenate([dvw, qk[...]], axis=0)).astype(BF)
        edt[...] = nn(dt, e[...]).astype(BF)
        cc[...], m3[...], da2[...], dz2[...], dcc[...], dgain[...] = ccv, m3v, da2v, dz2v, dccv, dg
        z2[...] = jnp.where(own, z2v, 0.0)
        half = D // 2
        pairs_other[8 * HEADS + 8 :, :] = jnp.zeros((8, D), BF)

        @pl.when(meta[1] == 0)
        def _():
            de_other[...] = de[:, half:]
            pairs_other[: 8 * HEADS, :] = ebv
            pairs_other[8 * HEADS : 8 * HEADS + 8, :] = dccv

        @pl.when(meta[1] != 0)
        def _():
            de_other[...] = de[:, :half]
            pairs_other[: 8 * HEADS, :] = edt[...]
            pairs_other[8 * HEADS : 8 * HEADS + 8, :] = qc[...]

    rows, spread = (8, D), (8 * HEADS, D)
    return call(
        body, "dec_core", [meta, e, segr, qk, qc, z1, g, gw, gains, *arrays],
        [SM] + [VM] * 8 + [ANY] * n,
        [((ROW_LEN, D), BF), (rows, BF), (rows, F32), (rows, BF), ((8, FF), BF), ((8, FF), BF), (rows, BF),
         (rows, F32), (rows, BF), (spread, BF), (spread, BF), ((1, D), F32),
         ((ROW_LEN, D // 2), BF), ((8 * HEADS + 16, D), BF)], [VM] * 14,
        [pltpu.VMEM((2 * D, D), BF), pltpu.VMEM((FF, D), BF), pltpu.SemaphoreType.DMA((5,))],
        us=10,
    )


def dec_after(meta, z, z1, dz2, qc, dcc, edt, ebar, got, gains, acts, duc, fc, self_own, self_got, sets):
    arrays, plan = plan_of(sets)
    n = len(arrays)

    def body(meta, z, z1, dz2, qc, dcc, edt, ebar, got, gains, *rest):
        acts, rest = rest[:8], rest[8:]
        self_own, self_got, parts, rest = rest[0], rest[1], rest[2 : 2 + n], rest[2 + n :]
        acts_keep, acts_send, dec_grad, dg_attn, dg_self, keep, send, w_self, w, buf, sems = rest
        start_fetch(meta, parts, plan, [(0, GROUP, lambda core, g: core * D + GROUP * g)], w, sems.at[1])
        start_self(meta, self_own, self_got, w_self, sems.at[0])
        zero = meta[1] == 0
        left = jnp.concatenate([jnp.where(zero, edt[...], ebar[...]), got[: 8 * HEADS, :]], axis=0)
        right = jnp.where(zero, qc[...], dcc[...])
        right = jnp.concatenate([spread_heads(right), spread_heads(got[8 * HEADS : 8 * HEADS + 8, :])], axis=0)
        buf[...] = tn(left, right).astype(BF)
        for grp in range(GROUPS):
            start_store(meta, buf.at[pl.ds(grp * GROUP, GROUP)], grp, 0, keep, send, sems.at[3], pl.ds(GROUP, GROUP))
        drain(w, sems.at[1])
        dqv = join_heads(nn(edt[...], w[D:, :])).astype(BF)
        back, dg = rms_back(z1[...], gains[0:1, :], nt(dqv, w[0:D, :]))
        dz1 = dz2[...] + back
        ds1v = dz1.astype(BF)
        drain(w_self, sems.at[0])
        dsvv = nt(ds1v, w_self[:, D:]).astype(BF)
        back0, dg0 = rms_back(z[...].astype(F32), gains[2:3, :], nt(dsvv, w_self[:, :D]))
        own = own_rows(meta)
        dec_grad[...] = jnp.where(own, dz1 + back0, 0.0).astype(BF)
        dg_attn[...], dg_self[...] = dg, dg0
        row = jnp.concatenate([ref[...] for ref in acts[:6]] + [dqv, ds1v, dsvv] + [ref[...] for ref in acts[6:]], axis=1)
        half = row.shape[1] // 2
        for core, (one, two) in enumerate(((acts_keep, acts_send), (acts_send, acts_keep))):

            @pl.when(meta[1] == core)
            def _():
                one[...] = row[:, :half]
                two[...] = row[:, half:]

        drain(buf, sems.at[3])

    rows = (8, D)
    return call(
        body, "dec_after",
        [meta, z, z1, dz2, qc, dcc, edt, ebar, got, gains, *acts, duc, fc, self_own, self_got, *arrays],
        [SM] + [VM] * 17 + [ANY] * (2 + n),
        [((8, (9 * D + 2 * FF) // 2), BF)] * 2 + [(rows, BF)] + [((1, D), F32)] * 2 + [(WIDE_PART, BF)] * 2, [VM] * 5 + [ANY] * 2,
        [pltpu.VMEM((D, 2 * D), BF), pltpu.VMEM((2 * D, D), BF), pltpu.VMEM((D, D), BF),
         pltpu.SemaphoreType.DMA((4,))],
        us=6,
    )


def dec_weight_grads(place, own, got, g_all, w_back, rows, self_rows):
    def body(place, own, got, *rest):
        for core, (left, right) in enumerate(((own, got), (got, own))):
            pl.when(place[1] == core)(functools.partial(halves, place, left, right, *rest))

    def halves(place, left, right, g_all, w_back, dec_q, dec_o, dec_i, dec_b, self_v, self_o, y):
        half = left.shape[1]
        chip, core = place[0], place[1]
        chips = D // rows

        def cut(at, width):
            parts = []
            while width:
                ref, first = (left, at) if at < half else (right, at - half)
                count = min(width, half - first)
                parts.append(ref[:, first : first + count])
                at, width = at + count, width - count
            return parts[0] if len(parts) == 1 else jnp.concatenate(parts, axis=1)

        def picked(at, first, count, width=D):
            row = lax.broadcasted_iota(jnp.int32, (count, width), 0) + first
            col = lax.broadcasted_iota(jnp.int32, (count, width), 1)
            return nt((row == col).astype(F32).astype(BF), cut(at * D, width)).astype(BF)

        first, first_self = chip * rows, (core * chips + chip) * self_rows
        m1, sv, m2, cc, m3, da2, dqc, ds1, dsv, duc, fc = list(range(10)) + [13]
        dec_q[...] = nn(picked(m2, first, rows), cut(dqc * D, D))
        dec_o[...] = nn(picked(cc, first, rows), cut(da2 * D, D))
        dec_i[...] = nn(picked(m3, first, rows), cut(duc * D, FF))
        self_v[...] = nn(picked(m1, first_self, self_rows), cut(dsv * D, D))
        self_o[...] = nn(picked(sv, first_self, self_rows), cut(ds1 * D, D))
        hidden = picked(fc, 4 * first, 4 * rows, FF)
        dec_b[...] = nn(hidden, g_all[...])
        y[...] = tn(hidden, w_back[...]).astype(BF)

    return call(
        body, "dec_weight_grads", [place, own, got, g_all, w_back], [SM, VM, VM, VM, VM],
        [((rows, D), F32), ((rows, D), F32), ((rows, FF), F32), ((4 * rows, D), F32), ((self_rows, D), F32),
         ((self_rows, D), F32), (g_all.shape, BF)], [VM] * 7,
        [], us=0.2,
    )


def prepare(meta, w_query, w_key, w_value, w_out, w_in, w_back):
    def body(meta, query, key, value, out, w_in, w_back, kept, sent):
        for core, (one, two) in enumerate(((kept, sent), (sent, kept))):

            @pl.when(meta[1] == core)
            def _():
                for half, (dst, squares) in enumerate(((one, (query, out)), (two, (key, value)))):
                    for k in range(2):
                        at = 2 * half + k
                        dst[k * GROUP : (k + 1) * GROUP, :] = squares[k][...]
                        dst[(2 + k) * GROUP : (3 + k) * GROUP, :] = w_in[:, at * D : (at + 1) * D]
                        dst[(4 + k) * GROUP : (5 + k) * GROUP, :] = w_back[at * GROUP : (at + 1) * GROUP, :]

    half = ((6 * GROUP, D), BF)
    return call(
        body, "prepare", [meta, w_query, w_key, w_value, w_out, w_in, w_back], [SM] + [VM] * 6, [half] * 2, [VM] * 2, [], us=2
    )


def per_device(
    enc_in, dec_in, segment, d_out, attn_gain, w_query, w_key, w_value, w_out, ffn_gain, w_in, w_back,
    self_gain, self_value, self_out, rel_table,
):
    core, chip = lax.axis_index("section"), lax.axis_index("dp")
    chips = lax.axis_size("dp")
    rows = w_query.shape[1]
    first = core == 0
    pre = low_bits(rows)
    meta = jnp.stack([chip >> pre, core]).astype(jnp.int32)
    self_rows = self_value.shape[0]
    at_self = (core * chips + chip) * self_rows

    kept, sent = prepare(
        meta, *[filled(w[0], pre, chip, 0) for w in (w_query, w_key, w_value, w_out, w_in, w_back)]
    )
    got = across(sent)
    enc_piece, dec_piece = jnp.where(first, kept, got), jnp.where(first, got, kept)
    count = 4 * GROUP

    shared = lax.all_gather(jnp.concatenate([dec_piece[:count], self_value, self_out, enc_piece[5 * GROUP :]]), "dp")

    gains = jnp.zeros((8, D), BF)
    gains = lax.dynamic_update_slice(gains, jnp.concatenate([attn_gain, ffn_gain]), (0, chip * rows))
    gains = lax.dynamic_update_slice(gains, self_gain[None], (2, at_self))
    little = Chain([jnp.concatenate([gains, d_out])[None]], [0], 0)
    for bit in range(pre):
        little.step(bit)

    def chain(*parts):
        return Chain([jnp.concatenate(parts)[None]], [0], pre)

    cut = 3 * GROUP + 2 * GROUP // 3
    sq = chain(enc_piece[: 2 * GROUP])
    wide = chain(enc_piece[2 * GROUP : cut], enc_piece[4 * GROUP : 5 * GROUP], enc_piece[cut : 4 * GROUP])

    windows = jnp.einsum(
        "adtb,bh->hadt", window_onehots(), rel_table, precision=lax.Precision.HIGHEST
    ).reshape(HEADS, 6, 2 * TILE)
    x = lax.dynamic_index_in_dim(enc_in, core, 0, False)
    seg = lax.dynamic_index_in_dim(segment, core, 0, False)
    segr, segc = seg[None, :], seg[:, None]

    sq.step(Z1), little.step(X + pre)
    phase(sq, little)
    sq.step(Z0), little.step(Y + pre)
    phase(sq, wide, little)
    sa, sb = sq.split(GROUP)
    sa.step(X), sb.step(Y), wide.step(Z1), little.step(Z0 + pre)
    phase(sa, sb, wide, little)
    sa.step(Y), sb.step(X), wide.step(Z0), little.step(Z1 + pre)
    sa_got, sb_got = [across(sa.parts[0])], [across(sb.parts[0])]
    x = phase(sa, sb, wide, little, x)
    wa, wb = wide.split(cut - 2 * GROUP)
    wa.step(X), wb.step(Y)
    sa_got += [across(sa.parts[1])]
    sb_got += [across(sb.parts[1])]

    order = np.argsort(np.array(little.ids))
    places = jnp.take(jnp.asarray(order, jnp.int32), jnp.bitwise_xor(jnp.arange(chips), chip))
    little = jnp.concatenate(little.parts)
    gains = jnp.sum(little[:, :8].astype(F32), axis=0)
    gains_got = across(gains)
    gains0, gains1 = jnp.where(first, gains, gains_got), jnp.where(first, gains_got, gains)
    gains1 = jnp.where(jnp.arange(8)[:, None] == 2, gains0 + gains1, gains1)
    n1, q, k, v, c, h1, n2, lse = enc_attention(meta, x, gains0, segr, segc, windows, sa.sets(sa_got), sb.sets(sb_got))
    h1, little = phase(wa, wb, h1, little)
    wa.step(Y), wb.step(X)
    wa_got, wb_got = [across(wa.parts[0])], [across(wb.parts[0])]

    g_all = jnp.take(little[:, 8:], places, axis=0).reshape(8 * chips, D)
    lanes = -(-4 * rows // TILE) * TILE
    gw = jnp.pad(nt(g_all, w_back[0]).astype(BF), ((0, 0), (0, lanes - 4 * rows))).reshape(chips, 8, lanes)
    gw = lax.all_to_all(gw, "dp", 0, 0)
    h1, shared, gw = phase(wa, wb, h1, shared, gw)
    wa_got += [across(wa.parts[1])]
    wb_got += [across(wb.parts[1])]
    back_at = count + 2 * self_rows
    shared_back = shared[:: 2**pre, back_at:]
    back_got = across(shared_back)

    def self_part(index):
        at = count + index * self_rows
        return shared[:, at : at + self_rows].reshape(D // 2, D)

    self_own = jnp.concatenate([self_part(0), self_part(1)], axis=1)
    gw = gw[:, :, : 4 * rows].transpose(1, 0, 2).reshape(8, FF)
    gw_got = across(gw)
    wa_got, wb_got, back_got, h1, n1, c, n2, shared, self_own, gw, gw_got = phase(
        wa_got, wb_got, back_got, h1, n1, c, n2, shared, self_own, gw, gw_got
    )
    gw = jnp.where(first, gw_got, gw)
    self_got, shared_got = across(self_own), across(shared)
    n1_got, c_got, n2_got = across(n1), across(c), across(n2)
    w_in_from = in_sources(wa.sets(wa_got), wb.sets(wb_got))
    w_back_from = back_sources(wb.sets(wb_got), shared_back if pre else shared, 0 if pre else back_at, back_got)
    f, slope, e = enc_ffn(meta, h1, n2, w_in_from, w_back_from)
    e, shared_got, n1_got, c_got, n2_got, self_got = phase(e, shared_got, n1_got, c_got, n2_got, self_got)
    dec_sets = [(v[:: 2**pre] if pre else v, None, other) for other, v in enumerate((shared, shared_got))]
    m1, sv, z1, m2, qc, qk, gm = dec_before(meta, dec_in, d_out, gains1, self_own, self_got, dec_sets)
    f, qk = phase(f, qk)
    f_got = across(f)
    de, cc, z2, m3, fc, duc, da2, dz2, dcc, edt, ebar, dg_ffn1, de_other, pairs_other = dec_core(
        meta, e, segr, qk, qc, z1, gm, gw, gains1, dec_sets
    )

    def two(parts):
        return Sum(parts[0], parts[1], pre), Sum(parts[2], parts[3], pre)

    de_got, pairs_got = across(de_other), across(pairs_other)
    du, du_other = enc_hidden_grad(meta, de, slope, w_back_from)
    de_got, pairs_got, du, du_other, edt = phase(de_got, pairs_got, du, du_other, edt)
    du_got = across(du_other)
    acts, acts_send, dec_grad, dg_attn1, dg_self, k_keep, k_send = dec_after(
        meta, dec_in, z1, dz2, qc, dcc, edt, ebar, pairs_got, gains1, [m1, sv, m2, cc, m3, da2], duc, fc,
        self_own, self_got, dec_sets,
    )
    acts, acts_send, f, f_got = phase(acts, acts_send, f, f_got)
    acts_got, width = across(acts_send), acts.shape[1]
    own = (jnp.arange(8)[:, None] // 4) == core
    acts = jnp.where(own, acts, acts_got)
    acts = lax.all_gather(acts, "dp").reshape(8 * chips, width)
    back_a, back_b = two(enc_w_back_grad(meta, de, de_got, f, f_got))
    n2, du_got = phase(back_a, back_b, n2, du_got)
    back_a.step(Y), back_b.step(X)
    in_a, in_b = two(enc_w_in_grad(meta, du, du_got, n2, n2_got, k_keep, k_send))
    h1 = phase(in_a, in_b, h1)
    in_a.step(Y), in_b.step(X)
    dh1, da, dg_ffn0 = enc_ffn_back(meta, du, h1, de, gains0, w_in_from)
    da = phase(back_a, back_b, da)
    back_a.step(X), back_b.step(Y)
    dq, dk, dv, diag, other = enc_attention_back(meta, da, q, k, v, lse, segr, segc, windows, sb.sets(sb_got))
    dq, other = phase(back_a, back_b, in_a, in_b, dq, other)
    got = across(other)
    in_a.step(X), in_b.step(Y)
    backs = merged([back_a, back_b])
    backs.step(Z0)
    keep, send, dg_attn0 = enc_input_grad(meta, dq, dk, dv, x, dh1, gains0, sa.sets(sa_got), sb.sets(sb_got))
    got, dq, dg_attn0 = phase(backs, got, dq, dg_attn0)
    backs.step(Z1)
    table = jnp.einsum("hdt,dtb->bh", diag, diagonal_onehots(), precision=lax.Precision.HIGHEST)
    little = jnp.concatenate([
        dg_attn0, dg_ffn0, dg_attn1, dg_ffn1, dg_self,
        jnp.pad(table.reshape(1, -1), ((0, 0), (0, D - BUCKETS * HEADS))), jnp.zeros((2, D), F32),
    ])
    little = little + across(little)
    for bit in range(pre):
        little = little + along(little, bit)
    other = along(little, Z0 + pre)
    square_a, square_b = two(enc_square_grads(meta, n1, n1_got, c, c_got, dq, dk, dv, da, got))
    acts, other = phase(square_a, square_b, in_a, in_b, acts, other)
    little = little + other
    square_a.step(Y), square_b.step(X)
    theirs = across(acts)
    other = along(little, Z1 + pre)
    ins = merged([in_a, in_b])
    ins.step(Z0)

    dec_q, dec_o, dec_i, dec_b, g_self_value, g_self_out, y = dec_weight_grads(
        jnp.stack([chip, core]), acts, theirs, g_all, w_back[0], rows, self_rows
    )
    other, y = phase(square_a, square_b, ins, backs, other, y)
    little = little + other
    square_a.step(X), square_b.step(Y), ins.step(Z1)
    other = along(little, X + pre)
    other, y, send, z2, dec_grad = phase(square_a, square_b, other, y, send, z2, dec_grad)
    little = little + other
    squares = merged([square_a, square_b])
    squares.step(Z0)
    other = along(little, Y + pre)
    z2 = z2 + across(z2)
    y = lax.all_to_all(y.reshape(chips, 8, D), "dp", 0, 0)
    other, y = phase(squares, ins, other, y)
    little = little + other
    squares.step(Z1)
    backs_sum, ins_sum, square_sum = backs.total(), ins.total(), squares.total()
    dec_out = (z2 + jnp.sum(y.astype(F32), axis=0)).astype(BF)
    dec_out = jnp.where(first, across(dec_out), dec_out)
    mine = chip * rows

    g_rel_table = little[5, : BUCKETS * HEADS].reshape(BUCKETS, HEADS)

    def cut(index, at, count):
        return lax.dynamic_slice_in_dim(little[index], at, count, 0)

    g_attn_gain = cut(jnp.where(first, 0, 2), mine, rows)[None]
    g_ffn_gain = cut(jnp.where(first, 1, 3), mine, rows)[None]
    g_self_gain = cut(4, at_self, self_rows)

    backs_got, ins_got, square_got = [across(v.astype(BF)).astype(F32) for v in (backs_sum, ins_sum, square_sum)]

    def group(value, index):
        return value[index * GROUP : (index + 1) * GROUP]

    def placed(enc_value, dec_value):
        return jnp.where(first, narrowed(enc_value, pre, chip), dec_value)[None]

    g_w_query = placed(group(square_sum, 0), dec_q)
    g_w_out = placed(group(square_sum, 1), dec_o)
    g_w_key = narrowed(jnp.where(first, group(square_got, 0), group(ins_got, 1)), pre, chip)[None]
    g_w_value = narrowed(jnp.where(first, group(square_got, 1), group(ins_sum, 1)), pre, chip)[None]
    g_w_in = placed(
        jnp.concatenate([group(ins_sum, 0), group(ins_sum, 2), group(ins_got, 0), group(ins_got, 2)], axis=1), dec_i
    )
    half = D // 2
    tall = [
        jnp.concatenate([group(v, i)[:, j * half : (j + 1) * half] for i in range(2) for j in range(2)])
        for v in (backs_sum, backs_got)
    ]
    g_w_back = placed(jnp.concatenate(tall, axis=1), dec_b)

    other_half = across(send)
    enc_in_grad = jnp.where(first, jnp.stack([keep, other_half]), jnp.stack([other_half, keep]))
    dec_grad = dec_grad + across(dec_grad)
    half = D // 2
    dec_out = jnp.where(first, dec_out[:, :half], dec_out[:, half:])
    dec_in_grad = jnp.where(first, dec_grad[:, :half], dec_grad[:, half:])
    return (
        dec_out, enc_in_grad, dec_in_grad, g_attn_gain, g_w_query, g_w_key, g_w_value, g_w_out, g_ffn_gain,
        g_w_in, g_w_back, g_self_gain, g_self_value, g_self_out, g_rel_table,
    )


def solution(mesh):
    return jax.shard_map(
        per_device,
        mesh=mesh,
        in_specs=(
            P("dp", None, None),
            P("dp", None),
            P("dp", None),
            P("dp", None),
            P("section", "dp"),
            P("section", "dp", None),
            P("section", "dp", None),
            P("section", "dp", None),
            P("section", "dp", None),
            P("section", "dp"),
            P("section", "dp", None),
            P("section", "dp", None),
            P(("section", "dp")),
            P(("section", "dp"), None),
            P(("section", "dp"), None),
            P(),
        ),
        out_specs=(
            P("dp", "section"),
            P("dp", None, "section"),
            P("dp", "section"),
            P("section", "dp"),
            P("section", "dp", None),
            P("section", "dp", None),
            P("section", "dp", None),
            P("section", "dp", None),
            P("section", "dp"),
            P("section", "dp", None),
            P("section", "dp", None),
            P(("section", "dp")),
            P(("section", "dp"), None),
            P(("section", "dp"), None),
            P(),
        ),
        check_vma=False,
    )
```

```python
import functools

import jax
import jax.numpy as jnp
import numpy as np
from jax import lax
from jax.experimental import pallas as pl
from jax.experimental.pallas import tpu as pltpu
from jax.sharding import PartitionSpec as P

D = 768
HEADS = 12
HEAD_DIM = 64
FF = 3072
BUCKETS = 32
MAX_DIST = 128
ROW_LEN = 512
SEGS = 4
GROUP = 48
GROUPS = D // GROUP
X, Y, Z0, Z1 = 0, 1, 2, 3
TILE = 128
EPS = 1e-06
MASKED = -1000000000.0
BF = jnp.bfloat16
F32 = jnp.float32
SPEED = 0.25
VMEM_LIMIT = 58 * 1024 * 1024


def bucket_of(offset):
    half, exact = BUCKETS // 2, BUCKETS // 4
    exponent, growth = half - exact, MAX_DIST // exact
    distance = abs(offset)
    if distance < exact:
        level = distance
    else:
        k = 0
        while k < exponent and exact**exponent * growth ** (k + 1) <= distance**exponent:
            k += 1
        level = min(exact + k, half - 1)
    return (half if offset > 0 else 0) + level


def window_onehots():
    table = np.zeros((2, 3, 2 * TILE, BUCKETS), np.float32)
    for d in range(3):
        for t in range(2 * TILE):
            table[0, d, t, bucket_of(TILE * (d - 1) - TILE + t)] = 1.0
            table[1, d, t, bucket_of(TILE * (d - 1) + TILE - t)] = 1.0
    return table


def diagonal_onehots():
    table = np.zeros((5, 2 * TILE, BUCKETS), np.float32)
    table[1:4] = window_onehots()[1]
    table[0, :, bucket_of(-TILE - 1)] = 1.0
    table[4, :, bucket_of(TILE + 1)] = 1.0
    return table


def across(value):
    return lax.ppermute(value, "section", [(0, 1), (1, 0)])


def along(value, bit):
    count = lax.axis_size("dp")
    return lax.ppermute(value, "dp", [(i, i ^ (1 << bit)) for i in range(count)])


def bit_of(index, bit):
    return lax.rem(lax.div(index, 1 << bit), 2)


def low_bits(rows):
    count = 0
    while rows < GROUP:
        rows *= 2
        count += 1
    return count


def filled(piece, pre, chip, axis):
    for bit in range(pre):
        other = along(piece, bit)
        upper = bit_of(chip, bit) == 1
        first = jnp.where(upper, other, piece)
        second = jnp.where(upper, piece, other)
        piece = jnp.concatenate([first, second], axis=axis)
    return piece


def narrowed(total, pre, chip):
    for bit in reversed(range(pre)):
        length = total.shape[0] // 2
        upper = bit_of(chip, bit)
        kept = lax.dynamic_slice_in_dim(total, upper * length, length, 0)
        sent = lax.dynamic_slice_in_dim(total, (1 - upper) * length, length, 0)
        total = added(kept, along(sent.astype(BF), bit), F32)
    return total


def phase(*things):
    tree = [thing.arrays() if isinstance(thing, (Chain, Sum)) else thing for thing in things]
    out = []
    for thing, value in zip(things, lax.optimization_barrier(tree)):
        if isinstance(thing, (Chain, Sum)):
            thing.replace(value)
        else:
            out.append(value)
    return out[0] if len(out) == 1 else out


class Chain:
    def __init__(self, parts, ids, pre):
        self.parts, self.ids, self.pre = parts, ids, pre

    def arrays(self):
        return list(self.parts)

    def replace(self, values):
        self.parts = values

    def split(self, at):
        cut = [[part[:, :at] for part in self.parts], [part[:, at:] for part in self.parts]]
        return [Chain(parts, self.ids, self.pre) for parts in cut]

    def step(self, bit):
        held = self.parts[0] if len(self.parts) == 1 else jnp.concatenate(self.parts, axis=0)
        self.parts = [held, along(held, bit + self.pre)]
        self.old_ids = self.ids
        self.ids = self.ids + [g ^ (1 << bit) for g in self.ids]

    def sets(self, others):
        first, last = self.old_ids, self.ids[len(self.old_ids) :]
        return [(self.parts[0], first, 0), (self.parts[1], last, 0), (others[0], first, 1), (others[1], last, 1)]


def added(left, right, kind=BF):
    return (left.astype(F32) + right.astype(F32)).astype(kind)


class Sum:
    def __init__(self, keep, send, pre):
        self.mine, self.other, self.pre, self.fresh = keep, send, pre, True

    def arrays(self):
        return [self.mine, self.other]

    def replace(self, values):
        self.mine, self.other = values

    def step(self, bit):
        if self.fresh:
            send, self.fresh = self.other, False
        else:
            half = self.mine.shape[0] // 2
            send = added(self.mine[half:], self.other[half:])
            self.mine = added(self.mine[:half], self.other[:half])
        self.other = along(send, bit + self.pre)

    def total(self):
        return added(self.mine[0], self.other[0], F32)


def merged(sums):
    one = Sum(
        jnp.concatenate([part.mine for part in sums], axis=1),
        jnp.concatenate([part.other for part in sums], axis=1),
        sums[0].pre,
    )
    one.fresh = False
    return one


def nn(a, b):
    return lax.dot_general(a, b, (((1,), (0,)), ((), ())), preferred_element_type=F32)


def nt(a, b):
    return lax.dot_general(a, b, (((1,), (1,)), ((), ())), preferred_element_type=F32)


def tn(a, b):
    return lax.dot_general(a, b, (((0,), (0,)), ((), ())), preferred_element_type=F32)


def rms(v, gain):
    return v * lax.rsqrt(jnp.mean(v * v, axis=-1, keepdims=True) + EPS) * gain


def rms_back(v, gain, dy):
    r = lax.rsqrt(jnp.mean(v * v, axis=-1, keepdims=True) + EPS)
    dgain = jnp.sum(dy * v * r, axis=0, keepdims=True)
    dyg = dy * gain
    dv = r * dyg - v * (r * r * r) * jnp.mean(v * dyg, axis=-1, keepdims=True)
    return dv, dgain


def gelu_both(u):
    c = 0.7978845608028654
    square = u * u
    half = 0.5 + 0.5 * jnp.tanh(u * (c + (0.044715 * c) * square))
    value = u * half
    return value, half + value * (1.0 - half) * (2.0 * c + (6.0 * 0.044715 * c) * square)


def square_row(b):
    return lambda core, g: (core * 2 + b) * D + GROUP * g


def back_row(b):
    return lambda core, g: 4 * GROUP * g + GROUP * (2 * core + b)


def in_items(first):
    return [(first + GROUP * b, GROUP, square_row(b), lambda core, g, b=b: 2 * core + b) for b in range(2)]


def in_sources(a_sets, b_sets):
    cut = 2 * GROUP // 3
    later = lambda core, g: square_row(1)(core, g) + cut
    block = lambda core, g: 2 * core + 1
    return [
        (a_sets, [(0, GROUP, square_row(0), lambda core, g: 2 * core), (GROUP, cut, square_row(1), block)]),
        (b_sets, [(GROUP, GROUP - cut, later, block)]),
    ]


def back_sources(b_sets, shared, first, got):
    quarter = lambda core, g: g // 4
    return [
        (b_sets, [(0, GROUP, back_row(0), quarter)]),
        ([(shared, None, 0)], [(first, GROUP, back_row(1), quarter)]),
        ([(got, None, 1)], [(0, GROUP, back_row(1), quarter)]),
    ]


def arrays_of(sources):
    return [part for sets, items in sources for part, ids, other in sets]


def start_sources(meta, refs, sources, dst, sems, turn=None):
    at = 0
    for k, (sets, items) in enumerate(sources):
        plan = [(ids, other) for part, ids, other in sets]
        if turn is not None:
            items = (items[:1] if turn == 0 else items[1:]) if k == 0 else items * turn
        start_fetch(meta, refs[at : at + len(plan)], plan, items, dst, sems)
        at += len(plan)


def start_fetch(meta, refs, plan, items, dst, sem, only=None):
    if only is not None:
        for other in range(2):
            part = [(ref, entry) for ref, entry in zip(refs, plan) if entry[1] == other]

            @pl.when(jnp.bitwise_xor(meta[1], other) == only)
            def _():
                start_fetch(meta, [r for r, e in part], [e for r, e in part], items, dst, sem)

        return
    me, core = meta[0], meta[1]
    for first, count, row_of, *sem_of in items:
        for ref, (ids, other) in zip(refs, plan):
            source = 1 - core if other else core
            for slot in range(ref.shape[0]):
                group = jnp.int32(slot) if ids is None else jnp.bitwise_xor(me, ids[slot])
                off = pl.multiple_of(row_of(source, group), 16)
                at = sem.at[sem_of[0](source, group)] if sem_of else sem
                pltpu.make_async_copy(ref.at[slot, pl.ds(first, count)], dst.at[pl.ds(off, count)], at).start()


def start_copy(src, dst, sem):
    pltpu.make_async_copy(src, dst, sem).start()


def drain(ref, sem):
    pltpu.make_async_copy(ref, ref, sem).wait()


def slot_of(meta, group, b):
    rel = jnp.bitwise_xor(meta[0], group)
    x, y, z0, z1 = [jnp.bitwise_and(rel // (1 << bit), 1) for bit in range(4)]
    return (8 * y + 4 * x if b == 0 else 8 * x + 4 * y) + 2 * z0 + z1


def start_store(meta, src, group, b, keep, send, sem, rows=slice(None), cols=slice(None)):
    slot = slot_of(meta, group, b)
    at = (rows, cols)

    @pl.when(slot < GROUPS // 2)
    def _():
        pltpu.make_async_copy(src, keep.at[(slot,) + at], sem).start()

    @pl.when(slot >= GROUPS // 2)
    def _():
        pltpu.make_async_copy(src, send.at[(slot - GROUPS // 2,) + at], sem).start()


def head_lanes(h):
    lane = lax.broadcasted_iota(jnp.int32, (1, D), 1)
    return (lane >= h * HEAD_DIM) & (lane < (h + 1) * HEAD_DIM)


def pair_lanes(hh):
    lane = lax.broadcasted_iota(jnp.int32, (1, TILE), 1)
    return (lane < HEAD_DIM) if hh == 0 else (lane >= HEAD_DIM)


def masked(value, lanes):
    return jnp.where(lanes, value, jnp.zeros_like(value))


def fill_bias(window_ref, tiles, transposed):
    part = 1 if transposed else 0

    def one(h, carry):
        for d in range(3):
            row = jnp.broadcast_to(window_ref[h, pl.ds(part * 3 + d, 1), :], (TILE, 2 * TILE))
            rolled = pltpu.roll(row, TILE, 1, stride=1, stride_axis=0)
            tiles[h, d + 1] = rolled[:, :TILE]
        low = window_ref[h, pl.ds(0, 1), pl.ds(0, 1)]
        high = window_ref[h, pl.ds(2, 1), pl.ds(2 * TILE - 1, 1)]
        tiles[h, 0] = jnp.broadcast_to(low, (TILE, TILE))
        tiles[h, 4] = jnp.broadcast_to(high, (TILE, TILE))
        return carry

    lax.fori_loop(0, HEADS, one, 0)


def spec(space):
    return space if isinstance(space, pl.BlockSpec) else pl.BlockSpec(memory_space=space)


def call(body, name, ins, spaces, outs, out_spaces, scratch, us, aliases={}, grid=()):
    if grid:
        specs = {
            "grid_spec": pltpu.PrefetchScalarGridSpec(
                num_scalar_prefetch=1,
                grid=grid,
                in_specs=[spec(s) for s in spaces[1:]],
                out_specs=[spec(s) for s in out_spaces],
                scratch_shapes=scratch,
            )
        }
    else:
        specs = {
            "in_specs": [spec(s) for s in spaces],
            "out_specs": [spec(s) for s in out_spaces],
            "scratch_shapes": scratch,
        }
    return pl.pallas_call(
        body,
        name=name,
        out_shape=[jax.ShapeDtypeStruct(s, k) for s, k in outs],
        input_output_aliases=aliases,
        compiler_params=pltpu.CompilerParams(vmem_limit_bytes=VMEM_LIMIT),
        cost_estimate=pl.CostEstimate(flops=int(us * SPEED * 1.1e9), bytes_accessed=int(us * SPEED * 1e6), transcendentals=0),
        **specs,
    )(*ins)


VM, SM, ANY = pltpu.VMEM, pltpu.SMEM, pl.ANY


def plan_of(sets):
    return [part for part, ids, other in sets], [(ids, other) for part, ids, other in sets]


def bias_block(tiles, h, ib):
    return jnp.concatenate([
        jnp.concatenate([tiles[h, min(max(jb - (2 * ib + i), -2), 2) + 2] for i in range(2)], axis=1)
        for jb in range(ROW_LEN // TILE)
    ], axis=0)


def enc_attention(meta, x, gains, segr, segc, windows, a_sets, b_sets):
    a_arrays, a_plan = plan_of(a_sets)
    b_arrays, b_plan = plan_of(b_sets)
    n = len(a_arrays)
    wide = 2 * TILE

    def body(meta, x, gains, segr, segc, windows, *rest):
        a_parts, b_parts, rest = rest[:n], rest[n : 2 * n], rest[2 * n :]
        n1, q, k, v, c, h1, n2, lse, w, tiles, sems = rest
        start_fetch(meta, a_parts, a_plan, [(0, GROUP, square_row(0))], w, sems.at[0])
        start_fetch(meta, b_parts, b_plan, [(0, GROUP, square_row(1))], w, sems.at[0])
        fill_bias(windows, tiles, True)
        xf = x[...].astype(F32)
        n1[...] = rms(xf, gains[0:1, :]).astype(BF)
        drain(w, sems.at[0])
        for ref, at in ((q, 0), (k, 2), (v, 3)):
            ref[...] = nn(n1[...], w[at * D : (at + 1) * D, :]).astype(BF)
        lse[...] = jnp.zeros_like(lse)

        def pair(pr, carry):
            cols = pl.ds(pl.multiple_of(pr * TILE, TILE), TILE)
            for ib in range(ROW_LEN // wide):
                rows = slice(ib * wide, (ib + 1) * wide)
                same = segc[...] == segr[:, rows]
                total = None
                for hh in range(2):
                    h = 2 * pr + hh
                    lanes = pair_lanes(hh)
                    s = nt(masked(k[:, cols], lanes), q[rows, cols]) + bias_block(tiles, h, ib)
                    s = jnp.where(same, s, MASKED)
                    top = jnp.max(s, axis=0, keepdims=True)
                    ex = jnp.exp(s - top)
                    tot = jnp.sum(ex, axis=0, keepdims=True)
                    p = (ex * (1.0 / tot)).astype(BF)
                    part = tn(p, masked(v[:, cols], lanes))
                    total = part if total is None else total + part
                    lse[pl.ds(h, 1), rows] = top + jnp.log(tot)
                c[rows, cols] = total.astype(BF)
            return carry

        lax.fori_loop(0, HEADS // 2, pair, 0)
        res = x[...].astype(F32) + nn(c[...], w[D : 2 * D, :])
        h1[...] = res
        n2[...] = rms(res, gains[1:2, :]).astype(BF)

    rows = (ROW_LEN, D)
    return call(
        body, "enc_attention", [meta, x, gains, segr, segc, windows, *a_arrays, *b_arrays],
        [SM, VM, VM, VM, VM, VM] + [ANY] * (2 * n),
        [(rows, BF)] * 5 + [(rows, F32), (rows, BF), ((TILE, ROW_LEN), F32), ], [VM] * 8,
        [pltpu.VMEM((4 * D, D), BF), pltpu.VMEM((HEADS, 5, TILE, TILE), F32), pltpu.SemaphoreType.DMA((2,))],
        us=20,
    )


PART = (GROUPS // 2, GROUP, D)
WIDE_PART = (GROUPS // 2, 2 * GROUP, D)
BLOCKS = FF // D


def enc_ffn(meta, h1, n2, w_in_from, w_back_from):
    in_arrays, back_arrays = arrays_of(w_in_from), arrays_of(w_back_from)
    n, m = len(in_arrays), len(back_arrays)

    def body(meta, h1, n2, *rest):
        ins, backs, rest = rest[:n], rest[n : n + m], rest[n + m :]
        f_out, slope_out, e, w_in, w_back, acc, normed, f, slope, sems = rest
        start_copy(n2, normed, sems.at[8])
        start_sources(meta, ins, w_in_from, w_in, sems)
        start_copy(h1, acc, sems.at[9])
        start_sources(meta, backs, w_back_from, w_back, sems.at[pl.ds(4, 4)])
        drain(normed, sems.at[8])
        for at, b in enumerate((0, 2, 1, 3)):
            rows = slice(b * D, (b + 1) * D)
            slot = at % 2
            drain(w_in.at[rows], sems.at[b])
            value, grad = gelu_both(nn(normed[...], w_in[rows, :]))
            if at >= 2:
                drain(f.at[slot], sems.at[10 + slot])
                drain(slope.at[slot], sems.at[12 + slot])
            f[slot] = value.astype(BF)
            start_copy(f.at[slot], f_out.at[:, rows], sems.at[10 + slot])
            slope[slot] = grad.astype(BF)
            start_copy(slope.at[slot], slope_out.at[:, rows], sems.at[12 + slot])
            if at == 0:
                drain(acc, sems.at[9])
            drain(w_back.at[rows], sems.at[4 + b])
            acc[...] += nn(f[slot], w_back[rows, :])
        e[...] = acc[...].astype(BF)
        for slot in range(2):
            drain(f.at[slot], sems.at[10 + slot])
            drain(slope.at[slot], sems.at[12 + slot])

    block = (2, ROW_LEN, D)
    return call(
        body, "enc_ffn", [meta, h1, n2, *in_arrays, *back_arrays], [SM, ANY, ANY] + [ANY] * (n + m),
        [((ROW_LEN, FF), BF), ((ROW_LEN, FF), BF), ((ROW_LEN, D), BF)], [ANY, ANY, VM],
        [pltpu.VMEM((FF, D), BF), pltpu.VMEM((FF, D), BF), pltpu.VMEM((ROW_LEN, D), F32), pltpu.VMEM((ROW_LEN, D), BF),
         pltpu.VMEM(block, BF), pltpu.VMEM(block, BF), pltpu.SemaphoreType.DMA((14,))],
        us=15,
    )


PART = (GROUPS // 2, GROUP, D)
WIDE_PART = (GROUPS // 2, 2 * GROUP, D)
BLOCKS = FF // D


def enc_ffn(meta, h1, n2, w_in_from, w_back_from):
    in_arrays, back_arrays = arrays_of(w_in_from), arrays_of(w_back_from)
    n, m = len(in_arrays), len(back_arrays)

    def body(meta, h1, n2, *rest):
        ins, backs, rest = rest[:n], rest[n : n + m], rest[n + m :]
        f, slope, e, w_in, w_back, acc, sems = rest
        start_sources(meta, ins, w_in_from, w_in, sems)
        start_sources(meta, backs, w_back_from, w_back, sems.at[pl.ds(4, 4)])
        acc[...] = h1[...]

        def block(b, carry):
            rows = pl.ds(pl.multiple_of(b * D, D), D)

            drain(w_in.at[rows], sems.at[b])
            value, grad = gelu_both(nn(n2[...], w_in[rows, :]))
            fb = value.astype(BF)
            f[:, rows] = fb
            slope[:, rows] = grad.astype(BF)
            drain(w_back.at[rows], sems.at[4 + b])
            acc[...] += nn(fb, w_back[rows, :])
            return carry

        lax.fori_loop(0, FF // D, block, 0)
        e[...] = acc[...].astype(BF)

    return call(
        body, "enc_ffn", [meta, h1, n2, *in_arrays, *back_arrays], [SM, VM, VM] + [ANY] * (n + m),
        [((ROW_LEN, FF), BF), ((ROW_LEN, FF), BF), ((ROW_LEN, D), BF)], [VM] * 3,
        [pltpu.VMEM((FF, D), BF), pltpu.VMEM((FF, D), BF), pltpu.VMEM((ROW_LEN, D), F32),
         pltpu.SemaphoreType.DMA((8,))],
        us=15,
    )


def enc_hidden_grad(meta, de, slope, w_back_from):
    arrays = arrays_of(w_back_from)
    n = len(arrays)

    def body(meta, de, slope, *rest):
        parts, rest = rest[:n], rest[n:]
        du_out, other, w, slopes, du, sems = rest
        start_sources(meta, parts, w_back_from, w, sems)
        for b in range(BLOCKS):
            start_copy(slope.at[:, b * D : (b + 1) * D], slopes.at[b], sems.at[4 + b])
        for b in range(BLOCKS):
            cols = slice(b * D, (b + 1) * D)
            drain(w.at[cols], sems.at[b])
            drain(slopes.at[b], sems.at[4 + b])
            du[b] = (slopes[b].astype(F32) * nt(de[...], w[cols, :])).astype(BF)
            start_copy(du.at[b], du_out.at[:, cols], sems.at[8])

            @pl.when(meta[1] != b // 2)
            def _():
                start_copy(du.at[b], other.at[:, (b % 2) * D : (b % 2 + 1) * D], sems.at[9])

        drain(du, sems.at[8])
        drain(du.at[pl.ds(0, 2)], sems.at[9])

    block = (BLOCKS, ROW_LEN, D)
    return call(
        body, "enc_hidden_grad", [meta, de, slope, *arrays], [SM, VM, ANY] + [ANY] * n,
        [((ROW_LEN, FF), BF), ((ROW_LEN, FF // 2), BF)], [ANY, ANY],
        [pltpu.VMEM((FF, D), BF), pltpu.VMEM(block, BF), pltpu.VMEM(block, BF), pltpu.SemaphoreType.DMA((10,))],
        us=8,
    )


def enc_w_back_grad(meta, de, de_got, f, f_got):
    half = D // 2

    def body(meta, de, de_got, f, f_got, keep_a, send_a, keep_b, send_b, mine, theirs, fs, buf, sems):
        start_copy(de.at[:, pl.ds(pl.multiple_of(meta[1] * half, TILE), half)], mine, sems.at[2])
        start_copy(de_got, theirs, sems.at[3])
        for b in range(BLOCKS):
            for k, ref in enumerate((f, f_got)):
                start_copy(ref.at[:, b * D : (b + 1) * D], fs.at[b, k], sems.at[4 + b])
        drain(mine, sems.at[2])
        drain(theirs, sems.at[3])
        for b in range(BLOCKS):
            at = b % 2
            if b >= 2:
                drain(buf.at[at], sems.at[at])
            drain(fs.at[b], sems.at[4 + b])
            buf[at] = (tn(fs[b, 0], mine[...]) + tn(fs[b, 1], theirs[...])).astype(BF)
            for k in range(D // GROUP):
                group, piece = b * (D // GROUP // 4) + k // 4, k % 4
                keep, send = (keep_a, send_a) if piece < 2 else (keep_b, send_b)
                start_store(meta, buf.at[at, pl.ds(k * GROUP, GROUP)], group, piece // 2, keep, send, sems.at[at],
                            cols=pl.ds((piece % 2) * half, half))
        drain(buf.at[0], sems.at[0])
        drain(buf.at[1], sems.at[1])

    part = pltpu.VMEM((ROW_LEN, half), BF)
    return call(
        body, "enc_w_back_grad", [meta, de, de_got, f, f_got], [SM] + [ANY] * 4,
        [(PART, BF)] * 4, [ANY] * 4,
        [part, part, pltpu.VMEM((BLOCKS, 2, ROW_LEN, D), BF), pltpu.VMEM((2, D, half), BF), pltpu.SemaphoreType.DMA((8,))],
        us=7,
    )


def enc_w_in_grad(meta, du, du_got, n2, n2_got, wide_keep, wide_send):
    def body(meta, du, du_got, n2, n2_got, wide_keep, wide_send, keep_a, send_a, keep_b, send_b, buf, sems):
        for b in range(2):
            cols = pl.ds(pl.multiple_of(meta[1] * (FF // 2) + b * D, TILE), D)
            buf[b] = (tn(n2[...], du[:, cols]) + tn(n2_got[...], du_got[:, b * D : (b + 1) * D])).astype(BF)
            keep, send = (keep_a, send_a) if b == 0 else (keep_b, send_b)
            for g in range(GROUPS):
                rows = pl.ds(0, GROUP)
                start_store(meta, buf.at[b, pl.ds(g * GROUP, GROUP)], g, b, keep, send, sems.at[b], rows)
        drain(buf.at[0], sems.at[0])
        drain(buf.at[1], sems.at[1])

    return call(
        body, "enc_w_in_grad", [meta, du, du_got, n2, n2_got, wide_keep, wide_send], [SM] + [VM] * 4 + [ANY] * 2,
        [(WIDE_PART, BF), (WIDE_PART, BF), (PART, BF), (PART, BF)], [ANY] * 4,
        [pltpu.VMEM((2, D, D), BF), pltpu.SemaphoreType.DMA((2,))],
        us=7, aliases={5: 0, 6: 1},
    )


def enc_ffn_back(meta, du, h1, de, gains, w_in_from):
    arrays = arrays_of(w_in_from)
    n = len(arrays)

    def body(meta, du, h1, de, gains, *rest):
        parts, rest = rest[:n], rest[n:]
        dh1, da, dgain, w, acc, dus, h1s, des, sems = rest
        for first in range(2):
            for b in (first, first + 2):
                start_copy(du.at[:, b * D : (b + 1) * D], dus.at[b], sems.at[4 + b])
            start_sources(meta, parts, w_in_from, w, sems, first)
        start_copy(h1, h1s, sems.at[8])
        start_copy(de, des, sems.at[9])
        for k, b in enumerate((0, 2, 1, 3)):
            cols = slice(b * D, (b + 1) * D)
            drain(w.at[cols], sems.at[b])
            drain(dus.at[b], sems.at[4 + b])
            part = nt(dus[b], w[cols, :])
            acc[...] = part if k == 0 else acc[...] + part
        drain(h1s, sems.at[8])
        drain(des, sems.at[9])
        dv, dg = rms_back(h1s[...], gains[1:2, :], acc[...])
        total = des[...].astype(F32) + dv
        dh1[...] = total
        da[...] = total.astype(BF)
        dgain[...] = dg

    rows = (ROW_LEN, D)
    return call(
        body, "enc_ffn_back", [meta, du, h1, de, gains, *arrays], [SM, ANY, ANY, ANY, VM] + [ANY] * n,
        [(rows, F32), (rows, BF), ((1, D), F32)], [VM, VM, VM],
        [pltpu.VMEM((FF, D), BF), pltpu.VMEM(rows, F32), pltpu.VMEM((BLOCKS, ROW_LEN, D), BF), pltpu.VMEM(rows, F32),
         pltpu.VMEM(rows, BF), pltpu.SemaphoreType.DMA((10,))],
        us=8,
    )


def enc_attention_back(meta, da, q, k, v, lse, segr, segc, windows, sets):
    arrays, plan = plan_of(sets)
    n = len(arrays)
    wide = 2 * TILE

    def body(meta, da, q_in, k_in, v_in, lse, segr, segc, windows, *rest):
        parts, rest = rest[:n], rest[n:]
        dq_out, dk_out, dv_out, diag, other, w, dc, tiles, sums, kacc, vacc, q, k, v, dq, dk, dv, sems = rest
        sem = sems.at[0]
        start_fetch(meta, parts, plan, [(0, GROUP, lambda core, g: GROUP * g)], w, sem, only=0)
        for at, (src, dst) in enumerate(((q_in, q), (k_in, k), (v_in, v))):
            start_copy(src, dst, sems.at[1 + at])
        fill_bias(windows, tiles, True)
        drain(w, sem)
        dc[...] = nt(da[...], w[...]).astype(BF)
        for at, ref in enumerate((q, k, v)):
            drain(ref, sems.at[1 + at])
        row = lax.broadcasted_iota(jnp.int32, (TILE, TILE), 0)
        col = lax.broadcasted_iota(jnp.int32, (TILE, TILE), 1)
        flip = (row + col == TILE - 1).astype(F32)

        def pair(pr, carry):
            cols = pl.ds(pl.multiple_of(pr * TILE, TILE), TILE)
            for hh in range(2):
                h = 2 * pr + hh
                lanes = pair_lanes(hh)
                km, vm = masked(k[:, cols], lanes), masked(v[:, cols], lanes)
                sums[...] = jnp.zeros_like(sums)
                for ib in range(ROW_LEN // wide):
                    rows = slice(ib * wide, (ib + 1) * wide)
                    same = segc[...] == segr[:, rows]
                    qp, dcp = q[rows, cols], dc[rows, cols]
                    s = jnp.where(same, nt(km, qp) + bias_block(tiles, h, ib), MASKED)
                    prob = jnp.exp(s - lse[pl.ds(h, 1), rows])
                    dprob = nt(vm, dcp)
                    inner = jnp.sum(prob * dprob, axis=0, keepdims=True)
                    ds = (prob * (dprob - inner)).astype(BF)
                    dvp = nn(prob.astype(BF), masked(dcp, lanes))
                    dkp = nn(ds, masked(qp, lanes))
                    dqp = tn(ds, km)
                    if hh == 0 and ib == 0:
                        vacc[...], kacc[...] = dvp, dkp
                    else:
                        vacc[...] += dvp
                        kacc[...] += dkp
                    if hh == 0:
                        dq[rows, cols] = dqp.astype(BF)
                    else:
                        dq[rows, cols] = dq[rows, cols] + dqp.astype(BF)
                    for jb in range(ROW_LEN // TILE):
                        for i in range(2):
                            d = min(max(jb - (2 * ib + i), -2), 2) + 2
                            sums[d] += ds[jb * TILE : (jb + 1) * TILE, i * TILE : (i + 1) * TILE].astype(F32)
                for d in range(5):
                    if d in (0, 4):
                        line = jnp.sum(sums[d], axis=0, keepdims=True)
                        diag[h, d : d + 1, :] = jnp.concatenate([line, jnp.zeros_like(line)], axis=1)
                    else:
                        turned = lax.dot_general(
                            flip, sums[d], (((1,), (0,)), ((), ())),
                            precision=lax.Precision.HIGHEST, preferred_element_type=F32,
                        )
                        wider = jnp.concatenate([turned, jnp.zeros_like(turned)], axis=1)
                        rolled = pltpu.roll(wider, 1, 1, stride=1, stride_axis=0)
                        diag[h, d : d + 1, :] = jnp.sum(rolled, axis=0, keepdims=True)
            dk[:, cols] = kacc[...].astype(BF)
            dv[:, cols] = vacc[...].astype(BF)
            return carry

        lax.fori_loop(0, HEADS // 2, pair, 0)

        for core, (one, two) in enumerate(((dk, dv), (dq, da))):

            @pl.when(meta[1] == core)
            def _():
                start_copy(one, other.at[0], sems.at[1])
                start_copy(two, other.at[1], sems.at[1])

        for src, dst in ((dq, dq_out), (dk, dk_out), (dv, dv_out)):
            start_copy(src, dst, sems.at[2])
        drain(dk, sems.at[1])
        drain(dv, sems.at[1])
        for ref in (dq, dk, dv):
            drain(ref, sems.at[2])

    rows = (ROW_LEN, D)
    return call(
        body, "enc_attention_back", [meta, da, q, k, v, lse, segr, segc, windows, *arrays],
        [SM, VM, ANY, ANY, ANY] + [VM] * 4 + [ANY] * n,
        [(rows, BF), (rows, BF), (rows, BF), ((HEADS, 5, 2 * TILE), F32), ((2,) + rows, BF)], [ANY, ANY, ANY, VM, ANY],
        [pltpu.VMEM((D, D), BF), pltpu.VMEM(rows, BF), pltpu.VMEM((HEADS, 5, TILE, TILE), F32),
         pltpu.VMEM((5, TILE, TILE), F32), pltpu.VMEM((ROW_LEN, TILE), F32), pltpu.VMEM((ROW_LEN, TILE), F32)]
        + [pltpu.VMEM(rows, BF)] * 6 + [pltpu.SemaphoreType.DMA((4,))],
        us=25,
    )


def enc_square_grads(meta, n1, n1_got, c, c_got, dq, dk, dv, da, got):
    def body(meta, n1, n1_got, c, c_got, dq, dk, dv, da, got, keep_a, send_a, keep_b, send_b, buf, sems):
        for core, (one, left, left_got, two) in enumerate(((dq, c, c_got, da), (dk, n1, n1_got, dv))):

            @pl.when(meta[1] == core)
            def _():
                buf[0] = (tn(n1[...], one[...]) + tn(n1_got[...], got[0])).astype(BF)
                for g in range(GROUPS):
                    start_store(meta, buf.at[0, pl.ds(g * GROUP, GROUP)], g, 0, keep_a, send_a, sems.at[0])
                buf[1] = (tn(left[...], two[...]) + tn(left_got[...], got[1])).astype(BF)
                for g in range(GROUPS):
                    start_store(meta, buf.at[1, pl.ds(g * GROUP, GROUP)], g, 1, keep_b, send_b, sems.at[1])

        drain(buf.at[0], sems.at[0])
        drain(buf.at[1], sems.at[1])

    return call(
        body, "enc_square_grads", [meta, n1, n1_got, c, c_got, dq, dk, dv, da, got], [SM] + [VM] * 9,
        [(PART, BF)] * 4, [ANY] * 4,
        [pltpu.VMEM((2, D, D), BF), pltpu.SemaphoreType.DMA((2,))],
        us=1,
    )


def enc_input_grad(meta, dq, dk, dv, x, dh1, gains, a_sets, b_sets):
    a_arrays, a_plan = plan_of(a_sets)
    b_arrays, b_plan = plan_of(b_sets)
    n = len(a_arrays)

    def body(meta, dq, dk, dv, x, dh1, gains, *rest):
        a_parts, b_parts, rest = rest[:n], rest[n : 2 * n], rest[2 * n :]
        keep, send, dgain, w, grads, xs, dh1s, sems = rest
        start_fetch(meta, a_parts, a_plan, [(0, GROUP, lambda core, g: core * D + GROUP * g, lambda core, g: core)], w, sems)
        start_fetch(meta, b_parts, b_plan, [(0, GROUP, lambda core, g: 2 * D + GROUP * g, lambda core, g: 2)], w, sems, only=1)
        for k, ref in enumerate((dq, dk, dv)):
            start_copy(ref, grads.at[k], sems.at[3 + k])
        start_copy(x, xs, sems.at[6])
        start_copy(dh1, dh1s, sems.at[7])
        total = None
        for k in range(3):
            drain(w.at[pl.ds(k * D, D)], sems.at[k])
            drain(grads.at[k], sems.at[3 + k])
            part = nt(grads[k], w[k * D : (k + 1) * D, :])
            total = part if total is None else total + part
        drain(xs, sems.at[6])
        drain(dh1s, sems.at[7])
        dx, dg = rms_back(xs[...].astype(F32), gains[0:1, :], total)
        out = (dh1s[...] + dx).astype(BF)
        dgain[...] = dg
        half = D // 2

        @pl.when(meta[1] == 0)
        def _():
            keep[...] = out[:, :half]
            send[...] = out[:, half:]

        @pl.when(meta[1] != 0)
        def _():
            keep[...] = out[:, half:]
            send[...] = out[:, :half]

    return call(
        body, "enc_input_grad", [meta, dq, dk, dv, x, dh1, gains, *a_arrays, *b_arrays],
        [SM] + [ANY] * 5 + [VM] + [ANY] * (2 * n),
        [((ROW_LEN, D // 2), BF), ((ROW_LEN, D // 2), BF), ((1, D), F32)], [VM] * 3,
        [pltpu.VMEM((3 * D, D), BF), pltpu.VMEM((3, ROW_LEN, D), BF), pltpu.VMEM((ROW_LEN, D), BF),
         pltpu.VMEM((ROW_LEN, D), F32), pltpu.SemaphoreType.DMA((8,))],
        us=1,
    )


def spread_heads(value):
    return jnp.concatenate([masked(value, head_lanes(h)) for h in range(HEADS)], axis=0)


def join_heads(value):
    total = jnp.zeros((8, D), F32)
    for h in range(HEADS):
        total = total + masked(value[8 * h : 8 * h + 8, :], head_lanes(h))
    return total


def own_rows(meta):
    row = lax.broadcasted_iota(jnp.int32, (8, 1), 0)
    return (row >= 4 * meta[1]) & (row < 4 * meta[1] + 4)


def start_self(meta, own, got, dst, sem):
    half = D // 2
    pltpu.make_async_copy(own, dst.at[pl.ds(pl.multiple_of(meta[1] * half, 16), half)], sem).start()
    pltpu.make_async_copy(got, dst.at[pl.ds(pl.multiple_of((1 - meta[1]) * half, 16), half)], sem).start()


def dec_before(meta, z, d_out, gains, self_own, self_got, sets):
    arrays, plan = plan_of(sets)
    n = len(arrays)

    def body(meta, z, d_out, gains, self_own, self_got, *rest):
        parts, rest = rest[:n], rest[n:]
        m1, sv, z1, m2, qc, qk, gm, w_self, w, sems = rest
        start_self(meta, self_own, self_got, w_self, sems.at[0])
        start_fetch(meta, parts, plan, [(0, GROUP, lambda core, g: core * D + GROUP * g)], w, sems.at[1])
        zf = z[...].astype(F32)
        gm[...] = jnp.where(own_rows(meta), d_out[...].astype(F32), 0.0).astype(BF)
        m1v = rms(zf, gains[2:3, :]).astype(BF)
        drain(w_self, sems.at[0])
        drain(w, sems.at[1])
        svv = nn(m1v, w_self[:, :D]).astype(BF)
        z1v = zf + nn(svv, w_self[:, D:])
        m2v = rms(z1v, gains[0:1, :]).astype(BF)
        qcv = nn(m2v, w[0:D, :]).astype(BF)
        qk[...] = nt(spread_heads(qcv), w[D:, :]).astype(BF)
        m1[...], sv[...], z1[...], m2[...], qc[...] = m1v, svv, z1v, m2v, qcv

    rows = (8, D)
    return call(
        body, "dec_before", [meta, z, d_out, gains, self_own, self_got, *arrays],
        [SM, VM, VM, VM, ANY, ANY] + [ANY] * n,
        [(rows, BF), (rows, BF), (rows, F32), (rows, BF), (rows, BF), ((8 * HEADS, D), BF), (rows, BF)], [VM] * 7,
        [pltpu.VMEM((D, 2 * D), BF), pltpu.VMEM((2 * D, D), BF), pltpu.SemaphoreType.DMA((2,))],
        us=6,
    )


def dec_core(meta, e, segr, qk, qc, z1, g, gw, gains, sets):
    arrays, plan = plan_of(sets)
    n = len(arrays)

    def body(meta, e, segr, qk, qc, z1, g, gw, gains, *rest):
        parts, rest = rest[:n], rest[n:]
        de, cc, z2, m3, fc, duc, da2, dz2, dcc, edt, ebar, dgain, de_other, pairs_other, w, w_in, sems = rest
        start_fetch(meta, parts, plan, [(GROUP, GROUP, lambda core, g: core * D + GROUP * g)], w, sems.at[0])
        start_fetch(meta, parts, plan, in_items(2 * GROUP), w_in, sems.at[pl.ds(1, 4)])
        pairs = lax.broadcasted_iota(jnp.int32, (8 * HEADS, 1), 0)
        owner = segr[...] == jnp.bitwise_and(pairs, 7) - 4 * meta[1]
        t = jnp.where(owner, nt(qk[...], e[...]), MASKED)
        ex = jnp.where(owner, jnp.exp(t - jnp.max(t, axis=-1, keepdims=True)), 0.0)
        tot = jnp.sum(ex, axis=-1, keepdims=True)
        prob = ex * (1.0 / jnp.where(tot > 0.0, tot, 1.0))
        pc = prob.astype(BF)
        ebv = nn(pc, e[...]).astype(BF)
        ebar[...] = ebv
        drain(w, sems.at[0])
        ccv = join_heads(nn(ebv, w[D:, :])).astype(BF)
        z2v = z1[...] + nn(ccv, w[0:D, :])
        m3v = rms(z2v, gains[1:2, :]).astype(BF)
        dm3 = jnp.zeros((8, D), F32)
        own = own_rows(meta)
        for b in (0, 2, 1, 3):
            cols = slice(b * D, (b + 1) * D)
            drain(w_in.at[cols], sems.at[1 + b])
            value, slope = gelu_both(nn(m3v, w_in[cols, :]))
            fc[:, cols] = jnp.where(own, value, 0.0).astype(BF)
            ducv = jnp.where(own, slope * gw[:, cols].astype(F32), 0.0).astype(BF)
            duc[:, cols] = ducv
            dm3 = dm3 + nt(ducv, w_in[cols, :])
        back, dg = rms_back(z2v, gains[1:2, :], dm3)
        dz2v = g[...].astype(F32) + back
        da2v = dz2v.astype(BF)
        dccv = nt(da2v, w[0:D, :]).astype(BF)
        dvw = nt(spread_heads(dccv), w[D:, :]).astype(BF)
        dprob = nt(dvw, e[...])
        dt = (prob * (dprob - jnp.sum(prob * dprob, axis=-1, keepdims=True))).astype(BF)
        de[...] = tn(jnp.concatenate([pc, dt], axis=0), jnp.concatenate([dvw, qk[...]], axis=0)).astype(BF)
        edt[...] = nn(dt, e[...]).astype(BF)
        cc[...], m3[...], da2[...], dz2[...], dcc[...], dgain[...] = ccv, m3v, da2v, dz2v, dccv, dg
        z2[...] = jnp.where(own, z2v, 0.0)
        half = D // 2
        pairs_other[8 * HEADS + 8 :, :] = jnp.zeros((8, D), BF)

        @pl.when(meta[1] == 0)
        def _():
            de_other[...] = de[:, half:]
            pairs_other[: 8 * HEADS, :] = ebv
            pairs_other[8 * HEADS : 8 * HEADS + 8, :] = dccv

        @pl.when(meta[1] != 0)
        def _():
            de_other[...] = de[:, :half]
            pairs_other[: 8 * HEADS, :] = edt[...]
            pairs_other[8 * HEADS : 8 * HEADS + 8, :] = qc[...]

    rows, spread = (8, D), (8 * HEADS, D)
    return call(
        body, "dec_core", [meta, e, segr, qk, qc, z1, g, gw, gains, *arrays],
        [SM] + [VM] * 8 + [ANY] * n,
        [((ROW_LEN, D), BF), (rows, BF), (rows, F32), (rows, BF), ((8, FF), BF), ((8, FF), BF), (rows, BF),
         (rows, F32), (rows, BF), (spread, BF), (spread, BF), ((1, D), F32),
         ((ROW_LEN, D // 2), BF), ((8 * HEADS + 16, D), BF)], [VM] * 14,
        [pltpu.VMEM((2 * D, D), BF), pltpu.VMEM((FF, D), BF), pltpu.SemaphoreType.DMA((5,))],
        us=10,
    )


def dec_after(meta, z, z1, dz2, qc, dcc, edt, ebar, got, gains, acts, duc, fc, self_own, self_got, sets):
    arrays, plan = plan_of(sets)
    n = len(arrays)

    def body(meta, z, z1, dz2, qc, dcc, edt, ebar, got, gains, *rest):
        acts, rest = rest[:8], rest[8:]
        self_own, self_got, parts, rest = rest[0], rest[1], rest[2 : 2 + n], rest[2 + n :]
        acts_keep, acts_send, dec_grad, dg_attn, dg_self, keep, send, w_self, w, buf, sems = rest
        start_fetch(meta, parts, plan, [(0, GROUP, lambda core, g: core * D + GROUP * g)], w, sems.at[1])
        start_self(meta, self_own, self_got, w_self, sems.at[0])
        zero = meta[1] == 0
        left = jnp.concatenate([jnp.where(zero, edt[...], ebar[...]), got[: 8 * HEADS, :]], axis=0)
        right = jnp.where(zero, qc[...], dcc[...])
        right = jnp.concatenate([spread_heads(right), spread_heads(got[8 * HEADS : 8 * HEADS + 8, :])], axis=0)
        buf[...] = tn(left, right).astype(BF)
        for grp in range(GROUPS):
            start_store(meta, buf.at[pl.ds(grp * GROUP, GROUP)], grp, 0, keep, send, sems.at[3], pl.ds(GROUP, GROUP))
        drain(w, sems.at[1])
        dqv = join_heads(nn(edt[...], w[D:, :])).astype(BF)
        back, dg = rms_back(z1[...], gains[0:1, :], nt(dqv, w[0:D, :]))
        dz1 = dz2[...] + back
        ds1v = dz1.astype(BF)
        drain(w_self, sems.at[0])
        dsvv = nt(ds1v, w_self[:, D:]).astype(BF)
        back0, dg0 = rms_back(z[...].astype(F32), gains[2:3, :], nt(dsvv, w_self[:, :D]))
        own = own_rows(meta)
        dec_grad[...] = jnp.where(own, dz1 + back0, 0.0).astype(BF)
        dg_attn[...], dg_self[...] = dg, dg0
        row = jnp.concatenate([ref[...] for ref in acts[:6]] + [dqv, ds1v, dsvv] + [ref[...] for ref in acts[6:]], axis=1)
        half = row.shape[1] // 2
        for core, (one, two) in enumerate(((acts_keep, acts_send), (acts_send, acts_keep))):

            @pl.when(meta[1] == core)
            def _():
                one[...] = row[:, :half]
                two[...] = row[:, half:]

        drain(buf, sems.at[3])

    rows = (8, D)
    return call(
        body, "dec_after",
        [meta, z, z1, dz2, qc, dcc, edt, ebar, got, gains, *acts, duc, fc, self_own, self_got, *arrays],
        [SM] + [VM] * 17 + [ANY] * (2 + n),
        [((8, (9 * D + 2 * FF) // 2), BF)] * 2 + [(rows, BF)] + [((1, D), F32)] * 2 + [(WIDE_PART, BF)] * 2, [VM] * 5 + [ANY] * 2,
        [pltpu.VMEM((D, 2 * D), BF), pltpu.VMEM((2 * D, D), BF), pltpu.VMEM((D, D), BF),
         pltpu.SemaphoreType.DMA((4,))],
        us=6,
    )


def dec_weight_grads(place, own, got, g_all, w_back, rows, self_rows):
    def body(place, own, got, *rest):
        for core, (left, right) in enumerate(((own, got), (got, own))):
            pl.when(place[1] == core)(functools.partial(halves, place, left, right, *rest))

    def halves(place, left, right, g_all, w_back, dec_q, dec_o, dec_i, dec_b, self_v, self_o, y):
        half = left.shape[1]
        chip, core = place[0], place[1]
        chips = D // rows

        def cut(at, width):
            parts = []
            while width:
                ref, first = (left, at) if at < half else (right, at - half)
                count = min(width, half - first)
                parts.append(ref[:, first : first + count])
                at, width = at + count, width - count
            return parts[0] if len(parts) == 1 else jnp.concatenate(parts, axis=1)

        def picked(at, first, count, width=D):
            row = lax.broadcasted_iota(jnp.int32, (count, width), 0) + first
            col = lax.broadcasted_iota(jnp.int32, (count, width), 1)
            return nt((row == col).astype(F32).astype(BF), cut(at * D, width)).astype(BF)

        first, first_self = chip * rows, (core * chips + chip) * self_rows
        m1, sv, m2, cc, m3, da2, dqc, ds1, dsv, duc, fc = list(range(10)) + [13]
        dec_q[...] = nn(picked(m2, first, rows), cut(dqc * D, D))
        dec_o[...] = nn(picked(cc, first, rows), cut(da2 * D, D))
        dec_i[...] = nn(picked(m3, first, rows), cut(duc * D, FF))
        self_v[...] = nn(picked(m1, first_self, self_rows), cut(dsv * D, D))
        self_o[...] = nn(picked(sv, first_self, self_rows), cut(ds1 * D, D))
        hidden = picked(fc, 4 * first, 4 * rows, FF)
        dec_b[...] = nn(hidden, g_all[...])
        y[...] = tn(hidden, w_back[...]).astype(BF)

    return call(
        body, "dec_weight_grads", [place, own, got, g_all, w_back], [SM, VM, VM, VM, VM],
        [((rows, D), F32), ((rows, D), F32), ((rows, FF), F32), ((4 * rows, D), F32), ((self_rows, D), F32),
         ((self_rows, D), F32), (g_all.shape, BF)], [VM] * 7,
        [], us=0.2,
    )


def prepare(meta, w_query, w_key, w_value, w_out, w_in, w_back):
    def body(meta, query, key, value, out, w_in, w_back, kept, sent):
        for core, (one, two) in enumerate(((kept, sent), (sent, kept))):

            @pl.when(meta[1] == core)
            def _():
                for half, (dst, squares) in enumerate(((one, (query, out)), (two, (key, value)))):
                    for k in range(2):
                        at = 2 * half + k
                        dst[k * GROUP : (k + 1) * GROUP, :] = squares[k][...]
                        dst[(2 + k) * GROUP : (3 + k) * GROUP, :] = w_in[:, at * D : (at + 1) * D]
                        dst[(4 + k) * GROUP : (5 + k) * GROUP, :] = w_back[at * GROUP : (at + 1) * GROUP, :]

    half = ((6 * GROUP, D), BF)
    return call(
        body, "prepare", [meta, w_query, w_key, w_value, w_out, w_in, w_back], [SM] + [VM] * 6, [half] * 2, [VM] * 2, [], us=2
    )


def per_device(
    enc_in, dec_in, segment, d_out, attn_gain, w_query, w_key, w_value, w_out, ffn_gain, w_in, w_back,
    self_gain, self_value, self_out, rel_table,
):
    core, chip = lax.axis_index("section"), lax.axis_index("dp")
    chips = lax.axis_size("dp")
    rows = w_query.shape[1]
    first = core == 0
    pre = low_bits(rows)
    meta = jnp.stack([chip >> pre, core]).astype(jnp.int32)
    self_rows = self_value.shape[0]
    at_self = (core * chips + chip) * self_rows

    kept, sent = prepare(
        meta, *[filled(w[0], pre, chip, 0) for w in (w_query, w_key, w_value, w_out, w_in, w_back)]
    )
    got = across(sent)
    enc_piece, dec_piece = jnp.where(first, kept, got), jnp.where(first, got, kept)
    count = 4 * GROUP

    shared = lax.all_gather(jnp.concatenate([dec_piece[:count], self_value, self_out, enc_piece[5 * GROUP :]]), "dp")

    gains = jnp.zeros((8, D), BF)
    gains = lax.dynamic_update_slice(gains, jnp.concatenate([attn_gain, ffn_gain]), (0, chip * rows))
    gains = lax.dynamic_update_slice(gains, self_gain[None], (2, at_self))
    little = Chain([jnp.concatenate([gains, d_out])[None]], [0], 0)
    for bit in range(pre):
        little.step(bit)

    def chain(*parts):
        return Chain([jnp.concatenate(parts)[None]], [0], pre)

    cut = 3 * GROUP + 2 * GROUP // 3
    sq = chain(enc_piece[: 2 * GROUP])
    wide = chain(enc_piece[2 * GROUP : cut], enc_piece[4 * GROUP : 5 * GROUP], enc_piece[cut : 4 * GROUP])

    windows = jnp.einsum(
        "adtb,bh->hadt", window_onehots(), rel_table, precision=lax.Precision.HIGHEST
    ).reshape(HEADS, 6, 2 * TILE)
    x = lax.dynamic_index_in_dim(enc_in, core, 0, False)
    seg = lax.dynamic_index_in_dim(segment, core, 0, False)
    segr, segc = seg[None, :], seg[:, None]

    sq.step(Z1), little.step(X + pre)
    phase(sq, little)
    sq.step(Z0), little.step(Y + pre)
    phase(sq, wide, little)
    sa, sb = sq.split(GROUP)
    sa.step(X), sb.step(Y), wide.step(Z1), little.step(Z0 + pre)
    phase(sa, sb, wide, little)
    sa.step(Y), sb.step(X), wide.step(Z0), little.step(Z1 + pre)
    sa_got, sb_got = [across(sa.parts[0])], [across(sb.parts[0])]
    x = phase(sa, sb, wide, little, x)
    wa, wb = wide.split(cut - 2 * GROUP)
    wa.step(X), wb.step(Y)
    sa_got += [across(sa.parts[1])]
    sb_got += [across(sb.parts[1])]

    order = np.argsort(np.array(little.ids))
    places = jnp.take(jnp.asarray(order, jnp.int32), jnp.bitwise_xor(jnp.arange(chips), chip))
    little = jnp.concatenate(little.parts)
    gains = jnp.sum(little[:, :8].astype(F32), axis=0)
    gains_got = across(gains)
    gains0, gains1 = jnp.where(first, gains, gains_got), jnp.where(first, gains_got, gains)
    gains1 = jnp.where(jnp.arange(8)[:, None] == 2, gains0 + gains1, gains1)
    n1, q, k, v, c, h1, n2, lse = enc_attention(meta, x, gains0, segr, segc, windows, sa.sets(sa_got), sb.sets(sb_got))
    h1, little = phase(wa, wb, h1, little)
    wa.step(Y), wb.step(X)
    wa_got, wb_got = [across(wa.parts[0])], [across(wb.parts[0])]

    g_all = jnp.take(little[:, 8:], places, axis=0).reshape(8 * chips, D)
    lanes = -(-4 * rows // TILE) * TILE
    gw = jnp.pad(nt(g_all, w_back[0]).astype(BF), ((0, 0), (0, lanes - 4 * rows))).reshape(chips, 8, lanes)
    gw = lax.all_to_all(gw, "dp", 0, 0)
    h1, shared, gw = phase(wa, wb, h1, shared, gw)
    wa_got += [across(wa.parts[1])]
    wb_got += [across(wb.parts[1])]
    back_at = count + 2 * self_rows
    shared_back = shared[:: 2**pre, back_at:]
    back_got = across(shared_back)

    def self_part(index):
        at = count + index * self_rows
        return shared[:, at : at + self_rows].reshape(D // 2, D)

    self_own = jnp.concatenate([self_part(0), self_part(1)], axis=1)
    gw = gw[:, :, : 4 * rows].transpose(1, 0, 2).reshape(8, FF)
    gw_got = across(gw)
    wa_got, wb_got, back_got, h1, n1, c, n2, shared, self_own, gw, gw_got = phase(
        wa_got, wb_got, back_got, h1, n1, c, n2, shared, self_own, gw, gw_got
    )
    gw = jnp.where(first, gw_got, gw)
    self_got, shared_got = across(self_own), across(shared)
    n1_got, c_got, n2_got = across(n1), across(c), across(n2)
    w_in_from = in_sources(wa.sets(wa_got), wb.sets(wb_got))
    w_back_from = back_sources(wb.sets(wb_got), shared_back if pre else shared, 0 if pre else back_at, back_got)
    f, slope, e = enc_ffn(meta, h1, n2, w_in_from, w_back_from)
    e, shared_got, n1_got, c_got, n2_got, self_got = phase(e, shared_got, n1_got, c_got, n2_got, self_got)
    dec_sets = [(v[:: 2**pre] if pre else v, None, other) for other, v in enumerate((shared, shared_got))]
    m1, sv, z1, m2, qc, qk, gm = dec_before(meta, dec_in, d_out, gains1, self_own, self_got, dec_sets)
    f, qk = phase(f, qk)
    f_got = across(f)
    de, cc, z2, m3, fc, duc, da2, dz2, dcc, edt, ebar, dg_ffn1, de_other, pairs_other = dec_core(
        meta, e, segr, qk, qc, z1, gm, gw, gains1, dec_sets
    )

    def two(parts):
        return Sum(parts[0], parts[1], pre), Sum(parts[2], parts[3], pre)

    de_got, pairs_got = across(de_other), across(pairs_other)
    du, du_other = enc_hidden_grad(meta, de, slope, w_back_from)
    de_got, pairs_got, du, du_other, edt = phase(de_got, pairs_got, du, du_other, edt)
    du_got = across(du_other)
    acts, acts_send, dec_grad, dg_attn1, dg_self, k_keep, k_send = dec_after(
        meta, dec_in, z1, dz2, qc, dcc, edt, ebar, pairs_got, gains1, [m1, sv, m2, cc, m3, da2], duc, fc,
        self_own, self_got, dec_sets,
    )
    acts, acts_send, f, f_got = phase(acts, acts_send, f, f_got)
    acts_got, width = across(acts_send), acts.shape[1]
    own = (jnp.arange(8)[:, None] // 4) == core
    acts = jnp.where(own, acts, acts_got)
    acts = lax.all_gather(acts, "dp").reshape(8 * chips, width)
    back_a, back_b = two(enc_w_back_grad(meta, de, de_got, f, f_got))
    n2, du_got = phase(back_a, back_b, n2, du_got)
    back_a.step(Y), back_b.step(X)
    in_a, in_b = two(enc_w_in_grad(meta, du, du_got, n2, n2_got, k_keep, k_send))
    h1 = phase(in_a, in_b, h1)
    in_a.step(Y), in_b.step(X)
    dh1, da, dg_ffn0 = enc_ffn_back(meta, du, h1, de, gains0, w_in_from)
    da = phase(back_a, back_b, da)
    back_a.step(X), back_b.step(Y)
    dq, dk, dv, diag, other = enc_attention_back(meta, da, q, k, v, lse, segr, segc, windows, sb.sets(sb_got))
    dq, other = phase(back_a, back_b, in_a, in_b, dq, other)
    got = across(other)
    in_a.step(X), in_b.step(Y)
    backs = merged([back_a, back_b])
    backs.step(Z0)
    keep, send, dg_attn0 = enc_input_grad(meta, dq, dk, dv, x, dh1, gains0, sa.sets(sa_got), sb.sets(sb_got))
    got, dq, dg_attn0 = phase(got, dq, dg_attn0)
    table = jnp.einsum("hdt,dtb->bh", diag, diagonal_onehots(), precision=lax.Precision.HIGHEST)
    little = jnp.concatenate([
        dg_attn0, dg_ffn0, dg_attn1, dg_ffn1, dg_self,
        jnp.pad(table.reshape(1, -1), ((0, 0), (0, D - BUCKETS * HEADS))), jnp.zeros((2, D), F32),
    ])
    little = little + across(little)
    for bit in range(pre):
        little = little + along(little, bit)
    other = along(little, Z0 + pre)
    square_a, square_b = two(enc_square_grads(meta, n1, n1_got, c, c_got, dq, dk, dv, da, got))
    acts, other = phase(square_a, square_b, in_a, in_b, backs, acts, other)
    backs.step(Z1)
    little = little + other
    square_a.step(Y), square_b.step(X)
    theirs = across(acts)
    other = along(little, Z1 + pre)
    ins = merged([in_a, in_b])
    ins.step(Z0)

    dec_q, dec_o, dec_i, dec_b, g_self_value, g_self_out, y = dec_weight_grads(
        jnp.stack([chip, core]), acts, theirs, g_all, w_back[0], rows, self_rows
    )
    other, y = phase(square_a, square_b, ins, backs, other, y)
    little = little + other
    square_a.step(X), square_b.step(Y), ins.step(Z1)
    other = along(little, X + pre)
    other, y, send, z2, dec_grad = phase(square_a, square_b, other, y, send, z2, dec_grad)
    little = little + other
    squares = merged([square_a, square_b])
    squares.step(Z0)
    other = along(little, Y + pre)
    z2 = z2 + across(z2)
    y = lax.all_to_all(y.reshape(chips, 8, D), "dp", 0, 0)
    other, y = phase(squares, ins, other, y)
    little = little + other
    squares.step(Z1)
    backs_sum, ins_sum, square_sum = backs.total(), ins.total(), squares.total()
    dec_out = (z2 + jnp.sum(y.astype(F32), axis=0)).astype(BF)
    dec_out = jnp.where(first, across(dec_out), dec_out)
    mine = chip * rows

    g_rel_table = little[5, : BUCKETS * HEADS].reshape(BUCKETS, HEADS)

    def cut(index, at, count):
        return lax.dynamic_slice_in_dim(little[index], at, count, 0)

    g_attn_gain = cut(jnp.where(first, 0, 2), mine, rows)[None]
    g_ffn_gain = cut(jnp.where(first, 1, 3), mine, rows)[None]
    g_self_gain = cut(4, at_self, self_rows)

    backs_got, ins_got, square_got = [across(v.astype(BF)).astype(F32) for v in (backs_sum, ins_sum, square_sum)]

    def group(value, index):
        return value[index * GROUP : (index + 1) * GROUP]

    def placed(enc_value, dec_value):
        return jnp.where(first, narrowed(enc_value, pre, chip), dec_value)[None]

    g_w_query = placed(group(square_sum, 0), dec_q)
    g_w_out = placed(group(square_sum, 1), dec_o)
    g_w_key = narrowed(jnp.where(first, group(square_got, 0), group(ins_got, 1)), pre, chip)[None]
    g_w_value = narrowed(jnp.where(first, group(square_got, 1), group(ins_sum, 1)), pre, chip)[None]
    g_w_in = placed(
        jnp.concatenate([group(ins_sum, 0), group(ins_sum, 2), group(ins_got, 0), group(ins_got, 2)], axis=1), dec_i
    )
    half = D // 2
    tall = [
        jnp.concatenate([group(v, i)[:, j * half : (j + 1) * half] for i in range(2) for j in range(2)])
        for v in (backs_sum, backs_got)
    ]
    g_w_back = placed(jnp.concatenate(tall, axis=1), dec_b)

    other_half = across(send)
    enc_in_grad = jnp.where(first, jnp.stack([keep, other_half]), jnp.stack([other_half, keep]))
    dec_grad = dec_grad + across(dec_grad)
    half = D // 2
    dec_out = jnp.where(first, dec_out[:, :half], dec_out[:, half:])
    dec_in_grad = jnp.where(first, dec_grad[:, :half], dec_grad[:, half:])
    return (
        dec_out, enc_in_grad, dec_in_grad, g_attn_gain, g_w_query, g_w_key, g_w_value, g_w_out, g_ffn_gain,
        g_w_in, g_w_back, g_self_gain, g_self_value, g_self_out, g_rel_table,
    )


def solution(mesh):
    return jax.shard_map(
        per_device,
        mesh=mesh,
        in_specs=(
            P("dp", None, None),
            P("dp", None),
            P("dp", None),
            P("dp", None),
            P("section", "dp"),
            P("section", "dp", None),
            P("section", "dp", None),
            P("section", "dp", None),
            P("section", "dp", None),
            P("section", "dp"),
            P("section", "dp", None),
            P("section", "dp", None),
            P(("section", "dp")),
            P(("section", "dp"), None),
            P(("section", "dp"), None),
            P(),
        ),
        out_specs=(
            P("dp", "section"),
            P("dp", None, "section"),
            P("dp", "section"),
            P("section", "dp"),
            P("section", "dp", None),
            P("section", "dp", None),
            P("section", "dp", None),
            P("section", "dp", None),
            P("section", "dp"),
            P("section", "dp", None),
            P("section", "dp", None),
            P(("section", "dp")),
            P(("section", "dp"), None),
            P(("section", "dp"), None),
            P(),
        ),
        check_vma=False,
    )
```
